32 devices in a mesh: section: 4 (over y, x), dp: 8 (over z, core).
Axes of the slice: x: 2, y: 2, z: 4, core: 2. Of those that a mesh axis runs over, the one named last changes fastest.
Arguments:
- frames_in: bfloat16 [1152, 4, 1024], P('dp', 'section'), may hold values from -6 to 6
- depth_counts: int32 [1152], P('dp'), may hold values from 2 to 4, as said below
- attn_gain_1: bfloat16 [4, 1024], P('section', 'dp'), may hold values from 0.099609375 to 1.8984375
- query_weight_1: bfloat16 [4, 1024, 1024], P('section', 'dp'), may hold values from -0.1875 to 0.1875
- key_weight_1: bfloat16 [4, 1024, 1024], P('section', 'dp'), may hold values from -0.1875 to 0.1875
- value_weight_1: bfloat16 [4, 1024, 1024], P('section', 'dp'), may hold values from -0.1875 to 0.1875
- out_weight_1: bfloat16 [4, 1024, 1024], P('section', 'dp'), may hold values from -0.25 to 0.25
- ffn_gain_1: bfloat16 [4, 1024], P('section', 'dp'), may hold values from 0.099609375 to 1.8984375
- gate_weight_1: bfloat16 [4, 1024, 4096], P('section', 'dp'), may hold values from -0.1875 to 0.1875
- up_weight_1: bfloat16 [4, 1024, 4096], P('section', 'dp'), may hold values from -0.1875 to 0.1875
- down_weight_1: bfloat16 [4, 4096, 1024], P('section', 'dp'), may hold values from -0.09375 to 0.09375
- attn_gain_2: bfloat16 [4, 1024], P('section', 'dp'), may hold values from 0.099609375 to 1.8984375
- query_weight_2: bfloat16 [4, 1024, 1024], P('section', 'dp'), may hold values from -0.1875 to 0.1875
- key_weight_2: bfloat16 [4, 1024, 1024], P('section', 'dp'), may hold values from -0.1875 to 0.1875
- value_weight_2: bfloat16 [4, 1024, 1024], P('section', 'dp'), may hold values from -0.1875 to 0.1875
- out_weight_2: bfloat16 [4, 1024, 1024], P('section', 'dp'), may hold values from -0.25 to 0.25
- ffn_gain_2: bfloat16 [4, 1024], P('section', 'dp'), may hold values from 0.099609375 to 1.8984375
- gate_weight_2: bfloat16 [4, 1024, 4096], P('section', 'dp'), may hold values from -0.1875 to 0.1875
- up_weight_2: bfloat16 [4, 1024, 4096], P('section', 'dp'), may hold values from -0.1875 to 0.1875
- down_weight_2: bfloat16 [4, 4096, 1024], P('section', 'dp'), may hold values from -0.09375 to 0.09375
- out_grad: bfloat16 [1152, 4, 1024], P('dp', 'section'), may hold values from -6 to 6
Outputs:
- frames_out: bfloat16 [1152, 4, 1024], P('dp', 'section')
- input_grad: bfloat16 [1152, 4, 1024], P('dp', 'section')
- grad_attn_gain_1: float32 [4, 1024], P('section', 'dp')
- grad_query_weight_1: float32 [4, 1024, 1024], P('section', 'dp')
- grad_key_weight_1: float32 [4, 1024, 1024], P('section', 'dp')
- grad_value_weight_1: float32 [4, 1024, 1024], P('section', 'dp')
- grad_out_weight_1: float32 [4, 1024, 1024], P('section', 'dp')
- grad_ffn_gain_1: float32 [4, 1024], P('section', 'dp')
- grad_gate_weight_1: float32 [4, 1024, 4096], P('section', 'dp')
- grad_up_weight_1: float32 [4, 1024, 4096], P('section', 'dp')
- grad_down_weight_1: float32 [4, 4096, 1024], P('section', 'dp')
- grad_attn_gain_2: float32 [4, 1024], P('section', 'dp')
- grad_query_weight_2: float32 [4, 1024, 1024], P('section', 'dp')
- grad_key_weight_2: float32 [4, 1024, 1024], P('section', 'dp')
- grad_value_weight_2: float32 [4, 1024, 1024], P('section', 'dp')
- grad_out_weight_2: float32 [4, 1024, 1024], P('section', 'dp')
- grad_ffn_gain_2: float32 [4, 1024], P('section', 'dp')
- grad_gate_weight_2: float32 [4, 1024, 4096], P('section', 'dp')
- grad_up_weight_2: float32 [4, 1024, 4096], P('section', 'dp')
- grad_down_weight_2: float32 [4, 4096, 1024], P('section', 'dp')
The draws below stay inside these ranges and needn't reach their ends.
Inputs may be any that keep to these rules, and one draw needn't show every extreme that they name: `depth_counts`: each frame's depth count is half of 4 or 4; each aligned block of 144 frames holds at least one frame of depth 4.
All inputs are finite; a program needn't handle non-finite values.
Results may differ from the reference program's by a relative error of at most 0.017.
Values may be sent and summed in bfloat16 or wider, within the bound.
A program may use at most 384 MiB of HBM per device.

```python
import jax
import jax.numpy as jnp
from jax import lax

D = 1024
HEADS = 16
HEAD_DIM = 64
FF = 4096
FRAMES_DEV = 144
DEPTH = 4
FRAMES = 1152
N_DP = 8


def draw_depth_counts(key, part):
    key = jax.random.fold_in(key, 11)
    first, second, third = jax.random.split(key, 3)
    blocks = FRAMES // FRAMES_DEV
    share = jax.random.randint(first, (blocks, 1), 1, 4)
    roll = jax.random.randint(second, (blocks, FRAMES_DEV), 0, 4)
    forced = jax.random.randint(third, (blocks, 1), 0, FRAMES_DEV)
    longer = (roll < share) | (jnp.arange(FRAMES_DEV)[None, :] == forced)
    counts = jnp.where(longer, DEPTH, DEPTH // 2)
    return counts.reshape(FRAMES).astype(jnp.int32)


def spiked(values, stream_key, source, target, parts, factor):
    def block_of(dim):
        return (jnp.arange(values.shape[dim]) // (values.shape[dim] // parts)).reshape((-1,) + (1,) * (values.ndim - 1 - dim))

    one_side = jax.random.permutation(stream_key, parts)[block_of(target)]
    other_side = (block_of(target) + parts // 2) % parts
    return jnp.where((block_of(source) == one_side) | (block_of(source) == other_side), factor * values, values)


def block_scale(key, extent, cuts, least, top_value):
    level = 1.0
    for dim, parts in cuts:
        draws = jax.random.uniform(jax.random.fold_in(jax.random.fold_in(key, 6), dim), (parts,), jnp.float32, least / len(cuts), top_value / len(cuts))
        level = level * jnp.repeat(jnp.exp(draws), extent[dim] // parts).reshape((-1,) + (1,) * (len(extent) - 1 - dim))
    return level


def noise(rng, shape, deviation, bound, pieces=(), kind=jnp.bfloat16):
    values = deviation * jax.random.normal(rng, shape, jnp.float32)
    if pieces:
        values = values * block_scale(rng, shape, pieces, -0.22, 0.18)
    return jnp.clip(values, -bound, bound).astype(kind)


def bell_draw_with(key, dims, scale, limit, cuts, heavy, dtype=jnp.bfloat16):
    values = scale * jax.random.normal(key, dims, jnp.float32)
    if cuts:
        values = values * block_scale(key, dims, cuts, -0.22, 0.18)
    return jnp.clip(spiked(values, jax.random.fold_in(key, 3), *heavy), -limit, limit).astype(dtype)


def setup_inputs(seed: int = 0) -> dict:
    splits = jax.random.split(jax.random.key(seed), 22)
    return {
        "frames_in": bell_draw_with(splits[0], (FRAMES, DEPTH, D), 1.0, 6.0, ((0, 8), (1, 4)), (0, 2, 8, 2.0)),
        "depth_counts": draw_depth_counts(jax.random.fold_in(splits[21], 71), 0),
        "attn_gain_1": jnp.clip(1.0 + 0.18 * jax.random.normal(splits[2], (DEPTH, D), jnp.float32), 0.099609375, 1.8984375).astype(jnp.bfloat16),
        "query_weight_1": noise(splits[3], (DEPTH, D, D), D ** -0.5, 0.1875, ((0, 4), (1, 8))),
        "key_weight_1": noise(splits[4], (DEPTH, D, D), D ** -0.5, 0.1875, ((0, 4), (1, 8))),
        "value_weight_1": noise(splits[5], (DEPTH, D, D), D ** -0.5, 0.1875, ((0, 4), (1, 8))),
        "out_weight_1": noise(splits[6], (DEPTH, D, D), (D // 2) ** -0.5, 0.25, ((0, 4), (1, 8))),
        "ffn_gain_1": jnp.clip(1.0 + 0.18 * jax.random.normal(splits[7], (DEPTH, D), jnp.float32), 0.099609375, 1.8984375).astype(jnp.bfloat16),
        "gate_weight_1": noise(splits[8], (DEPTH, D, FF), D ** -0.5, 0.1875, ((0, 4), (1, 8))),
        "up_weight_1": noise(splits[9], (DEPTH, D, FF), D ** -0.5, 0.1875, ((0, 4), (1, 8))),
        "down_weight_1": noise(splits[10], (DEPTH, FF, D), FF ** -0.5, 0.09375, ((0, 4), (1, 8))),
        "attn_gain_2": jnp.clip(1.0 + 0.18 * jax.random.normal(splits[11], (DEPTH, D), jnp.float32), 0.099609375, 1.8984375).astype(jnp.bfloat16),
        "query_weight_2": noise(splits[12], (DEPTH, D, D), D ** -0.5, 0.1875, ((0, 4), (1, 8))),
        "key_weight_2": noise(splits[13], (DEPTH, D, D), D ** -0.5, 0.1875, ((0, 4), (1, 8))),
        "value_weight_2": noise(splits[14], (DEPTH, D, D), D ** -0.5, 0.1875, ((0, 4), (1, 8))),
        "out_weight_2": noise(splits[15], (DEPTH, D, D), (D // 2) ** -0.5, 0.25, ((0, 4), (1, 8))),
        "ffn_gain_2": jnp.clip(1.0 + 0.18 * jax.random.normal(splits[16], (DEPTH, D), jnp.float32), 0.099609375, 1.8984375).astype(jnp.bfloat16),
        "gate_weight_2": noise(splits[17], (DEPTH, D, FF), D ** -0.5, 0.1875, ((0, 4), (1, 8))),
        "up_weight_2": noise(splits[18], (DEPTH, D, FF), D ** -0.5, 0.1875, ((0, 4), (1, 8))),
        "down_weight_2": noise(splits[19], (DEPTH, FF, D), FF ** -0.5, 0.09375, ((0, 4), (1, 8))),
        "out_grad": noise(splits[20], (FRAMES, DEPTH, D), 1.0, 6.0, ((0, 8), (1, 4))),
    }


EPSILON = 1e-05
HIGHEST = lax.Precision.HIGHEST

@jax.custom_vjp
def low(v):
    return lax.optimization_barrier(v.astype(jnp.bfloat16)).astype(jnp.float32)

@jax.custom_vjp
def low_back(v):
    return v

def low_keep(v):
    return (low(v), None)

def low_pass(kept, grad):
    return (grad,)

def back_keep(v):
    return (v, None)

def back_low(kept, grad):
    return (low(grad),)
low.defvjp(low_keep, low_pass)
low_back.defvjp(back_keep, back_low)

def rms_scale(state, gain):
    inverse = lax.rsqrt(lax.optimization_barrier(jnp.mean(state * state, axis=-1, keepdims=True)) + EPSILON)
    return state * inverse * gain[None]

def project(left, weight):
    return jnp.einsum('fpd,pde->fpe', left, weight, precision=HIGHEST)

def layer(state, params):
    attn_gain, query_w, key_w, value_w, out_w, ffn_gain, gate_w, up_w, down_w = params
    frames, depth = (state.shape[0], state.shape[1])
    normed = low(rms_scale(state, attn_gain))
    query = low_back(low(project(normed, query_w))).reshape(frames, depth, HEADS, HEAD_DIM)
    keys = low_back(low(project(normed, key_w))).reshape(frames, depth, HEADS, HEAD_DIM)
    values = low_back(low(project(normed, value_w))).reshape(frames, depth, HEADS, HEAD_DIM)
    scores = jnp.einsum('fphc,fshc->fhps', query, keys, precision=HIGHEST) * HEAD_DIM ** (-0.5)
    scores = low_back(scores)
    allowed = jnp.arange(depth)[:, None] >= jnp.arange(depth)[None, :]
    scores = jnp.where(allowed[None, None], scores, -1e+30)
    attend = low(jax.nn.softmax(scores, axis=-1))
    mixed = jnp.einsum('fhps,fshc->fphc', attend, values, precision=HIGHEST).reshape(frames, depth, D)
    mixed = low_back(low(mixed))
    middle = state + low_back(project(mixed, out_w))
    inner = low(rms_scale(middle, ffn_gain))
    gate = low_back(project(inner, gate_w))
    up = low_back(project(inner, up_w))
    hidden = low(jax.nn.silu(gate) * up)
    return middle + low_back(project(hidden, down_w))

def forward(state, counts, params):
    state = layer(state, params[0:9])
    state = layer(state, params[9:18])
    active = (jnp.arange(DEPTH)[None, :] < counts[:, None]).astype(jnp.float32)
    return state * active[:, :, None]

def reference(frames_in, depth_counts, attn_gain_1, query_weight_1, key_weight_1, value_weight_1, out_weight_1, ffn_gain_1, gate_weight_1, up_weight_1, down_weight_1, attn_gain_2, query_weight_2, key_weight_2, value_weight_2, out_weight_2, ffn_gain_2, gate_weight_2, up_weight_2, down_weight_2, out_grad):
    params = tuple((weight.astype(jnp.float32) for weight in (attn_gain_1, query_weight_1, key_weight_1, value_weight_1, out_weight_1, ffn_gain_1, gate_weight_1, up_weight_1, down_weight_1, attn_gain_2, query_weight_2, key_weight_2, value_weight_2, out_weight_2, ffn_gain_2, gate_weight_2, up_weight_2, down_weight_2)))
    inputs = frames_in.reshape(N_DP, FRAMES_DEV, DEPTH, D)
    counts = depth_counts.reshape(N_DP, FRAMES_DEV)
    cotangents = out_grad.reshape(N_DP, FRAMES_DEV, DEPTH, D)

    def step(totals, block):
        block_in, block_counts, block_grad = block

        def apply(state, *weights):
            return forward(state, block_counts, weights)
        result, pull = jax.vjp(apply, block_in.astype(jnp.float32), *params)
        pulled = pull(block_grad.astype(jnp.float32))
        totals = tuple((total + grad for total, grad in zip(totals, pulled[1:])))
        return (totals, (result.astype(jnp.bfloat16), pulled[0].astype(jnp.bfloat16)))
    zeros = tuple((jnp.zeros(param.shape, jnp.float32) for param in params))
    totals, (results, grads) = lax.scan(step, zeros, (inputs, counts, cotangents))
    return (results.reshape(FRAMES, DEPTH, D), grads.reshape(FRAMES, DEPTH, D), totals[0], totals[1], totals[2], totals[3], totals[4], totals[5], totals[6], totals[7], totals[8], totals[9], totals[10], totals[11], totals[12], totals[13], totals[14], totals[15], totals[16], totals[17])
```

```python
import functools

import jax
import jax.numpy as jnp
from jax import lax
from jax.sharding import PartitionSpec as P

HEAD_DIM = 64
MICRO = 2


EPSILON = 1e-05


def rms_apply(state, gain):
    inverse = lax.rsqrt(jnp.mean(state * state, axis=-1, keepdims=True) + EPSILON)
    return (state * inverse * gain.astype(jnp.float32)[None], inverse)


def rms_back(upper, state, inverse, gain):
    gain_grad = jnp.sum(upper * state * inverse, axis=0)
    scaled = upper * gain.astype(jnp.float32)[None]
    lower = inverse * scaled - state * (inverse * inverse * inverse) * jnp.mean(
        scaled * state, axis=-1, keepdims=True
    )
    return (lower, gain_grad)


def project(left, weight):
    return jnp.einsum("fpd,pde->fpe", left, weight, preferred_element_type=jnp.float32)


def project_back(grad, weight):
    return jnp.einsum("fpe,pde->fpd", grad, weight, preferred_element_type=jnp.float32)


def outer(left, grad):
    return jnp.einsum("fpd,fpe->pde", left, grad, preferred_element_type=jnp.float32)


def fetch(params):
    attn_gain, query_w, key_w, value_w, out_w, ffn_gain, gate_w, up_w, down_w = params
    return (
        lax.all_gather(attn_gain, "dp", axis=1, tiled=True),
        lax.all_gather(query_w, "dp", axis=1, tiled=True),
        lax.all_gather(key_w, "dp", axis=1, tiled=True),
        lax.all_gather(value_w, "dp", axis=1, tiled=True),
        lax.all_gather(out_w, "dp", axis=1, tiled=True),
        lax.all_gather(ffn_gain, "dp", axis=1, tiled=True),
        lax.all_gather(gate_w, "dp", axis=1, tiled=True),
        lax.all_gather(up_w, "dp", axis=1, tiled=True),
        lax.all_gather(down_w, "dp", axis=1, tiled=True),
    )


def fetch_again(params):
    attn_gain, query_w, key_w, value_w, out_w, ffn_gain, gate_w, up_w, down_w = params
    return (
        lax.all_gather(attn_gain, "dp", axis=1, tiled=True),
        lax.all_gather(query_w, "dp", axis=1, tiled=True),
        lax.all_gather(key_w, "dp", axis=1, tiled=True),
        lax.all_gather(value_w, "dp", axis=1, tiled=True),
        lax.all_gather(out_w, "dp", axis=1, tiled=True),
        lax.all_gather(ffn_gain, "dp", axis=1, tiled=True),
        lax.all_gather(gate_w, "dp", axis=1, tiled=True),
        lax.all_gather(up_w, "dp", axis=1, tiled=True),
        lax.all_gather(down_w, "dp", axis=1, tiled=True),
    )


def layer_forward(state, params, positions):
    attn_gain, query_w, key_w, value_w, out_w, ffn_gain, gate_w, up_w, down_w = params
    frames, local, width = state.shape
    heads = width // HEAD_DIM
    normed_full, inverse_one = rms_apply(state, attn_gain)
    normed = normed_full.astype(jnp.bfloat16)
    query = project(normed, query_w).astype(jnp.bfloat16)
    keys = project(normed, key_w).astype(jnp.bfloat16)
    values = project(normed, value_w).astype(jnp.bfloat16)
    all_keys, all_values = (
        lax.all_gather(keys, "section", axis=1, tiled=True),
        lax.all_gather(values, "section", axis=1, tiled=True),
    )
    depth = all_keys.shape[1]
    query_heads = query.reshape(frames, local, heads, HEAD_DIM)
    key_heads = all_keys.reshape(frames, depth, heads, HEAD_DIM)
    value_heads = all_values.reshape(frames, depth, heads, HEAD_DIM)
    scores = jnp.einsum(
        "fphc,fshc->fhps", query_heads, key_heads, preferred_element_type=jnp.float32
    ) * HEAD_DIM ** (-0.5)
    allowed = positions[:, None] >= jnp.arange(depth)[None, :]
    scores = jnp.where(allowed[None, None], scores, -1e30)
    largest = jnp.max(scores, axis=-1, keepdims=True)
    expd = jnp.exp(scores - largest)
    attend = expd / jnp.sum(expd, axis=-1, keepdims=True)
    attend_low = attend.astype(jnp.bfloat16)
    mixed = jnp.einsum(
        "fhps,fshc->fphc", attend_low, value_heads, preferred_element_type=jnp.float32
    )
    mixed = mixed.reshape(frames, local, width).astype(jnp.bfloat16)
    middle = state + project(mixed, out_w)
    inner_full, inverse_two = rms_apply(middle, ffn_gain)
    inner = inner_full.astype(jnp.bfloat16)
    gate = project(inner, gate_w)
    up = project(inner, up_w)
    hidden = (jax.nn.silu(gate) * up).astype(jnp.bfloat16)
    result = middle + project(hidden, down_w)
    kept = (
        state,
        inverse_one,
        normed,
        query_heads,
        key_heads,
        value_heads,
        attend,
        attend_low,
        mixed,
        middle,
        inverse_two,
        inner,
        gate,
        up,
        hidden,
    )
    return (result, kept)


def layer_backward(carried, params, kept):
    attn_gain, query_w, key_w, value_w, out_w, ffn_gain, gate_w, up_w, down_w = params
    (
        state,
        inverse_one,
        normed,
        query_heads,
        key_heads,
        value_heads,
        attend,
        attend_low,
        mixed,
        middle,
        inverse_two,
        inner,
        gate,
        up,
        hidden,
    ) = kept
    frames, local, width = state.shape
    depth = key_heads.shape[1]
    branch_grad = carried.astype(jnp.bfloat16)
    hidden_grad = project_back(branch_grad, down_w)
    sigma = jax.nn.sigmoid(gate)
    gate_grad = (hidden_grad * up * sigma * (1.0 + gate * (1.0 - sigma))).astype(jnp.bfloat16)
    up_grad = (hidden_grad * gate * sigma).astype(jnp.bfloat16)
    inner_grad = project_back(gate_grad, gate_w) + project_back(up_grad, up_w)
    lower_two, grad_ffn_gain = rms_back(inner_grad, middle, inverse_two, ffn_gain)
    middle_grad = carried + lower_two
    mixed_back = middle_grad.astype(jnp.bfloat16)
    mixed_grad = project_back(mixed_back, out_w).astype(jnp.bfloat16)
    mixed_heads = mixed_grad.reshape(frames, local, -1, HEAD_DIM)
    attend_grad = jnp.einsum(
        "fphc,fshc->fhps", mixed_heads, value_heads, preferred_element_type=jnp.float32
    )
    value_terms = jnp.einsum(
        "fhps,fphc->fshc", attend_low, mixed_heads, preferred_element_type=jnp.float32
    ).reshape(frames, depth, width)
    score_grad = attend * (attend_grad - jnp.sum(attend * attend_grad, axis=-1, keepdims=True))
    score_grad = score_grad.astype(jnp.bfloat16)
    scale = HEAD_DIM ** (-0.5)
    query_grad = (
        jnp.einsum("fhps,fshc->fphc", score_grad, key_heads, preferred_element_type=jnp.float32)
        * scale
    )
    query_grad = query_grad.reshape(frames, local, width).astype(jnp.bfloat16)
    key_terms = (
        jnp.einsum("fhps,fphc->fshc", score_grad, query_heads, preferred_element_type=jnp.float32)
        * scale
    )
    key_terms = key_terms.reshape(frames, depth, width)
    keys_sum, values_sum = (
        lax.psum_scatter(key_terms, "section", scatter_dimension=1, tiled=True),
        lax.psum_scatter(value_terms, "section", scatter_dimension=1, tiled=True),
    )
    keys_grad = keys_sum.astype(jnp.bfloat16)
    values_grad = values_sum.astype(jnp.bfloat16)
    normed_grad = (
        project_back(query_grad, query_w)
        + project_back(keys_grad, key_w)
        + project_back(values_grad, value_w)
    )
    lower_one, grad_attn_gain = rms_back(normed_grad, state, inverse_one, attn_gain)
    deferred = (
        grad_attn_gain,
        grad_ffn_gain,
        hidden,
        branch_grad,
        inner,
        gate_grad,
        up_grad,
        mixed,
        mixed_back,
        normed,
        query_grad,
        keys_grad,
        values_grad,
    )
    return (middle_grad + lower_one, deferred)


def join_deferred(pieces):
    gains = tuple(
        (sum((piece[index] for piece in pieces[1:])) + pieces[0][index] for index in (0, 1))
    )
    rest = tuple(
        (jnp.concatenate([piece[index] for piece in pieces], axis=0) for index in range(2, 13))
    )
    return gains + rest


def weight_terms(deferred):
    (
        grad_attn_gain,
        grad_ffn_gain,
        hidden,
        branch_grad,
        inner,
        gate_grad,
        up_grad,
        mixed,
        mixed_back,
        normed,
        query_grad,
        keys_grad,
        values_grad,
    ) = deferred
    return (
        grad_attn_gain,
        outer(normed, query_grad),
        outer(normed, keys_grad),
        outer(normed, values_grad),
        outer(mixed, mixed_back),
        grad_ffn_gain,
        outer(inner, gate_grad),
        outer(inner, up_grad),
        outer(hidden, branch_grad),
    )


def reduce_grads(full):
    (
        grad_attn_gain,
        grad_query,
        grad_key,
        grad_value,
        grad_out,
        grad_ffn_gain,
        grad_gate,
        grad_up,
        grad_down,
    ) = full
    return (
        lax.psum_scatter(grad_attn_gain, "dp", scatter_dimension=1, tiled=True),
        lax.psum_scatter(grad_query, "dp", scatter_dimension=1, tiled=True),
        lax.psum_scatter(grad_key, "dp", scatter_dimension=1, tiled=True),
        lax.psum_scatter(grad_value, "dp", scatter_dimension=1, tiled=True),
        lax.psum_scatter(grad_out, "dp", scatter_dimension=1, tiled=True),
        lax.psum_scatter(grad_ffn_gain, "dp", scatter_dimension=1, tiled=True),
        lax.psum_scatter(grad_gate, "dp", scatter_dimension=1, tiled=True),
        lax.psum_scatter(grad_up, "dp", scatter_dimension=1, tiled=True),
        lax.psum_scatter(grad_down, "dp", scatter_dimension=1, tiled=True),
    )


def body(
    frames_in,
    depth_counts,
    attn_gain_1,
    query_weight_1,
    key_weight_1,
    value_weight_1,
    out_weight_1,
    ffn_gain_1,
    gate_weight_1,
    up_weight_1,
    down_weight_1,
    attn_gain_2,
    query_weight_2,
    key_weight_2,
    value_weight_2,
    out_weight_2,
    ffn_gain_2,
    gate_weight_2,
    up_weight_2,
    down_weight_2,
    out_grad,
):
    layers = (
        (
            attn_gain_1,
            query_weight_1,
            key_weight_1,
            value_weight_1,
            out_weight_1,
            ffn_gain_1,
            gate_weight_1,
            up_weight_1,
            down_weight_1,
        ),
        (
            attn_gain_2,
            query_weight_2,
            key_weight_2,
            value_weight_2,
            out_weight_2,
            ffn_gain_2,
            gate_weight_2,
            up_weight_2,
            down_weight_2,
        ),
    )
    frames_dev = frames_in.shape[0]
    local = frames_in.shape[1]
    portion = frames_dev // MICRO
    positions = lax.axis_index("section") * local + jnp.arange(local)
    active = positions[None, :] < depth_counts[:, None]
    gathered = [fetch(layers[0]), fetch(layers[1])]
    keeps = [[], []]
    results = []
    for micro in range(MICRO):
        state = frames_in[micro * portion : (micro + 1) * portion].astype(jnp.float32)
        for number in (0, 1):
            state, kept = layer_forward(state, gathered[number], positions)
            keeps[number].append(kept)
        results.append(state)
    state = jnp.concatenate(results, axis=0)
    frames_out = jnp.where(active[:, :, None], state, 0.0).astype(jnp.bfloat16)
    masked = jnp.where(active[:, :, None], out_grad.astype(jnp.float32), 0.0)
    carries = [masked[micro * portion : (micro + 1) * portion] for micro in range(MICRO)]
    reduced = [None, None]
    for number in (1, 0):
        params = fetch_again(layers[number])
        pieces = []
        for micro in range(MICRO):
            carries[micro], deferred = layer_backward(carries[micro], params, keeps[number][micro])
            pieces.append(deferred)
        reduced[number] = reduce_grads(weight_terms(join_deferred(pieces)))
    first, second = reduced
    input_grad = jnp.concatenate(carries, axis=0).astype(jnp.bfloat16)
    return (
        frames_out,
        input_grad,
        first[0],
        first[1],
        first[2],
        first[3],
        first[4],
        first[5],
        first[6],
        first[7],
        first[8],
        second[0],
        second[1],
        second[2],
        second[3],
        second[4],
        second[5],
        second[6],
        second[7],
        second[8],
    )


HEAD_LANES = 128


def widen(value):
    return value.astype(jnp.float32)


def low(value):
    return value.astype(jnp.bfloat16)


def dot(left, right):
    return jnp.dot(left, right, preferred_element_type=jnp.float32)


def dot_rows(left, right):
    return lax.dot_general(left, right, (((0,), (0,)), ((), ())), preferred_element_type=jnp.float32)


def dot_back(left, right):
    return lax.dot_general(left, right, (((1,), (1,)), ((), ())), preferred_element_type=jnp.float32)


def to_columns(weights, count):
    rows = weights[0].shape[0]
    parts = [weight.reshape(rows, count, -1) for weight in weights]
    joined = jnp.concatenate(parts, axis=-1).transpose(1, 0, 2)
    return lax.all_to_all(joined, "dp", 0, 0).reshape(count * rows, -1)


def to_rows(grad, widths, count):
    rows = grad.shape[0] // count
    moved = lax.all_to_all(low(grad).reshape(count, rows, -1), "dp", 0, 0)
    outs = []
    start = 0
    for width in widths:
        part = moved[:, :, start : start + width].transpose(1, 0, 2)
        outs.append(widen(part.reshape(rows, -1)))
        start += width
    return outs


def gather(block):
    return lax.all_gather(block, "dp", axis=0, tiled=True)


def scatter(partial):
    return widen(lax.psum_scatter(low(partial), "dp", scatter_dimension=0, tiled=True))


def segment_sum(value, segments):
    high = low(value)
    rest = low(value - widen(high))
    return dot(high, segments) + dot(rest, segments)


def attend_of(query, keys, segments, place):
    scores = [
        jnp.where(index <= place, segment_sum(widen(query) * widen(key), segments) * HEAD_DIM ** (-0.5), -1e30)
        for index, key in enumerate(keys)
    ]
    largest = functools.reduce(jnp.maximum, scores)
    expd = [jnp.exp(score - largest) for score in scores]
    total = sum(expd)
    return [value / total for value in expd]


def norm(state, gain):
    inverse = lax.rsqrt(jnp.mean(state * state, axis=-1, keepdims=True) + EPSILON)
    return state * inverse * gain, inverse


def norm_back(upper, state, inverse, gain):
    gain_grad = jnp.sum(upper * state * inverse, axis=0)
    scaled = upper * gain
    lower = inverse * scaled - state * (inverse * inverse * inverse) * jnp.mean(scaled * state, axis=-1, keepdims=True)
    return lower, gain_grad


def split_body(*args):
    frames_in, depth_counts, out_grad = args[0][:, 0], args[1], args[-1][:, 0]
    count = lax.axis_size("dp")
    place = lax.axis_index("section")
    active = (place < depth_counts)[:, None]
    lanes = jnp.arange(HEAD_LANES) // HEAD_DIM
    segments = low((lanes[:, None] == lanes[None, :]).astype(jnp.float32))
    layers = [tuple(a[0] for a in args[2:11]), tuple(a[0] for a in args[11:20])]
    state = widen(frames_in)
    kept = []
    for attn_gain, query_w, key_w, value_w, out_w, ffn_gain, gate_w, up_w, down_w in layers:
        attn_gain = widen(lax.all_gather(attn_gain, "dp", axis=0, tiled=True))
        ffn_gain = widen(lax.all_gather(ffn_gain, "dp", axis=0, tiled=True))
        first_w = to_columns([query_w, key_w, value_w], count)
        second_w = to_columns([gate_w, up_w], count)
        normed, inverse_one = norm(state, attn_gain)
        normed = gather(low(normed))
        packed = low(dot(normed, first_w))
        width = packed.shape[1] // 3
        query = packed[:, :width]
        pairs = lax.all_gather(packed[:, width:], "section", axis=0)
        keys = [pairs[i, :, :width] for i in range(pairs.shape[0])]
        values = [pairs[i, :, width:] for i in range(pairs.shape[0])]
        attend = attend_of(query, keys, segments, place)
        mixed = low(sum(widen(low(a)) * widen(v) for a, v in zip(attend, values)))
        middle = state + scatter(dot(mixed, out_w))
        inner, inverse_two = norm(middle, ffn_gain)
        inner = gather(low(inner))
        both = dot(inner, second_w)
        half = both.shape[1] // 2
        gate, up = both[:, :half], both[:, half:]
        hidden = low(jax.nn.silu(gate) * up)
        after = middle + scatter(dot(hidden, down_w))
        kept.append((attn_gain, first_w, out_w, ffn_gain, second_w, down_w, state, inverse_one, normed, query, keys, values, attend, mixed, middle, inverse_two, inner, gate, up, hidden))
        state = after
    frames_out = low(jnp.where(active, state, 0.0))
    carried = jnp.where(active, widen(out_grad), 0.0)
    grads = [None, None]
    for number in (1, 0):
        attn_gain, first_w, out_w, ffn_gain, second_w, down_w, state, inverse_one, normed, query, keys, values, attend, mixed, middle, inverse_two, inner, gate, up, hidden = kept[number]
        branch = gather(low(carried))
        grad_down = dot_rows(hidden, branch)
        hidden_grad = dot_back(branch, down_w)
        sigma = jax.nn.sigmoid(gate)
        both_grad = low(jnp.concatenate([hidden_grad * up * sigma * (1.0 + gate * (1.0 - sigma)), hidden_grad * gate * sigma], axis=1))
        half = gate.shape[1]
        grad_gate, grad_up = to_rows(dot_rows(inner, both_grad), (half, half), count)
        lower, ffn_gain_grad = norm_back(scatter(dot_back(both_grad, second_w)), middle, inverse_two, ffn_gain)
        middle_grad = carried + lower
        back = gather(low(middle_grad))
        grad_out = dot_rows(mixed, back)
        mixed_grad = widen(low(dot_back(back, out_w)))
        attend_grad = [segment_sum(mixed_grad * widen(v), segments) for v in values]
        inside = sum(a * g for a, g in zip(attend, attend_grad))
        score_grad = [widen(low(a * (g - inside))) for a, g in zip(attend, attend_grad)]
        scale = HEAD_DIM ** (-0.5)
        query_grad = low(sum(g * widen(k) for g, k in zip(score_grad, keys)) * scale)
        terms = jnp.stack([low(jnp.concatenate([g * widen(query) * scale, widen(low(a)) * mixed_grad], axis=1)) for g, a in zip(score_grad, attend)])
        pair_grad = low(jnp.sum(widen(lax.all_to_all(terms, "section", 0, 0)), axis=0))
        packed_grad = jnp.concatenate([query_grad, pair_grad], axis=1)
        width = query.shape[1]
        grad_query, grad_key, grad_value = to_rows(dot_rows(normed, packed_grad), (width, width, width), count)
        lower, attn_gain_grad = norm_back(scatter(dot_back(packed_grad, first_w)), state, inverse_one, attn_gain)
        carried = middle_grad + lower
        gains = lax.psum_scatter(jnp.stack([attn_gain_grad, ffn_gain_grad]), "dp", scatter_dimension=1, tiled=True)
        grads[number] = (gains[0], grad_query, grad_key, grad_value, grad_out, gains[1], grad_gate, grad_up, grad_down)
    outs = [frames_out[:, None], low(carried)[:, None]]
    return tuple(outs) + tuple(g[None] for layer in grads for g in layer)


def solution(mesh):
    in_specs = (
        P("dp", "section", None),
        P("dp"),
        P("section", "dp"),
        P("section", "dp", None),
        P("section", "dp", None),
        P("section", "dp", None),
        P("section", "dp", None),
        P("section", "dp"),
        P("section", "dp", None),
        P("section", "dp", None),
        P("section", "dp", None),
        P("section", "dp"),
        P("section", "dp", None),
        P("section", "dp", None),
        P("section", "dp", None),
        P("section", "dp", None),
        P("section", "dp"),
        P("section", "dp", None),
        P("section", "dp", None),
        P("section", "dp", None),
        P("dp", "section", None),
    )
    out_specs = (
        P("dp", "section", None),
        P("dp", "section", None),
        P("section", "dp"),
        P("section", "dp", None),
        P("section", "dp", None),
        P("section", "dp", None),
        P("section", "dp", None),
        P("section", "dp"),
        P("section", "dp", None),
        P("section", "dp", None),
        P("section", "dp", None),
        P("section", "dp"),
        P("section", "dp", None),
        P("section", "dp", None),
        P("section", "dp", None),
        P("section", "dp", None),
        P("section", "dp"),
        P("section", "dp", None),
        P("section", "dp", None),
        P("section", "dp", None),
    )
    parts = mesh.shape["dp"]
    heads = 1024 // HEAD_DIM
    chosen = split_body if heads % parts == 0 and heads // parts * HEAD_DIM == HEAD_LANES else body
    return jax.shard_map(chosen, mesh=mesh, in_specs=in_specs, out_specs=out_specs, check_vma=False)
```

```python
import functools

import jax
import jax.numpy as jnp
from jax import lax
from jax.experimental import pallas as pl
from jax.experimental.pallas import tpu as pltpu
from jax.sharding import PartitionSpec as P

HEAD_DIM = 64
MICRO = 2


EPSILON = 1e-05
VMEM_BYTES = 63 * 2**20


def rms_apply(state, gain):
    inverse = lax.rsqrt(jnp.mean(state * state, axis=-1, keepdims=True) + EPSILON)
    return (state * inverse * gain.astype(jnp.float32)[None], inverse)


def rms_back(upper, state, inverse, gain):
    gain_grad = jnp.sum(upper * state * inverse, axis=0)
    scaled = upper * gain.astype(jnp.float32)[None]
    lower = inverse * scaled - state * (inverse * inverse * inverse) * jnp.mean(
        scaled * state, axis=-1, keepdims=True
    )
    return (lower, gain_grad)


def project(left, weight):
    return jnp.einsum("fpd,pde->fpe", left, weight, preferred_element_type=jnp.float32)


def project_back(grad, weight):
    return jnp.einsum("fpe,pde->fpd", grad, weight, preferred_element_type=jnp.float32)


def outer(left, grad):
    return jnp.einsum("fpd,fpe->pde", left, grad, preferred_element_type=jnp.float32)


def fetch(params):
    attn_gain, query_w, key_w, value_w, out_w, ffn_gain, gate_w, up_w, down_w = params
    return (
        lax.all_gather(attn_gain, "dp", axis=1, tiled=True),
        lax.all_gather(query_w, "dp", axis=1, tiled=True),
        lax.all_gather(key_w, "dp", axis=1, tiled=True),
        lax.all_gather(value_w, "dp", axis=1, tiled=True),
        lax.all_gather(out_w, "dp", axis=1, tiled=True),
        lax.all_gather(ffn_gain, "dp", axis=1, tiled=True),
        lax.all_gather(gate_w, "dp", axis=1, tiled=True),
        lax.all_gather(up_w, "dp", axis=1, tiled=True),
        lax.all_gather(down_w, "dp", axis=1, tiled=True),
    )


def fetch_again(params):
    attn_gain, query_w, key_w, value_w, out_w, ffn_gain, gate_w, up_w, down_w = params
    return (
        lax.all_gather(attn_gain, "dp", axis=1, tiled=True),
        lax.all_gather(query_w, "dp", axis=1, tiled=True),
        lax.all_gather(key_w, "dp", axis=1, tiled=True),
        lax.all_gather(value_w, "dp", axis=1, tiled=True),
        lax.all_gather(out_w, "dp", axis=1, tiled=True),
        lax.all_gather(ffn_gain, "dp", axis=1, tiled=True),
        lax.all_gather(gate_w, "dp", axis=1, tiled=True),
        lax.all_gather(up_w, "dp", axis=1, tiled=True),
        lax.all_gather(down_w, "dp", axis=1, tiled=True),
    )


def layer_forward(state, params, positions):
    attn_gain, query_w, key_w, value_w, out_w, ffn_gain, gate_w, up_w, down_w = params
    frames, local, width = state.shape
    heads = width // HEAD_DIM
    normed_full, inverse_one = rms_apply(state, attn_gain)
    normed = normed_full.astype(jnp.bfloat16)
    query = project(normed, query_w).astype(jnp.bfloat16)
    keys = project(normed, key_w).astype(jnp.bfloat16)
    values = project(normed, value_w).astype(jnp.bfloat16)
    all_keys, all_values = (
        lax.all_gather(keys, "section", axis=1, tiled=True),
        lax.all_gather(values, "section", axis=1, tiled=True),
    )
    depth = all_keys.shape[1]
    query_heads = query.reshape(frames, local, heads, HEAD_DIM)
    key_heads = all_keys.reshape(frames, depth, heads, HEAD_DIM)
    value_heads = all_values.reshape(frames, depth, heads, HEAD_DIM)
    scores = jnp.einsum(
        "fphc,fshc->fhps", query_heads, key_heads, preferred_element_type=jnp.float32
    ) * HEAD_DIM ** (-0.5)
    allowed = positions[:, None] >= jnp.arange(depth)[None, :]
    scores = jnp.where(allowed[None, None], scores, -1e30)
    largest = jnp.max(scores, axis=-1, keepdims=True)
    expd = jnp.exp(scores - largest)
    attend = expd / jnp.sum(expd, axis=-1, keepdims=True)
    attend_low = attend.astype(jnp.bfloat16)
    mixed = jnp.einsum(
        "fhps,fshc->fphc", attend_low, value_heads, preferred_element_type=jnp.float32
    )
    mixed = mixed.reshape(frames, local, width).astype(jnp.bfloat16)
    middle = state + project(mixed, out_w)
    inner_full, inverse_two = rms_apply(middle, ffn_gain)
    inner = inner_full.astype(jnp.bfloat16)
    gate = project(inner, gate_w)
    up = project(inner, up_w)
    hidden = (jax.nn.silu(gate) * up).astype(jnp.bfloat16)
    result = middle + project(hidden, down_w)
    kept = (
        state,
        inverse_one,
        normed,
        query_heads,
        key_heads,
        value_heads,
        attend,
        attend_low,
        mixed,
        middle,
        inverse_two,
        inner,
        gate,
        up,
        hidden,
    )
    return (result, kept)


def layer_backward(carried, params, kept):
    attn_gain, query_w, key_w, value_w, out_w, ffn_gain, gate_w, up_w, down_w = params
    (
        state,
        inverse_one,
        normed,
        query_heads,
        key_heads,
        value_heads,
        attend,
        attend_low,
        mixed,
        middle,
        inverse_two,
        inner,
        gate,
        up,
        hidden,
    ) = kept
    frames, local, width = state.shape
    depth = key_heads.shape[1]
    branch_grad = carried.astype(jnp.bfloat16)
    hidden_grad = project_back(branch_grad, down_w)
    sigma = jax.nn.sigmoid(gate)
    gate_grad = (hidden_grad * up * sigma * (1.0 + gate * (1.0 - sigma))).astype(jnp.bfloat16)
    up_grad = (hidden_grad * gate * sigma).astype(jnp.bfloat16)
    inner_grad = project_back(gate_grad, gate_w) + project_back(up_grad, up_w)
    lower_two, grad_ffn_gain = rms_back(inner_grad, middle, inverse_two, ffn_gain)
    middle_grad = carried + lower_two
    mixed_back = middle_grad.astype(jnp.bfloat16)
    mixed_grad = project_back(mixed_back, out_w).astype(jnp.bfloat16)
    mixed_heads = mixed_grad.reshape(frames, local, -1, HEAD_DIM)
    attend_grad = jnp.einsum(
        "fphc,fshc->fhps", mixed_heads, value_heads, preferred_element_type=jnp.float32
    )
    value_terms = jnp.einsum(
        "fhps,fphc->fshc", attend_low, mixed_heads, preferred_element_type=jnp.float32
    ).reshape(frames, depth, width)
    score_grad = attend * (attend_grad - jnp.sum(attend * attend_grad, axis=-1, keepdims=True))
    score_grad = score_grad.astype(jnp.bfloat16)
    scale = HEAD_DIM ** (-0.5)
    query_grad = (
        jnp.einsum("fhps,fshc->fphc", score_grad, key_heads, preferred_element_type=jnp.float32)
        * scale
    )
    query_grad = query_grad.reshape(frames, local, width).astype(jnp.bfloat16)
    key_terms = (
        jnp.einsum("fhps,fphc->fshc", score_grad, query_heads, preferred_element_type=jnp.float32)
        * scale
    )
    key_terms = key_terms.reshape(frames, depth, width)
    keys_sum, values_sum = (
        lax.psum_scatter(key_terms, "section", scatter_dimension=1, tiled=True),
        lax.psum_scatter(value_terms, "section", scatter_dimension=1, tiled=True),
    )
    keys_grad = keys_sum.astype(jnp.bfloat16)
    values_grad = values_sum.astype(jnp.bfloat16)
    normed_grad = (
        project_back(query_grad, query_w)
        + project_back(keys_grad, key_w)
        + project_back(values_grad, value_w)
    )
    lower_one, grad_attn_gain = rms_back(normed_grad, state, inverse_one, attn_gain)
    deferred = (
        grad_attn_gain,
        grad_ffn_gain,
        hidden,
        branch_grad,
        inner,
        gate_grad,
        up_grad,
        mixed,
        mixed_back,
        normed,
        query_grad,
        keys_grad,
        values_grad,
    )
    return (middle_grad + lower_one, deferred)


def join_deferred(pieces):
    gains = tuple(
        (sum((piece[index] for piece in pieces[1:])) + pieces[0][index] for index in (0, 1))
    )
    rest = tuple(
        (jnp.concatenate([piece[index] for piece in pieces], axis=0) for index in range(2, 13))
    )
    return gains + rest


def weight_terms(deferred):
    (
        grad_attn_gain,
        grad_ffn_gain,
        hidden,
        branch_grad,
        inner,
        gate_grad,
        up_grad,
        mixed,
        mixed_back,
        normed,
        query_grad,
        keys_grad,
        values_grad,
    ) = deferred
    return (
        grad_attn_gain,
        outer(normed, query_grad),
        outer(normed, keys_grad),
        outer(normed, values_grad),
        outer(mixed, mixed_back),
        grad_ffn_gain,
        outer(inner, gate_grad),
        outer(inner, up_grad),
        outer(hidden, branch_grad),
    )


def reduce_grads(full):
    (
        grad_attn_gain,
        grad_query,
        grad_key,
        grad_value,
        grad_out,
        grad_ffn_gain,
        grad_gate,
        grad_up,
        grad_down,
    ) = full
    return (
        lax.psum_scatter(grad_attn_gain, "dp", scatter_dimension=1, tiled=True),
        lax.psum_scatter(grad_query, "dp", scatter_dimension=1, tiled=True),
        lax.psum_scatter(grad_key, "dp", scatter_dimension=1, tiled=True),
        lax.psum_scatter(grad_value, "dp", scatter_dimension=1, tiled=True),
        lax.psum_scatter(grad_out, "dp", scatter_dimension=1, tiled=True),
        lax.psum_scatter(grad_ffn_gain, "dp", scatter_dimension=1, tiled=True),
        lax.psum_scatter(grad_gate, "dp", scatter_dimension=1, tiled=True),
        lax.psum_scatter(grad_up, "dp", scatter_dimension=1, tiled=True),
        lax.psum_scatter(grad_down, "dp", scatter_dimension=1, tiled=True),
    )


def body(
    frames_in,
    depth_counts,
    attn_gain_1,
    query_weight_1,
    key_weight_1,
    value_weight_1,
    out_weight_1,
    ffn_gain_1,
    gate_weight_1,
    up_weight_1,
    down_weight_1,
    attn_gain_2,
    query_weight_2,
    key_weight_2,
    value_weight_2,
    out_weight_2,
    ffn_gain_2,
    gate_weight_2,
    up_weight_2,
    down_weight_2,
    out_grad,
):
    layers = (
        (
            attn_gain_1,
            query_weight_1,
            key_weight_1,
            value_weight_1,
            out_weight_1,
            ffn_gain_1,
            gate_weight_1,
            up_weight_1,
            down_weight_1,
        ),
        (
            attn_gain_2,
            query_weight_2,
            key_weight_2,
            value_weight_2,
            out_weight_2,
            ffn_gain_2,
            gate_weight_2,
            up_weight_2,
            down_weight_2,
        ),
    )
    frames_dev = frames_in.shape[0]
    local = frames_in.shape[1]
    portion = frames_dev // MICRO
    positions = lax.axis_index("section") * local + jnp.arange(local)
    active = positions[None, :] < depth_counts[:, None]
    gathered = [fetch(layers[0]), fetch(layers[1])]
    keeps = [[], []]
    results = []
    for micro in range(MICRO):
        state = frames_in[micro * portion : (micro + 1) * portion].astype(jnp.float32)
        for number in (0, 1):
            state, kept = layer_forward(state, gathered[number], positions)
            keeps[number].append(kept)
        results.append(state)
    state = jnp.concatenate(results, axis=0)
    frames_out = jnp.where(active[:, :, None], state, 0.0).astype(jnp.bfloat16)
    masked = jnp.where(active[:, :, None], out_grad.astype(jnp.float32), 0.0)
    carries = [masked[micro * portion : (micro + 1) * portion] for micro in range(MICRO)]
    reduced = [None, None]
    for number in (1, 0):
        params = fetch_again(layers[number])
        pieces = []
        for micro in range(MICRO):
            carries[micro], deferred = layer_backward(carries[micro], params, keeps[number][micro])
            pieces.append(deferred)
        reduced[number] = reduce_grads(weight_terms(join_deferred(pieces)))
    first, second = reduced
    input_grad = jnp.concatenate(carries, axis=0).astype(jnp.bfloat16)
    return (
        frames_out,
        input_grad,
        first[0],
        first[1],
        first[2],
        first[3],
        first[4],
        first[5],
        first[6],
        first[7],
        first[8],
        second[0],
        second[1],
        second[2],
        second[3],
        second[4],
        second[5],
        second[6],
        second[7],
        second[8],
    )


HEAD_LANES = 128
CHAIN = 4
CHUNK = 16
MESH = pl.DeviceIdType.MESH


def widen(value):
    return value.astype(jnp.float32)


def low(value):
    return value.astype(jnp.bfloat16)


def dot(left, right):
    return jnp.dot(left, right, preferred_element_type=jnp.float32)


def dot_rows(left, right):
    return lax.dot_general(left, right, (((0,), (0,)), ((), ())), preferred_element_type=jnp.float32)


def dot_back(left, right):
    return lax.dot_general(left, right, (((1,), (1,)), ((), ())), preferred_element_type=jnp.float32)


def looped(count, step):
    lax.fori_loop(0, count, lambda index, carry: (step(index), carry)[1], 0)


def by_rows(rows, step, size=CHUNK):
    looped(rows // size, lambda index: step(pl.ds(pl.multiple_of(index * size, size), size)))


def split_kernel(*refs):
    (frames_ref, cot_ref, active_ref, gains_ref, segments_ref), refs = refs[:5], refs[5:]
    weights, refs = (refs[:7], refs[7:14]), refs[14:]
    (frames_out, input_grad, gains_out), refs = refs[:3], refs[3:]
    grads, refs = (refs[:7], refs[7:14]), refs[14:]
    (
        first_w, second_w, out_w, down_w, normed, inner, branch, back, query, pairs, mixed, both, hidden,
        both_grad, packed_grad, pair_in, pair_out, part, core_in, chain_in, chain_out, states, carry,
        gain_in, gain_full, gain_sum, gain_back, stage_first, stage_second, stage_down, stage_out,
    ), refs = refs[:31], refs[31:]
    (
        gather_send, gather_recv, core_send, core_recv, chain_send, chain_recv, pair_send, pair_recv,
        terms_send, terms_recv, weight_send, weight_recv, grad_send, grad_recv, gain_send, gain_recv,
        sum_send, sum_recv, local_sem,
    ) = refs

    rows, width = frames_ref.shape
    count = 2 * CHAIN
    lanes = width // count
    hidden_cols = second_w.shape[2] // 2
    group = 2 * rows
    depth = pairs.shape[1]
    scale = HEAD_DIM ** (-0.5)
    place = lax.axis_index("section")
    spot = lax.axis_index("dp")
    z = spot // 2
    core = spot % 2
    twin = 1 - core

    def at(chip, which):
        return (place, chip * 2 + which)

    def send(source, target, send_sem, recv_sem, device):
        pltpu.make_async_remote_copy(
            src_ref=source, dst_ref=target, send_sem=send_sem, recv_sem=recv_sem, device_id=device, device_id_type=MESH
        ).start()

    def wait(ref, sem):
        pltpu.make_async_copy(ref, ref, sem).wait()

    def block(index):
        return pl.ds(pl.multiple_of(index * rows, rows), rows)

    def grouped(index):
        return pl.ds(pl.multiple_of(index * group, group), group)

    def column(index, size):
        return pl.ds(pl.multiple_of(index * size, size), size)

    def other(step):
        hop, cross = step // 2, step % 2
        chip = jnp.where(hop == 1, z + 1 - 2 * (z % 2), jnp.where(hop == 2, (z + 2) % 4, jnp.where(hop == 3, 3 - z, z)))
        return chip * 2 + jnp.where(cross == 1, twin, core)

    barrier = pltpu.get_barrier_semaphore()
    for step in range(1, count):
        pl.semaphore_signal(barrier, inc=1, device_id=(place, (spot + step) % count), device_id_type=MESH)
    for step in range(1, depth):
        pl.semaphore_signal(barrier, inc=1, device_id=((place + step) % depth, spot), device_id_type=MESH)

    loads = []
    for layer in range(2):
        loads.append(pltpu.make_async_copy(weights[layer][3], out_w.at[layer], local_sem.at[2 * layer]))
        loads.append(pltpu.make_async_copy(weights[layer][6], down_w.at[layer], local_sem.at[2 * layer + 1]))
    for load in loads:
        load.start()
    mine = pl.ds(pl.multiple_of(spot * lanes, lanes), lanes)

    def weight_parts(layer):
        for number in range(3):
            yield weights[layer][number], first_w, number * lanes, lanes, number
        for number in range(2):
            yield weights[layer][4 + number], second_w, number * hidden_cols, hidden_cols, 3 + number

    def own_weights(layer):
        for source, held, start, size, number in weight_parts(layer):
            yield pltpu.make_async_copy(
                source.at[:, column(spot, size)], held.at[layer, mine, start : start + size], weight_recv.at[layer, number, spot]
            )

    for layer in range(2):
        for copy in own_weights(layer):
            copy.start()

    def send_weights(layer, numbers, step):
        target = other(step)
        for source, held, start, size, number in weight_parts(layer):
            if number in numbers:
                send(
                    source.at[:, column(target, size)],
                    held.at[layer, mine, start : start + size],
                    weight_send.at[layer, number, step],
                    weight_recv.at[layer, number, spot],
                    (place, target),
                )

    def wait_weights(layer, numbers):
        def arrived(index):
            for _, held, start, size, number in weight_parts(layer):
                if number in numbers:
                    wait(held.at[layer, column(index, lanes), start : start + size], weight_recv.at[layer, number, index])

        looped(count, arrived)

    def finish_weights(layer):
        def sent(index):
            for _, held, start, size, number in weight_parts(layer):
                wait(held.at[layer, pl.ds(0, lanes), start : start + size], weight_send.at[layer, number, index + 1])

        looped(count - 1, sent)

    for layer in range(2):
        for source in range(1, depth):

            @pl.when(place < source)
            def _():
                pairs[layer, source] = jnp.zeros(pairs.shape[2:], pairs.dtype)

            @pl.when(place >= source)
            def _():
                pair_in[layer, source - 1] = jnp.zeros(pair_in.shape[2:], pair_in.dtype)

    for parity in range(2):

        @pl.when(z == 0)
        def _():
            for index in range(CHAIN):
                chain_in[parity, index] = jnp.zeros(chain_in.shape[2:], chain_in.dtype)

        @pl.when(z == CHAIN - 1)
        def _():
            for index in (0, 1, 2, 4):
                chain_in[parity, index] = jnp.zeros(chain_in.shape[2:], chain_in.dtype)

    gain_in[spot] = gains_ref[...]
    gain_sum[...] = jnp.zeros_like(gain_sum)

    pl.semaphore_wait(barrier, count - 1 + depth - 1)

    for step in range(1, count):
        send(gains_ref, gain_in.at[spot], gain_send.at[step], gain_recv.at[spot], (place, other(step)))
    looped(count - 1, lambda index: send_weights(0, (0, 1, 2), index + 1))

    def gather_start(number, held):
        own = held.at[block(spot)]
        send(own, own, gather_send.at[number, 0], gather_recv.at[number, spot], at(z, twin))

        @pl.when(z < CHAIN - 1)
        def _():
            send(own, own, gather_send.at[number, 1], gather_recv.at[number, spot], at(z + 1, core))

        @pl.when(z > 0)
        def _():
            send(own, own, gather_send.at[number, 2], gather_recv.at[number, spot], at(z - 1, core))

    def gather_loop(number, held, compute, slack):
        def step(index):
            below, above = z - index, z + index

            @pl.when((index > 0) & (below >= 0))
            def _():
                here = held.at[block(below * 2 + core)]
                wait(here, gather_recv.at[number, below * 2 + core])

                @pl.when(z < CHAIN - 1)
                def _():
                    send(here, here, gather_send.at[number, 2 + index], gather_recv.at[number, below * 2 + core], at(z + 1, core))

                send(here, here, gather_send.at[number, 8 + index], gather_recv.at[number, below * 2 + core], at(z, twin))

            @pl.when((index > 0) & (above < CHAIN))
            def _():
                here = held.at[block(above * 2 + core)]
                wait(here, gather_recv.at[number, above * 2 + core])

                @pl.when(z > 0)
                def _():
                    send(here, here, gather_send.at[number, 5 + index], gather_recv.at[number, above * 2 + core], at(z - 1, core))

                send(here, here, gather_send.at[number, 11 + index], gather_recv.at[number, above * 2 + core], at(z, twin))

            slack(index)

            def side(which):
                chip = z - index + 2 * index * which

                @pl.when((chip >= 0) & (chip < CHAIN) & (index + 1 > which))
                def _():
                    wait(held.at[block(chip * 2 + twin)], gather_recv.at[number, chip * 2 + twin])
                    compute(chip)

            looped(2, side)

        looped(CHAIN, step)

    def gather_finish(number, held):
        one = held.at[block(0)]
        wait(one, gather_send.at[number, 0])

        @pl.when(z < CHAIN - 1)
        def _():
            wait(one, gather_send.at[number, 1])

        @pl.when(z > 0)
        def _():
            wait(one, gather_send.at[number, 2])

        def step(index):
            @pl.when(z - index >= 0)
            def _():
                @pl.when(z < CHAIN - 1)
                def _():
                    wait(one, gather_send.at[number, 2 + index])

                wait(one, gather_send.at[number, 8 + index])

            @pl.when(z + index < CHAIN)
            def _():
                @pl.when(z > 0)
                def _():
                    wait(one, gather_send.at[number, 5 + index])

                wait(one, gather_send.at[number, 11 + index])

        looped(CHAIN - 1, lambda index: step(index + 1))

    def order(index):
        first = 3 * (1 - z // 2)
        second = 2 * (1 - z % 2) + z // 2
        third = 1 + z % 2
        return jnp.where(index == 0, first, jnp.where(index == 1, second, jnp.where(index == 2, third, z)))

    def scatter_loop(number, compute, sink, slack):
        parity = number % 2

        def step(index):
            @pl.when(index < CHAIN)
            def _():
                slot = index % 2

                @pl.when(index > 1)
                def _():
                    wait(part.at[slot, twin], core_send.at[number, index - 2])

                compute(order(index), part.at[slot])
                send(part.at[slot, twin], core_in.at[parity, index], core_send.at[number, index], core_recv.at[number, index], at(z, twin))

            @pl.when(index > 0)
            def _():
                held = index - 1
                slot = held % 2
                target = order(held)
                wait(core_in.at[parity, held], core_recv.at[number, held])

                @pl.when(held < CHAIN - 1)
                def _():
                    @pl.when(((target > z) & (z > 0)) | ((target < z) & (z < CHAIN - 1)))
                    def _():
                        wait(chain_in.at[parity, target], chain_recv.at[number, target])

                    def add(at_rows):
                        total = part[slot, core, at_rows] + core_in[parity, held, at_rows]
                        chain_out[held, at_rows] = low(total + widen(chain_in[parity, target, at_rows]))

                    by_rows(rows, add)

                    @pl.when(target > z)
                    def _():
                        send(chain_out.at[held], chain_in.at[parity, target], chain_send.at[number, held], chain_recv.at[number, target], at(z + 1, core))

                    @pl.when(target < z)
                    def _():
                        landing = jnp.where(target == z - 1, CHAIN, target)
                        send(chain_out.at[held], chain_in.at[parity, landing], chain_send.at[number, held], chain_recv.at[number, landing], at(z - 1, core))

                @pl.when(held == CHAIN - 1)
                def _():
                    @pl.when(z > 0)
                    def _():
                        wait(chain_in.at[parity, z], chain_recv.at[number, z])

                    @pl.when(z < CHAIN - 1)
                    def _():
                        wait(chain_in.at[parity, CHAIN], chain_recv.at[number, CHAIN])

                    def total(at_rows):
                        sink(
                            at_rows,
                            part[slot, core, at_rows]
                            + core_in[parity, held, at_rows]
                            + widen(chain_in[parity, z, at_rows])
                            + widen(chain_in[parity, CHAIN, at_rows]),
                        )

                    by_rows(rows, total)

            slack(index)

        looped(CHAIN + 1, step)

        def sent(index):
            wait(chain_out.at[index], chain_send.at[number, index])

        looped(CHAIN - 1, sent)
        for index in (CHAIN - 2, CHAIN - 1):
            wait(part.at[index % 2, twin], core_send.at[number, index])

    def gain_row(index):
        return gain_full[index : index + 1, :]

    def inverse_of(value):
        return lax.rsqrt(jnp.mean(value * value, axis=-1, keepdims=True) + EPSILON)

    def at_own(at_rows):
        return pl.ds(pl.multiple_of(spot * rows + at_rows.start, CHUNK), CHUNK)

    def project_first(layer):
        def compute(chip):
            here = grouped(chip)
            packed = low(dot(normed[layer, here], first_w[layer]))
            query[layer, here] = packed[:, :lanes]
            pairs[layer, place, here] = packed[:, lanes:]
            for step in range(1, depth):

                @pl.when(place + step < depth)
                def _():
                    ref = pairs.at[layer, place, here]
                    send(ref, ref, pair_send.at[layer, step, chip], pair_recv.at[layer, place, chip], (place + step, spot))

        return compute

    def finish_pairs(layer):
        def sent(chip):
            for step in range(1, depth):

                @pl.when(place + step < depth)
                def _():
                    wait(pairs.at[layer, place, grouped(chip)], pair_send.at[layer, step, chip])

        looped(CHAIN, sent)

    part_rows = group // 3

    def segment_sums(values):
        size = values[0].shape[0]
        high = [low(value) for value in values]
        rest = [low(value - widen(upper)) for value, upper in zip(values, high)]
        sums = dot(jnp.concatenate(high + rest, axis=0), segments_ref[...])
        half = len(values) * size
        return [sums[i * size : (i + 1) * size] + sums[half + i * size : half + (i + 1) * size] for i in range(len(values))]

    def attend_of(query_rows, keys):
        scores = segment_sums([query_rows * key for key in keys])
        scores = [jnp.where(index <= place, score * scale, -1e30) for index, score in enumerate(scores)]
        largest = functools.reduce(jnp.maximum, scores)
        expd = [jnp.exp(score - largest) for score in scores]
        inverse = 1.0 / functools.reduce(jnp.add, expd)
        return [value * inverse for value in expd]

    def attention(layer):
        def compute(chip, target):
            here = grouped(chip)
            for source in range(depth - 1):

                @pl.when(source < place)
                def _():
                    wait(pairs.at[layer, source, here], pair_recv.at[layer, source, chip])

            def rowset(index):
                at_rows = pl.ds(pl.multiple_of(chip * group + index * part_rows, part_rows), part_rows)
                query_rows = widen(query[layer, at_rows])
                keys = [widen(pairs[layer, source, at_rows, :lanes]) for source in range(depth)]
                attend = attend_of(query_rows, keys)
                terms = [widen(low(a)) * widen(pairs[layer, source, at_rows, lanes:]) for source, a in enumerate(attend)]
                mixed[layer, at_rows] = low(functools.reduce(jnp.add, terms))

            looped(group // part_rows, rowset)
            product = dot(mixed[layer, here], out_w[layer])
            target[0] = product[:rows]
            target[1] = product[rows:]

        return compute

    def normalize(value, gain):
        return low(value * inverse_of(value) * gain)

    def middle_sink(layer):
        def sink(at_rows, total):
            value = states[2 * layer, at_rows] + total
            states[2 * layer + 1, at_rows] = value
            inner[layer, at_own(at_rows)] = normalize(value, gain_row(2 * layer + 1))

        return sink

    def project_second(layer):
        def compute(chip):
            here = grouped(chip)
            product = dot(inner[layer, here], second_w[layer])
            part[0, 0] = product[:rows]
            part[0, 1] = product[rows:]
            for half in range(2):

                def gated(at_rows):
                    gate = part[0, half, at_rows, :hidden_cols]
                    up = part[0, half, at_rows, hidden_cols:]
                    to = pl.ds(pl.multiple_of(chip * group + half * rows + at_rows.start, CHUNK), CHUNK)
                    both[layer, to, :hidden_cols] = low(gate)
                    both[layer, to, hidden_cols:] = low(up)
                    hidden[layer, to] = low(gate * jax.nn.sigmoid(gate) * up)

                by_rows(rows, gated)

        return compute

    def project_down(layer):
        def compute(chip, target):
            product = dot(hidden[layer, grouped(chip)], down_w[layer])
            target[0] = product[:rows]
            target[1] = product[rows:]

        return compute

    def state_sink(at_rows, total):
        value = states[1, at_rows] + total
        states[2, at_rows] = value
        normed[1, at_own(at_rows)] = normalize(value, gain_row(2))

    def frames_sink(at_rows, total):
        value = states[3, at_rows] + total
        frames_out[at_rows] = low(jnp.where(active_ref[at_rows] > 0.0, value, 0.0))

    def hidden_back(layer):
        def compute(chip):
            here = grouped(chip)
            product = dot_back(branch[here], down_w[layer])
            part[0, 0, :, :hidden_cols] = product[:rows]
            part[0, 1, :, :hidden_cols] = product[rows:]
            for half in range(2):

                def gated(at_rows):
                    upper = part[0, half, at_rows, :hidden_cols]
                    to = pl.ds(pl.multiple_of(chip * group + half * rows + at_rows.start, CHUNK), CHUNK)
                    gate = widen(both[layer, to, :hidden_cols])
                    up = widen(both[layer, to, hidden_cols:])
                    sigma = jax.nn.sigmoid(gate)
                    scaled = upper * sigma
                    both_grad[to, :hidden_cols] = low(scaled * up * (1.0 + gate * (1.0 - sigma)))
                    both_grad[to, hidden_cols:] = low(scaled * gate)

                by_rows(rows, gated)

        return compute

    def project_second_back(layer):
        def compute(chip, target):
            product = dot_back(both_grad[grouped(chip)], second_w[layer])
            target[0] = product[:rows]
            target[1] = product[rows:]

        return compute

    def norm_back(total, value, gain, index):
        inverse = inverse_of(value)
        product = total * value * inverse
        gain_sum[index] += product[:8] + product[8:]
        scaled = total * gain
        return inverse * scaled - value * (inverse * inverse * inverse) * jnp.mean(scaled * value, axis=-1, keepdims=True)

    def inner_sink(layer):
        def sink(at_rows, total):
            index = 2 * layer + 1
            value = carry[at_rows] + norm_back(total, states[index, at_rows], gain_row(index), index)
            carry[at_rows] = value
            back[at_own(at_rows)] = low(value)

        return sink

    def attention_back(layer):
        def compute(chip):
            here = grouped(chip)
            product = low(dot_back(back[here], out_w[layer]))
            part[0, 0, :, :lanes] = widen(product[:rows])
            part[0, 1, :, :lanes] = widen(product[rows:])
            third = rows // 3

            def rowset(index):
                half, piece = index // 3, index % 3
                at_part = pl.ds(pl.multiple_of(piece * third, third), third)
                at_rows = pl.ds(pl.multiple_of(chip * group + half * rows + piece * third, third), third)
                upper = part[0, half, at_part, :lanes]
                query_rows = widen(query[layer, at_rows])
                keys = [widen(pairs[layer, source, at_rows, :lanes]) for source in range(depth)]
                attend = attend_of(query_rows, keys)
                attend_grad = segment_sums([upper * widen(pairs[layer, source, at_rows, lanes:]) for source in range(depth)])
                inside = functools.reduce(jnp.add, [a * g for a, g in zip(attend, attend_grad)])
                score_grad = [widen(low(a * (g - inside))) for a, g in zip(attend, attend_grad)]
                packed_grad[at_rows, :lanes] = low(functools.reduce(jnp.add, [g * k for g, k in zip(score_grad, keys)]) * scale)
                for source in range(depth):
                    pair_out[source, at_rows, :lanes] = low(score_grad[source] * query_rows * scale)
                    pair_out[source, at_rows, lanes:] = low(widen(low(attend[source])) * upper)

            looped(6, rowset)
            for target in range(depth - 1):

                @pl.when(target < place)
                def _():
                    send(
                        pair_out.at[target, here],
                        pair_in.at[layer, place - 1, here],
                        terms_send.at[layer, target, chip],
                        terms_recv.at[layer, place - 1, chip],
                        (target, spot),
                    )

        return compute

    def finish_terms(layer):
        def sent(chip):
            for target in range(depth - 1):

                @pl.when(target < place)
                def _():
                    wait(pair_out.at[target, grouped(chip)], terms_send.at[layer, target, chip])

        looped(CHAIN, sent)

    def project_first_back(layer):
        def compute(chip, target):
            here = grouped(chip)
            for source in range(1, depth):

                @pl.when(source > place)
                def _():
                    wait(pair_in.at[layer, source - 1, here], terms_recv.at[layer, source - 1, chip])

            def rowset(index):
                at_rows = pl.ds(pl.multiple_of(chip * group + index * 48, 48), 48)
                total = widen(pair_out[place, at_rows])
                for source in range(1, depth):
                    total += widen(pair_in[layer, source - 1, at_rows])
                packed_grad[at_rows, lanes:] = low(total)

            looped(group // 48, rowset)
            product = dot_back(packed_grad[here], first_w[layer])
            target[0] = product[:rows]
            target[1] = product[rows:]

        return compute

    def carry_sink(layer):
        def sink(at_rows, total):
            index = 2 * layer
            value = carry[at_rows] + norm_back(total, states[index, at_rows], gain_row(index), index)
            if layer:
                carry[at_rows] = value
                branch[at_own(at_rows)] = low(value)
            else:
                input_grad[at_rows] = low(value)

        return sink

    def grad_parts(layer, kind):
        if kind == 0:
            for number in range(3):
                yield number * lanes, lanes, grads[layer][number], number
        else:
            for number in range(2):
                yield number * hidden_cols, hidden_cols, grads[layer][4 + number], 3 + number

    def grad_task(layer, kind, step):
        target = other(step)
        stage = (stage_first, stage_second)[kind]
        left = (normed, inner)[kind]
        right = (packed_grad, both_grad)[kind]
        stage[step] = low(dot_rows(left[layer, :, column(target, lanes)], right[...]))

        @pl.when(step > 0)
        def _():
            for start, size, out, number in grad_parts(layer, kind):
                send(
                    stage.at[step, :, start : start + size],
                    out.at[:, column(spot, size)],
                    grad_send.at[layer, number, step],
                    grad_recv.at[layer, number, spot],
                    (place, target),
                )

        @pl.when(step == 0)
        def _():
            for start, size, out, number in grad_parts(layer, kind):
                pltpu.make_async_copy(
                    stage.at[step, :, start : start + size], out.at[:, column(spot, size)], grad_recv.at[layer, number, spot]
                ).start()

    def grad_sent(layer, kind):
        def sent(index):
            for start, size, out, number in grad_parts(layer, kind):
                wait(out.at[:, 0:size], grad_send.at[layer, number, index + 1])

        looped(count - 1, sent)
        for start, size, out, number in grad_parts(layer, kind):
            wait(out.at[:, 0:size], grad_recv.at[layer, number, spot])

    def grad_arrived(layer, kind):
        def arrived(index):
            source = other(index + 1)
            for start, size, out, number in grad_parts(layer, kind):
                wait(out.at[:, column(source, size)], grad_recv.at[layer, number, source])

        looped(count - 1, arrived)

    def down_task(layer, index):
        size = stage_down.shape[0] // 4
        at_rows = pl.ds(pl.multiple_of(index * size, size), size)
        stage_down[at_rows] = low(dot_rows(hidden[layer, :, column(index, size)], branch[...]))

    def down_start(layer):
        return pltpu.make_async_copy(stage_down, grads[layer][6], local_sem.at[4 + 2 * layer])

    def out_task(layer):
        stage_out[...] = low(dot_rows(mixed[layer], back[...]))

    def out_start(layer):
        return pltpu.make_async_copy(stage_out, grads[layer][3], local_sem.at[5 + 2 * layer])

    def send_sums(layer):
        for index in (2 * layer, 2 * layer + 1):

            def step(number):
                target = other(number + 1)
                send(
                    gain_sum.at[index, :, column(target, lanes)],
                    gain_back.at[index, spot],
                    sum_send.at[index, number + 1],
                    sum_recv.at[index, spot],
                    (place, target),
                )

            looped(count - 1, step)
            gain_back[index, spot] = gain_sum[index, :, column(spot, lanes)]

    def finish_sums(layer):
        for index in (2 * layer, 2 * layer + 1):

            def step(number):
                source = other(number + 1)
                wait(gain_back.at[index, source], sum_recv.at[index, source])
                wait(gain_back.at[index, 0], sum_send.at[index, number + 1])

            looped(count - 1, step)
            gains_out[index : index + 1, :] = jnp.sum(gain_back[index], axis=(0, 1), keepdims=True)[0]

    def nothing(index):
        pass

    states[0] = widen(frames_ref[...])
    carry[...] = jnp.where(active_ref[...] > 0.0, widen(cot_ref[...]), 0.0)

    def gains_arrived(index):
        source = other(index + 1)
        wait(gain_in.at[source], gain_recv.at[source])

    looped(count - 1, gains_arrived)
    for source in range(count):
        gain_full[:, source * lanes : (source + 1) * lanes] = gain_in[source]

    def first_rows(at_rows):
        normed[0, at_own(at_rows)] = normalize(states[0, at_rows], gain_row(0))
        branch[at_own(at_rows)] = low(carry[at_rows])

    by_rows(rows, first_rows)

    def second_weights(layer):
        def slack(index):
            @pl.when(index > 0)
            def _():
                send_weights(layer, (3, 4), index)

        return slack

    def more_second_weights(layer):
        def slack(index):
            @pl.when(index > 0)
            def _():
                send_weights(layer, (3, 4), index + 3)

        return slack

    def next_weights(index):
        @pl.when(index > 0)
        def _():
            send_weights(1, (0, 1, 2), 2 * index)

        @pl.when(index < CHAIN)
        def _():
            send_weights(1, (0, 1, 2), 2 * index + 1)

    def after_half(task):
        def slack(index):
            @pl.when(index > 0)
            def _():
                task(index - 1)

        return slack

    gather_start(0, normed.at[0])
    wait_weights(0, (0, 1, 2))
    gather_loop(0, normed.at[0], project_first(0), second_weights(0))
    loads[0].wait()
    scatter_loop(0, attention(0), middle_sink(0), more_second_weights(0))
    gather_finish(0, normed.at[0])
    gather_start(1, inner.at[0])
    wait_weights(0, (3, 4))
    gather_loop(1, inner.at[0], project_second(0), next_weights)
    loads[1].wait()
    scatter_loop(1, project_down(0), state_sink, nothing)
    gather_finish(1, inner.at[0])
    finish_weights(0)
    finish_pairs(0)

    gather_start(2, normed.at[1])
    wait_weights(1, (0, 1, 2))
    gather_loop(2, normed.at[1], project_first(1), second_weights(1))
    loads[2].wait()
    scatter_loop(2, attention(1), middle_sink(1), more_second_weights(1))
    gather_finish(2, normed.at[1])
    gather_start(3, inner.at[1])
    wait_weights(1, (3, 4))
    gather_loop(3, inner.at[1], project_second(1), nothing)
    loads[3].wait()
    gather_start(4, branch)
    scatter_loop(3, project_down(1), frames_sink, nothing)
    gather_finish(3, inner.at[1])
    finish_weights(1)
    finish_pairs(1)

    for layer in (1, 0):
        number = 4 if layer else 6
        if not layer:
            gather_start(number, branch)
        gather_loop(number, branch, hidden_back(layer), nothing)
        gather_finish(number, branch)
        if not layer:
            down_start(1).wait()
            out_start(1).wait()
            grad_sent(1, 0)
            grad_sent(1, 1)

        def second_grads(index, layer=layer):
            @pl.when(index > 0)
            def _():
                grad_task(layer, 1, 2 * index - 2)
                grad_task(layer, 1, 2 * index - 1)

        scatter_loop(number, project_second_back(layer), inner_sink(layer), second_grads)
        gather_start(number + 1, back)

        def down_grads(index, layer=layer):
            down_task(layer, index)

        gather_loop(number + 1, back, attention_back(layer), down_grads)
        down_start(layer).start()

        def out_grads(index, layer=layer):
            @pl.when(index == 1)
            def _():
                out_task(layer)
                out_start(layer).start()

        scatter_loop(number + 1, project_first_back(layer), carry_sink(layer), out_grads)
        gather_finish(number + 1, back)
        finish_terms(layer)
        looped(count, lambda index, layer=layer: grad_task(layer, 0, index))
        send_sums(layer)

    down_start(0).wait()
    out_start(0).wait()
    for layer in (1, 0):
        finish_sums(layer)
        for kind in range(2):
            grad_arrived(layer, kind)
    for kind in range(2):
        grad_sent(0, kind)
    for step in range(1, count):
        wait(gain_in.at[0], gain_send.at[step])


def split_body(*args):
    frames_in, depth_counts, out_grad = args[0][:, 0], args[1], args[-1][:, 0]
    rows, width = frames_in.shape
    depth = lax.axis_size("section")
    count = lax.axis_size("dp")
    lanes = width // count
    layers = [tuple(a[0] for a in args[2:11]), tuple(a[0] for a in args[11:20])]
    ff_cols = layers[0][6].shape[1]
    hidden_cols = ff_cols // count
    down_rows = layers[0][8].shape[0]
    place = lax.axis_index("section")
    active = (place < depth_counts).astype(jnp.float32)[:, None]
    gains = jnp.stack([layers[0][0], layers[0][5], layers[1][0], layers[1][5]]).astype(jnp.float32)
    gains = jnp.concatenate([gains, jnp.zeros((4, lanes), jnp.float32)])
    index = jnp.arange(lanes) // HEAD_DIM
    segments = (index[:, None] == index[None, :]).astype(jnp.bfloat16)
    weights = [layer[i] for layer in layers for i in (1, 2, 3, 4, 6, 7, 8)]
    total = rows * count
    low_type, full_type = jnp.bfloat16, jnp.float32
    grad_shapes = [(lanes, width)] * 4 + [(lanes, ff_cols)] * 2 + [(down_rows, width)]
    out_shape = (
        [jax.ShapeDtypeStruct((rows, width), low_type)] * 2
        + [jax.ShapeDtypeStruct((4, lanes), full_type)]
        + [jax.ShapeDtypeStruct(shape, low_type) for shape in grad_shapes * 2]
    )
    vmem, anywhere = pl.BlockSpec(memory_space=pltpu.VMEM), pl.BlockSpec(memory_space=pl.ANY)
    held = pltpu.VMEM
    sems = pltpu.SemaphoreType.DMA
    scratch = [
        held((2, width, 3 * lanes), low_type),
        held((2, width, 2 * hidden_cols), low_type),
        held((2, lanes, width), low_type),
        held((2, down_rows, width), low_type),
        held((2, total, width), low_type),
        held((2, total, width), low_type),
        held((total, width), low_type),
        held((total, width), low_type),
        held((2, total, lanes), low_type),
        held((2, depth, total, 2 * lanes), low_type),
        held((2, total, lanes), low_type),
        held((2, total, 2 * hidden_cols), low_type),
        held((2, total, hidden_cols), low_type),
        held((total, 2 * hidden_cols), low_type),
        held((total, 3 * lanes), low_type),
        held((2, depth - 1, total, 2 * lanes), low_type),
        held((depth, total, 2 * lanes), low_type),
        held((2, 2, rows, width), full_type),
        held((2, CHAIN, rows, width), full_type),
        held((2, CHAIN + 1, rows, width), low_type),
        held((CHAIN - 1, rows, width), low_type),
        held((4, rows, width), full_type),
        held((rows, width), full_type),
        held((count, 8, lanes), full_type),
        held((8, width), full_type),
        held((4, 8, width), full_type),
        held((4, count, 8, lanes), full_type),
        held((count, lanes, 3 * lanes), low_type),
        held((count, lanes, 2 * hidden_cols), low_type),
        held((down_rows, width), low_type),
        held((lanes, width), low_type),
        sems((8, 15)),
        sems((8, count)),
        sems((8, CHAIN)),
        sems((8, CHAIN)),
        sems((8, CHAIN)),
        sems((8, CHAIN + 1)),
        sems((2, depth, CHAIN)),
        sems((2, depth, CHAIN)),
        sems((2, depth, CHAIN)),
        sems((2, depth, CHAIN)),
        sems((2, 5, count)),
        sems((2, 5, count)),
        sems((2, 5, count)),
        sems((2, 5, count)),
        sems((count,)),
        sems((count,)),
        sems((4, count)),
        sems((4, count)),
        sems((8,)),
    ]
    outs = pl.pallas_call(
        split_kernel,
        out_shape=out_shape,
        in_specs=[vmem] * 5 + [anywhere] * 14,
        out_specs=[vmem] * 3 + [anywhere] * 14,
        scratch_shapes=scratch,
        compiler_params=pltpu.CompilerParams(
            collective_id=0, has_side_effects=True, vmem_limit_bytes=VMEM_BYTES
        ),
        cost_estimate=pl.CostEstimate(flops=2 * 6 * total * width * (4 * lanes + 3 * hidden_cols), bytes_accessed=1 << 26, transcendentals=1 << 22),
    )(frames_in, out_grad, active, gains, segments, *weights)
    gain_grads = outs[2]
    result = [outs[0][:, None], outs[1][:, None]]
    for layer in range(2):
        wide = [out.astype(jnp.float32)[None] for out in outs[3 + 7 * layer : 10 + 7 * layer]]
        result += [gain_grads[2 * layer][None], *wide[:4], gain_grads[2 * layer + 1][None], *wide[4:]]
    return tuple(result)


def solution(mesh):
    in_specs = (
        P("dp", "section", None),
        P("dp"),
        P("section", "dp"),
        P("section", "dp", None),
        P("section", "dp", None),
        P("section", "dp", None),
        P("section", "dp", None),
        P("section", "dp"),
        P("section", "dp", None),
        P("section", "dp", None),
        P("section", "dp", None),
        P("section", "dp"),
        P("section", "dp", None),
        P("section", "dp", None),
        P("section", "dp", None),
        P("section", "dp", None),
        P("section", "dp"),
        P("section", "dp", None),
        P("section", "dp", None),
        P("section", "dp", None),
        P("dp", "section", None),
    )
    out_specs = (
        P("dp", "section", None),
        P("dp", "section", None),
        P("section", "dp"),
        P("section", "dp", None),
        P("section", "dp", None),
        P("section", "dp", None),
        P("section", "dp", None),
        P("section", "dp"),
        P("section", "dp", None),
        P("section", "dp", None),
        P("section", "dp", None),
        P("section", "dp"),
        P("section", "dp", None),
        P("section", "dp", None),
        P("section", "dp", None),
        P("section", "dp", None),
        P("section", "dp"),
        P("section", "dp", None),
        P("section", "dp", None),
        P("section", "dp", None),
    )
    parts, sections = mesh.shape["dp"], mesh.shape["section"]
    chosen = split_body if parts == 2 * CHAIN and sections == 4 else body
    return jax.shard_map(chosen, mesh=mesh, in_specs=in_specs, out_specs=out_specs, check_vma=False)
```

```python
import functools

import jax
import jax.numpy as jnp
from jax import lax
from jax.experimental import pallas as pl
from jax.experimental.pallas import tpu as pltpu
from jax.sharding import PartitionSpec as P

HEAD_DIM = 64
MICRO = 2


EPSILON = 1e-05
VMEM_BYTES = 63 * 2**20


def rms_apply(state, gain):
    inverse = lax.rsqrt(jnp.mean(state * state, axis=-1, keepdims=True) + EPSILON)
    return (state * inverse * gain.astype(jnp.float32)[None], inverse)


def rms_back(upper, state, inverse, gain):
    gain_grad = jnp.sum(upper * state * inverse, axis=0)
    scaled = upper * gain.astype(jnp.float32)[None]
    lower = inverse * scaled - state * (inverse * inverse * inverse) * jnp.mean(
        scaled * state, axis=-1, keepdims=True
    )
    return (lower, gain_grad)


def project(left, weight):
    return jnp.einsum("fpd,pde->fpe", left, weight, preferred_element_type=jnp.float32)


def project_back(grad, weight):
    return jnp.einsum("fpe,pde->fpd", grad, weight, preferred_element_type=jnp.float32)


def outer(left, grad):
    return jnp.einsum("fpd,fpe->pde", left, grad, preferred_element_type=jnp.float32)


def fetch(params):
    attn_gain, query_w, key_w, value_w, out_w, ffn_gain, gate_w, up_w, down_w = params
    return (
        lax.all_gather(attn_gain, "dp", axis=1, tiled=True),
        lax.all_gather(query_w, "dp", axis=1, tiled=True),
        lax.all_gather(key_w, "dp", axis=1, tiled=True),
        lax.all_gather(value_w, "dp", axis=1, tiled=True),
        lax.all_gather(out_w, "dp", axis=1, tiled=True),
        lax.all_gather(ffn_gain, "dp", axis=1, tiled=True),
        lax.all_gather(gate_w, "dp", axis=1, tiled=True),
        lax.all_gather(up_w, "dp", axis=1, tiled=True),
        lax.all_gather(down_w, "dp", axis=1, tiled=True),
    )


def fetch_again(params):
    attn_gain, query_w, key_w, value_w, out_w, ffn_gain, gate_w, up_w, down_w = params
    return (
        lax.all_gather(attn_gain, "dp", axis=1, tiled=True),
        lax.all_gather(query_w, "dp", axis=1, tiled=True),
        lax.all_gather(key_w, "dp", axis=1, tiled=True),
        lax.all_gather(value_w, "dp", axis=1, tiled=True),
        lax.all_gather(out_w, "dp", axis=1, tiled=True),
        lax.all_gather(ffn_gain, "dp", axis=1, tiled=True),
        lax.all_gather(gate_w, "dp", axis=1, tiled=True),
        lax.all_gather(up_w, "dp", axis=1, tiled=True),
        lax.all_gather(down_w, "dp", axis=1, tiled=True),
    )


def layer_forward(state, params, positions):
    attn_gain, query_w, key_w, value_w, out_w, ffn_gain, gate_w, up_w, down_w = params
    frames, local, width = state.shape
    heads = width // HEAD_DIM
    normed_full, inverse_one = rms_apply(state, attn_gain)
    normed = normed_full.astype(jnp.bfloat16)
    query = project(normed, query_w).astype(jnp.bfloat16)
    keys = project(normed, key_w).astype(jnp.bfloat16)
    values = project(normed, value_w).astype(jnp.bfloat16)
    all_keys, all_values = (
        lax.all_gather(keys, "section", axis=1, tiled=True),
        lax.all_gather(values, "section", axis=1, tiled=True),
    )
    depth = all_keys.shape[1]
    query_heads = query.reshape(frames, local, heads, HEAD_DIM)
    key_heads = all_keys.reshape(frames, depth, heads, HEAD_DIM)
    value_heads = all_values.reshape(frames, depth, heads, HEAD_DIM)
    scores = jnp.einsum(
        "fphc,fshc->fhps", query_heads, key_heads, preferred_element_type=jnp.float32
    ) * HEAD_DIM ** (-0.5)
    allowed = positions[:, None] >= jnp.arange(depth)[None, :]
    scores = jnp.where(allowed[None, None], scores, -1e30)
    largest = jnp.max(scores, axis=-1, keepdims=True)
    expd = jnp.exp(scores - largest)
    attend = expd / jnp.sum(expd, axis=-1, keepdims=True)
    attend_low = attend.astype(jnp.bfloat16)
    mixed = jnp.einsum(
        "fhps,fshc->fphc", attend_low, value_heads, preferred_element_type=jnp.float32
    )
    mixed = mixed.reshape(frames, local, width).astype(jnp.bfloat16)
    middle = state + project(mixed, out_w)
    inner_full, inverse_two = rms_apply(middle, ffn_gain)
    inner = inner_full.astype(jnp.bfloat16)
    gate = project(inner, gate_w)
    up = project(inner, up_w)
    hidden = (jax.nn.silu(gate) * up).astype(jnp.bfloat16)
    result = middle + project(hidden, down_w)
    kept = (
        state,
        inverse_one,
        normed,
        query_heads,
        key_heads,
        value_heads,
        attend,
        attend_low,
        mixed,
        middle,
        inverse_two,
        inner,
        gate,
        up,
        hidden,
    )
    return (result, kept)


def layer_backward(carried, params, kept):
    attn_gain, query_w, key_w, value_w, out_w, ffn_gain, gate_w, up_w, down_w = params
    (
        state,
        inverse_one,
        normed,
        query_heads,
        key_heads,
        value_heads,
        attend,
        attend_low,
        mixed,
        middle,
        inverse_two,
        inner,
        gate,
        up,
        hidden,
    ) = kept
    frames, local, width = state.shape
    depth = key_heads.shape[1]
    branch_grad = carried.astype(jnp.bfloat16)
    hidden_grad = project_back(branch_grad, down_w)
    sigma = jax.nn.sigmoid(gate)
    gate_grad = (hidden_grad * up * sigma * (1.0 + gate * (1.0 - sigma))).astype(jnp.bfloat16)
    up_grad = (hidden_grad * gate * sigma).astype(jnp.bfloat16)
    inner_grad = project_back(gate_grad, gate_w) + project_back(up_grad, up_w)
    lower_two, grad_ffn_gain = rms_back(inner_grad, middle, inverse_two, ffn_gain)
    middle_grad = carried + lower_two
    mixed_back = middle_grad.astype(jnp.bfloat16)
    mixed_grad = project_back(mixed_back, out_w).astype(jnp.bfloat16)
    mixed_heads = mixed_grad.reshape(frames, local, -1, HEAD_DIM)
    attend_grad = jnp.einsum(
        "fphc,fshc->fhps", mixed_heads, value_heads, preferred_element_type=jnp.float32
    )
    value_terms = jnp.einsum(
        "fhps,fphc->fshc", attend_low, mixed_heads, preferred_element_type=jnp.float32
    ).reshape(frames, depth, width)
    score_grad = attend * (attend_grad - jnp.sum(attend * attend_grad, axis=-1, keepdims=True))
    score_grad = score_grad.astype(jnp.bfloat16)
    scale = HEAD_DIM ** (-0.5)
    query_grad = (
        jnp.einsum("fhps,fshc->fphc", score_grad, key_heads, preferred_element_type=jnp.float32)
        * scale
    )
    query_grad = query_grad.reshape(frames, local, width).astype(jnp.bfloat16)
    key_terms = (
        jnp.einsum("fhps,fphc->fshc", score_grad, query_heads, preferred_element_type=jnp.float32)
        * scale
    )
    key_terms = key_terms.reshape(frames, depth, width)
    keys_sum, values_sum = (
        lax.psum_scatter(key_terms, "section", scatter_dimension=1, tiled=True),
        lax.psum_scatter(value_terms, "section", scatter_dimension=1, tiled=True),
    )
    keys_grad = keys_sum.astype(jnp.bfloat16)
    values_grad = values_sum.astype(jnp.bfloat16)
    normed_grad = (
        project_back(query_grad, query_w)
        + project_back(keys_grad, key_w)
        + project_back(values_grad, value_w)
    )
    lower_one, grad_attn_gain = rms_back(normed_grad, state, inverse_one, attn_gain)
    deferred = (
        grad_attn_gain,
        grad_ffn_gain,
        hidden,
        branch_grad,
        inner,
        gate_grad,
        up_grad,
        mixed,
        mixed_back,
        normed,
        query_grad,
        keys_grad,
        values_grad,
    )
    return (middle_grad + lower_one, deferred)


def join_deferred(pieces):
    gains = tuple(
        (sum((piece[index] for piece in pieces[1:])) + pieces[0][index] for index in (0, 1))
    )
    rest = tuple(
        (jnp.concatenate([piece[index] for piece in pieces], axis=0) for index in range(2, 13))
    )
    return gains + rest


def weight_terms(deferred):
    (
        grad_attn_gain,
        grad_ffn_gain,
        hidden,
        branch_grad,
        inner,
        gate_grad,
        up_grad,
        mixed,
        mixed_back,
        normed,
        query_grad,
        keys_grad,
        values_grad,
    ) = deferred
    return (
        grad_attn_gain,
        outer(normed, query_grad),
        outer(normed, keys_grad),
        outer(normed, values_grad),
        outer(mixed, mixed_back),
        grad_ffn_gain,
        outer(inner, gate_grad),
        outer(inner, up_grad),
        outer(hidden, branch_grad),
    )


def reduce_grads(full):
    (
        grad_attn_gain,
        grad_query,
        grad_key,
        grad_value,
        grad_out,
        grad_ffn_gain,
        grad_gate,
        grad_up,
        grad_down,
    ) = full
    return (
        lax.psum_scatter(grad_attn_gain, "dp", scatter_dimension=1, tiled=True),
        lax.psum_scatter(grad_query, "dp", scatter_dimension=1, tiled=True),
        lax.psum_scatter(grad_key, "dp", scatter_dimension=1, tiled=True),
        lax.psum_scatter(grad_value, "dp", scatter_dimension=1, tiled=True),
        lax.psum_scatter(grad_out, "dp", scatter_dimension=1, tiled=True),
        lax.psum_scatter(grad_ffn_gain, "dp", scatter_dimension=1, tiled=True),
        lax.psum_scatter(grad_gate, "dp", scatter_dimension=1, tiled=True),
        lax.psum_scatter(grad_up, "dp", scatter_dimension=1, tiled=True),
        lax.psum_scatter(grad_down, "dp", scatter_dimension=1, tiled=True),
    )


def body(
    frames_in,
    depth_counts,
    attn_gain_1,
    query_weight_1,
    key_weight_1,
    value_weight_1,
    out_weight_1,
    ffn_gain_1,
    gate_weight_1,
    up_weight_1,
    down_weight_1,
    attn_gain_2,
    query_weight_2,
    key_weight_2,
    value_weight_2,
    out_weight_2,
    ffn_gain_2,
    gate_weight_2,
    up_weight_2,
    down_weight_2,
    out_grad,
):
    layers = (
        (
            attn_gain_1,
            query_weight_1,
            key_weight_1,
            value_weight_1,
            out_weight_1,
            ffn_gain_1,
            gate_weight_1,
            up_weight_1,
            down_weight_1,
        ),
        (
            attn_gain_2,
            query_weight_2,
            key_weight_2,
            value_weight_2,
            out_weight_2,
            ffn_gain_2,
            gate_weight_2,
            up_weight_2,
            down_weight_2,
        ),
    )
    frames_dev = frames_in.shape[0]
    local = frames_in.shape[1]
    portion = frames_dev // MICRO
    positions = lax.axis_index("section") * local + jnp.arange(local)
    active = positions[None, :] < depth_counts[:, None]
    gathered = [fetch(layers[0]), fetch(layers[1])]
    keeps = [[], []]
    results = []
    for micro in range(MICRO):
        state = frames_in[micro * portion : (micro + 1) * portion].astype(jnp.float32)
        for number in (0, 1):
            state, kept = layer_forward(state, gathered[number], positions)
            keeps[number].append(kept)
        results.append(state)
    state = jnp.concatenate(results, axis=0)
    frames_out = jnp.where(active[:, :, None], state, 0.0).astype(jnp.bfloat16)
    masked = jnp.where(active[:, :, None], out_grad.astype(jnp.float32), 0.0)
    carries = [masked[micro * portion : (micro + 1) * portion] for micro in range(MICRO)]
    reduced = [None, None]
    for number in (1, 0):
        params = fetch_again(layers[number])
        pieces = []
        for micro in range(MICRO):
            carries[micro], deferred = layer_backward(carries[micro], params, keeps[number][micro])
            pieces.append(deferred)
        reduced[number] = reduce_grads(weight_terms(join_deferred(pieces)))
    first, second = reduced
    input_grad = jnp.concatenate(carries, axis=0).astype(jnp.bfloat16)
    return (
        frames_out,
        input_grad,
        first[0],
        first[1],
        first[2],
        first[3],
        first[4],
        first[5],
        first[6],
        first[7],
        first[8],
        second[0],
        second[1],
        second[2],
        second[3],
        second[4],
        second[5],
        second[6],
        second[7],
        second[8],
    )


HEAD_LANES = 128
CHAIN = 4
CHUNK = 16
LAST_OUT = 3
MESH = pl.DeviceIdType.MESH


def widen(value):
    return value.astype(jnp.float32)


def low(value):
    return value.astype(jnp.bfloat16)


def dot(left, right):
    return jnp.dot(left, right, preferred_element_type=jnp.float32)


def dot_rows(left, right):
    return lax.dot_general(left, right, (((0,), (0,)), ((), ())), preferred_element_type=jnp.float32)


def dot_back(left, right):
    return lax.dot_general(left, right, (((1,), (1,)), ((), ())), preferred_element_type=jnp.float32)


def looped(count, step):
    lax.fori_loop(0, count, lambda index, carry: (step(index), carry)[1], 0)


def by_rows(rows, step, size=CHUNK):
    looped(rows // size, lambda index: step(pl.ds(pl.multiple_of(index * size, size), size)))


def split_kernel(*refs):
    (frames_ref, cot_ref, active_ref, gains_ref, segments_ref), refs = refs[:5], refs[5:]
    weights, refs = (refs[:7], refs[7:14]), refs[14:]
    (frames_out, input_grad, gains_out), refs = refs[:3], refs[3:]
    grads, refs = (refs[:7], refs[7:14]), refs[14:]
    (
        first_w, second_w, out_w, down_w, normed, inner, branch, back, query, pairs, mixed, both, hidden,
        both_grad, packed_grad, pair_in, pair_out, part, core_in, chain_in, chain_out, states, carry,
        gain_in, gain_full, gain_sum, gain_back, stage_first, stage_second, stage_down, stage_out, room,
    ), refs = refs[:32], refs[32:]
    (
        gather_send, gather_recv, core_send, core_recv, chain_send, chain_recv, pair_send, pair_recv,
        terms_send, terms_recv, weight_send, weight_recv, grad_send, grad_recv, gain_send, gain_recv,
        sum_send, sum_recv, local_sem,
    ) = refs

    rows, width = frames_ref.shape
    count = 2 * CHAIN
    lanes = width // count
    hidden_cols = second_w.shape[2] // 2
    depth = pairs.shape[1]
    scale = HEAD_DIM ** (-0.5)
    place = lax.axis_index("section")
    spot = lax.axis_index("dp")
    z = spot // 2
    core = spot % 2
    twin = 1 - core

    def at(chip, which):
        return (place, chip * 2 + which)

    def send(source, target, send_sem, recv_sem, device):
        pltpu.make_async_remote_copy(
            src_ref=source, dst_ref=target, send_sem=send_sem, recv_sem=recv_sem, device_id=device, device_id_type=MESH
        ).start()

    def wait(ref, sem):
        pltpu.make_async_copy(ref, ref, sem).wait()

    first_size = -(-rows // (2 * CHUNK)) * CHUNK
    sizes = (first_size, rows - first_size)
    spans = (pl.ds(0, first_size), pl.ds(first_size, rows - first_size))
    starts = (0, count * first_size)

    def half_rows(half, index):
        return pl.ds(pl.multiple_of(starts[half] + index * sizes[half], CHUNK), sizes[half])

    def grouped(half, chip):
        return pl.ds(pl.multiple_of(starts[half] + chip * 2 * sizes[half], 2 * CHUNK), 2 * sizes[half])

    def by_half(half, step):
        by_rows(sizes[half], lambda at_rows: step(pl.ds(pl.multiple_of(at_rows.start + spans[half].start, CHUNK), CHUNK)))

    def column(index, size):
        return pl.ds(pl.multiple_of(index * size, size), size)

    def other(step):
        hop, cross = step // 2, step % 2
        chip = jnp.where(hop == 1, z + 1 - 2 * (z % 2), jnp.where(hop == 2, (z + 2) % 4, jnp.where(hop == 3, 3 - z, z)))
        return chip * 2 + jnp.where(cross == 1, twin, core)

    barrier = pltpu.get_barrier_semaphore()
    for step in range(1, count):
        pl.semaphore_signal(barrier, inc=1, device_id=(place, (spot + step) % count), device_id_type=MESH)
    for step in range(1, depth):
        pl.semaphore_signal(barrier, inc=1, device_id=((place + step) % depth, spot), device_id_type=MESH)

    loads = []
    for layer in range(2):
        loads.append(pltpu.make_async_copy(weights[layer][3], out_w.at[layer], local_sem.at[2 * layer]))
        loads.append(pltpu.make_async_copy(weights[layer][6], down_w.at[layer], local_sem.at[2 * layer + 1]))
    for load in loads:
        load.start()
    mine = pl.ds(pl.multiple_of(spot * lanes, lanes), lanes)

    def weight_parts(layer):
        for number in range(3):
            yield weights[layer][number], first_w, number * lanes, lanes, number
        for number in range(2):
            yield weights[layer][4 + number], second_w, number * hidden_cols, hidden_cols, 3 + number

    def own_weights(layer):
        for source, held, start, size, number in weight_parts(layer):
            yield pltpu.make_async_copy(
                source.at[:, column(spot, size)], held.at[layer, mine, start : start + size], weight_recv.at[layer, number, spot]
            )

    for layer in range(2):
        for copy in own_weights(layer):
            copy.start()

    def send_weights(layer, numbers, step):
        target = other(step)
        for source, held, start, size, number in weight_parts(layer):
            if number in numbers:
                send(
                    source.at[:, column(target, size)],
                    held.at[layer, mine, start : start + size],
                    weight_send.at[layer, number, step],
                    weight_recv.at[layer, number, spot],
                    (place, target),
                )

    def far_first(index):
        return jnp.where(index < 4, index + 4, jnp.where(index < 6, index - 2, 7 - index))

    def second_job(job, emit):
        step = far_first(job // 4)
        rows_at = pl.ds(pl.multiple_of((job // 2) % 2 * (lanes // 2), lanes // 2), lanes // 2)
        for which in range(2):

            @pl.when((job % 2 == which) & (job >= 0) & (job < 4 * (count - 1)))
            def _():
                emit(step, which, rows_at)

    def send_second(layer, job):
        def emit(step, which, rows_at):
            target = other(step)
            start = which * hidden_cols
            to = pl.ds(pl.multiple_of(spot * lanes + rows_at.start, lanes // 2), lanes // 2)
            send(
                weights[layer][4 + which].at[rows_at, column(target, hidden_cols)],
                second_w.at[layer, to, start : start + hidden_cols],
                weight_send.at[layer, 3 + which, step],
                weight_recv.at[layer, 3 + which, spot],
                (place, target),
            )

        second_job(job, emit)

    def send_first(layer, job):
        @pl.when((job >= 0) & (job < count - 1))
        def _():
            send_weights(layer, (0, 1, 2), far_first(job))

    def wait_weights(layer, numbers):
        def arrived(index):
            for _, held, start, size, number in weight_parts(layer):
                if number in numbers:
                    wait(held.at[layer, column(index, lanes), start : start + size], weight_recv.at[layer, number, index])

        looped(count, arrived)

    def finish_weights(layer):
        def sent(index):
            for _, held, start, size, number in weight_parts(layer):
                wait(held.at[layer, pl.ds(0, lanes), start : start + size], weight_send.at[layer, number, index + 1])

        looped(count - 1, sent)

    for layer in range(2):
        for source in range(1, depth):

            @pl.when(place < source)
            def _():
                pairs[layer, source] = jnp.zeros(pairs.shape[2:], pairs.dtype)

            @pl.when(place >= source)
            def _():
                pair_in[layer, source - 1] = jnp.zeros(pair_in.shape[2:], pair_in.dtype)

    for parity in range(2):

        @pl.when(z == 0)
        def _():
            for index in range(CHAIN):
                chain_in[parity, index] = jnp.zeros(chain_in.shape[2:], chain_in.dtype)

        @pl.when(z == CHAIN - 1)
        def _():
            for index in (0, 1, 2, 4):
                chain_in[parity, index] = jnp.zeros(chain_in.shape[2:], chain_in.dtype)

    gain_in[spot] = gains_ref[...]
    gain_sum[...] = jnp.zeros_like(gain_sum)

    pl.semaphore_wait(barrier, count - 1 + depth - 1)

    for step in range(1, count):
        send(gains_ref, gain_in.at[spot], gain_send.at[step], gain_recv.at[spot], (place, other(step)))
    looped(count - 1, lambda index: send_first(0, index))

    def own_rows(half):
        return half_rows(half, spot)

    def gather_start(number, half, held):
        own = held.at[own_rows(half)]
        send(own, own, gather_send.at[number, half, 0], gather_recv.at[number, half, spot], at(z, twin))

        @pl.when(z < CHAIN - 1)
        def _():
            send(own, own, gather_send.at[number, half, 1], gather_recv.at[number, half, spot], at(z + 1, core))

        @pl.when(z > 0)
        def _():
            send(own, own, gather_send.at[number, half, 2], gather_recv.at[number, half, spot], at(z - 1, core))

    def gather_arrive(number, half, held, index):
        below, above = z - index, z + index

        @pl.when((index > 0) & (index < CHAIN) & (below >= 0))
        def _():
            source = below * 2 + core
            here = held.at[half_rows(half, source)]
            wait(here, gather_recv.at[number, half, source])

            @pl.when(z < CHAIN - 1)
            def _():
                send(here, here, gather_send.at[number, half, 2 + index], gather_recv.at[number, half, source], at(z + 1, core))

            send(here, here, gather_send.at[number, half, 8 + index], gather_recv.at[number, half, source], at(z, twin))

        @pl.when((index > 0) & (above < CHAIN))
        def _():
            source = above * 2 + core
            here = held.at[half_rows(half, source)]
            wait(here, gather_recv.at[number, half, source])

            @pl.when(z > 0)
            def _():
                send(here, here, gather_send.at[number, half, 5 + index], gather_recv.at[number, half, source], at(z - 1, core))

            send(here, here, gather_send.at[number, half, 11 + index], gather_recv.at[number, half, source], at(z, twin))

    def gather_compute(number, half, held, compute, index):
        def side(which):
            chip = z - index + 2 * index * which

            @pl.when((chip >= 0) & (chip < CHAIN) & (index + 1 > which) & (index < CHAIN))
            def _():
                source = chip * 2 + twin
                wait(held.at[half_rows(half, source)], gather_recv.at[number, half, source])
                if compute is not None:
                    compute(half, chip)

        looped(2, side)

    def gather_finish(number, half, held):
        one = held.at[half_rows(half, 0)]
        wait(one, gather_send.at[number, half, 0])

        @pl.when(z < CHAIN - 1)
        def _():
            wait(one, gather_send.at[number, half, 1])

        @pl.when(z > 0)
        def _():
            wait(one, gather_send.at[number, half, 2])

        def step(index):
            @pl.when(z - index >= 0)
            def _():
                @pl.when(z < CHAIN - 1)
                def _():
                    wait(one, gather_send.at[number, half, 2 + index])

                wait(one, gather_send.at[number, half, 8 + index])

            @pl.when(z + index < CHAIN)
            def _():
                @pl.when(z > 0)
                def _():
                    wait(one, gather_send.at[number, half, 5 + index])

                wait(one, gather_send.at[number, half, 11 + index])

        looped(CHAIN - 1, lambda index: step(index + 1))

    def order(index):
        first = 3 * (1 - z // 2)
        second = 2 - z // 2
        third = 1 - z % 2 + 2 * (z // 2)
        return jnp.where(index == 0, first, jnp.where(index == 1, second, jnp.where(index == 2, third, z)))

    def scatter_compute(number, half, compute, index):
        bank = 1 if number == LAST_OUT else 0
        span = spans[half]

        @pl.when(index < CHAIN)
        def _():
            slot = index % 2

            @pl.when(index > 1)
            def _():
                wait(part.at[slot, twin, span], core_send.at[number, half, index - 2])

            product = compute(half, order(index))
            part[slot, 0, span] = product[: sizes[half]]
            part[slot, 1, span] = product[sizes[half] :]
            send(
                part.at[slot, twin, span],
                core_in.at[bank, index, span],
                core_send.at[number, half, index],
                core_recv.at[number, half, index],
                at(z, twin),
            )

    def scatter_send(number, half, index, allowed):
        bank = 1 if number == LAST_OUT else 0
        span = spans[half]

        @pl.when((index > 0) & (index < CHAIN) & allowed)
        def _():
            held = index - 1
            slot = held % 2
            target = order(held)
            wait(core_in.at[bank, held, span], core_recv.at[number, half, held])

            @pl.when(((target > z) & (z > 0)) | ((target < z) & (z < CHAIN - 1)))
            def _():
                wait(chain_in.at[bank, target, span], chain_recv.at[number, half, target])

            def add(at_rows):
                total = part[slot, core, at_rows] + core_in[bank, held, at_rows]
                chain_out[bank, held, at_rows] = low(total + widen(chain_in[bank, target, at_rows]))

            by_half(half, add)

            @pl.when(target > z)
            def _():
                send(
                    chain_out.at[bank, held, span],
                    chain_in.at[bank, target, span],
                    chain_send.at[number, half, held],
                    chain_recv.at[number, half, target],
                    at(z + 1, core),
                )

            @pl.when(target < z)
            def _():
                landing = jnp.where(target == z - 1, CHAIN, target)
                send(
                    chain_out.at[bank, held, span],
                    chain_in.at[bank, landing, span],
                    chain_send.at[number, half, held],
                    chain_recv.at[number, half, landing],
                    at(z - 1, core),
                )

    def scatter_end(number, half, sink, index):
        bank = 1 if number == LAST_OUT else 0
        span = spans[half]
        held = CHAIN - 1
        slot = held % 2

        @pl.when(index == CHAIN)
        def _():
            wait(core_in.at[bank, held, span], core_recv.at[number, half, held])

            @pl.when(z > 0)
            def _():
                wait(chain_in.at[bank, z, span], chain_recv.at[number, half, z])

            @pl.when(z < CHAIN - 1)
            def _():
                wait(chain_in.at[bank, CHAIN, span], chain_recv.at[number, half, CHAIN])

            def total(at_rows):
                sink(
                    half,
                    at_rows,
                    part[slot, core, at_rows]
                    + core_in[bank, held, at_rows]
                    + widen(chain_in[bank, z, at_rows])
                    + widen(chain_in[bank, CHAIN, at_rows]),
                )

            by_half(half, total)

    def scatter_finish(number, half):
        span = spans[half]

        def sent(index):
            wait(chain_out.at[0, index, span], chain_send.at[number, half, index])

        looped(CHAIN - 1, sent)

    def core_finish(number, half):
        for index in (CHAIN - 2, CHAIN - 1):
            wait(part.at[index % 2, twin, spans[half]], core_send.at[number, half, index])

    pending = []

    def phase(scatters=(), gathers=(), slack=None):
        for number, half, held, _ in gathers:
            gather_start(number, half, held)

        outer = (z == 0) | (z == CHAIN - 1)
        inside = (z > 0) & (z < CHAIN - 1)

        def step(index):
            for number, half, compute, sink in scatters:
                scatter_compute(number, half, compute, index)
                scatter_send(number, half, index, outer)
            if slack is not None:
                slack(index, 0)
            for number, half, held, _ in gathers:
                gather_arrive(number, half, held, index)
            for number, half, compute, sink in scatters:
                scatter_send(number, half, index, inside)
            if slack is not None:
                slack(index, 1)
            for number, half, held, compute in gathers:
                gather_compute(number, half, held, compute, index)
            for number, half, compute, sink in scatters:
                scatter_end(number, half, sink, index)
            if slack is not None:
                slack(index, 2)

        looped(CHAIN + 1, step)
        for number, half, _, _ in scatters:
            core_finish(number, half)
        for done in pending:
            done()
        pending.clear()
        for number, half, held, _ in gathers:
            pending.append(functools.partial(gather_finish, number, half, held))
        for number, half, _, _ in scatters:
            pending.append(functools.partial(scatter_finish, number, half))

    def state_at(index, at_rows):
        return states[index - 1, at_rows] if index else widen(frames_ref[at_rows])

    def gain_row(index):
        return gain_full[index : index + 1, :]

    def inverse_of(value):
        return lax.rsqrt(jnp.mean(value * value, axis=-1, keepdims=True) + EPSILON)

    def at_own(half, at_rows):
        start = starts[half] + spot * sizes[half] + at_rows.start - spans[half].start
        return pl.ds(pl.multiple_of(start, CHUNK), CHUNK)

    def pieces(half, chip, step):
        looped(2, lambda which: step(which, half_rows(half, chip * 2 + which)))

    def project_first(layer):
        def compute(half, chip):
            here = grouped(half, chip)
            packed = low(dot(normed[layer, here], first_w[layer]))
            query[layer, here] = packed[:, :lanes]
            pairs[layer, place, here] = packed[:, lanes:]
            for step in range(1, depth):

                @pl.when(place + step < depth)
                def _():
                    ref = pairs.at[layer, place, here]
                    send(ref, ref, pair_send.at[layer, half, step, chip], pair_recv.at[layer, half, place, chip], (place + step, spot))

        return compute

    def finish_pairs(layer):
        for half in range(2):

            def sent(chip):
                for step in range(1, depth):

                    @pl.when(place + step < depth)
                    def _():
                        wait(pairs.at[layer, place, grouped(half, chip)], pair_send.at[layer, half, step, chip])

            looped(CHAIN, sent)

    def segment_sums(values):
        size = values[0].shape[0]
        high = [low(value) for value in values]
        rest = [low(value - widen(upper)) for value, upper in zip(values, high)]
        sums = dot(jnp.concatenate(high + rest, axis=0), segments_ref[...])
        half = len(values) * size
        return [sums[i * size : (i + 1) * size] + sums[half + i * size : half + (i + 1) * size] for i in range(len(values))]

    def attend_of(query_rows, keys):
        scores = segment_sums([query_rows * key for key in keys])
        scores = [jnp.where(index <= place, score * scale, -1e30) for index, score in enumerate(scores)]
        largest = functools.reduce(jnp.maximum, scores)
        expd = [jnp.exp(score - largest) for score in scores]
        inverse = 1.0 / functools.reduce(jnp.add, expd)
        return [value * inverse for value in expd]

    def attention(layer):
        def compute(half, chip):
            here = grouped(half, chip)
            for source in range(depth - 1):

                @pl.when(source < place)
                def _():
                    wait(pairs.at[layer, source, here], pair_recv.at[layer, half, source, chip])

            def rowset(which, at_rows):
                query_rows = widen(query[layer, at_rows])
                keys = [widen(pairs[layer, source, at_rows, :lanes]) for source in range(depth)]
                attend = attend_of(query_rows, keys)
                terms = [widen(low(a)) * widen(pairs[layer, source, at_rows, lanes:]) for source, a in enumerate(attend)]
                mixed[layer, at_rows] = low(functools.reduce(jnp.add, terms))

            pieces(half, chip, rowset)
            return dot(mixed[layer, here], out_w[layer])

        return compute

    def normalize(value, gain):
        return low(value * inverse_of(value) * gain)

    def middle_sink(layer):
        def sink(half, at_rows, total):
            value = state_at(2 * layer, at_rows) + total
            states[2 * layer, at_rows] = value
            inner[layer, at_own(half, at_rows)] = normalize(value, gain_row(2 * layer + 1))

        return sink

    def by_group(half, chip, step):
        def shifted(at_rows):
            start = starts[half] + chip * 2 * sizes[half] + at_rows.start
            step(at_rows, pl.ds(pl.multiple_of(start, CHUNK), CHUNK))

        by_rows(2 * sizes[half], shifted)

    def project_second(layer):
        def compute(half, chip):
            room[: 2 * sizes[half]] = dot(inner[layer, grouped(half, chip)], second_w[layer])

            def gated(at_rows, to):
                gate = room[at_rows, :hidden_cols]
                up = room[at_rows, hidden_cols:]
                both[layer, to, :hidden_cols] = low(gate)
                both[layer, to, hidden_cols:] = low(up)
                hidden[layer, to] = low(gate * jax.nn.sigmoid(gate) * up)

            by_group(half, chip, gated)

        return compute

    def project_down(layer):
        def compute(half, chip):
            return dot(hidden[layer, grouped(half, chip)], down_w[layer])

        return compute

    def state_sink(half, at_rows, total):
        value = state_at(1, at_rows) + total
        states[1, at_rows] = value
        normed[1, at_own(half, at_rows)] = normalize(value, gain_row(2))

    def frames_sink(half, at_rows, total):
        value = state_at(3, at_rows) + total
        frames_out[at_rows] = low(jnp.where(active_ref[at_rows] > 0.0, value, 0.0))

    def hidden_back(layer):
        def compute(half, chip):
            room[: 2 * sizes[half], :hidden_cols] = dot_back(branch[grouped(half, chip)], down_w[layer])

            def gated(at_rows, to):
                upper = room[at_rows, :hidden_cols]
                gate = widen(both[layer, to, :hidden_cols])
                up = widen(both[layer, to, hidden_cols:])
                sigma = jax.nn.sigmoid(gate)
                scaled = upper * sigma
                both_grad[to, :hidden_cols] = low(scaled * up * (1.0 + gate * (1.0 - sigma)))
                both_grad[to, hidden_cols:] = low(scaled * gate)

            by_group(half, chip, gated)

        return compute

    def second_and_back(half, chip):
        project_second(1)(half, chip)
        hidden_back(1)(half, chip)

    def project_second_back(layer):
        def compute(half, chip):
            return dot_back(both_grad[grouped(half, chip)], second_w[layer])

        return compute

    def norm_back(total, value, gain, index):
        inverse = inverse_of(value)
        product = total * value * inverse
        gain_sum[index] += product[:8] + product[8:]
        scaled = total * gain
        return inverse * scaled - value * (inverse * inverse * inverse) * jnp.mean(scaled * value, axis=-1, keepdims=True)

    def inner_sink(layer):
        def sink(half, at_rows, total):
            index = 2 * layer + 1
            value = carry[at_rows] + norm_back(total, state_at(index, at_rows), gain_row(index), index)
            carry[at_rows] = value
            back[at_own(half, at_rows)] = low(value)

        return sink

    def attention_back(layer):
        def compute(half, chip):
            here = grouped(half, chip)
            room[: 2 * sizes[half], :lanes] = widen(low(dot_back(back[here], out_w[layer])))

            def rowset(which, at_rows):
                upper = room[pl.ds(pl.multiple_of(which * sizes[half], CHUNK), sizes[half]), :lanes]
                query_rows = widen(query[layer, at_rows])
                keys = [widen(pairs[layer, source, at_rows, :lanes]) for source in range(depth)]
                attend = attend_of(query_rows, keys)
                attend_grad = segment_sums([upper * widen(pairs[layer, source, at_rows, lanes:]) for source in range(depth)])
                inside = functools.reduce(jnp.add, [a * g for a, g in zip(attend, attend_grad)])
                score_grad = [widen(low(a * (g - inside))) for a, g in zip(attend, attend_grad)]
                packed_grad[at_rows, :lanes] = low(functools.reduce(jnp.add, [g * k for g, k in zip(score_grad, keys)]) * scale)
                for source in range(depth):
                    pair_out[source, at_rows, :lanes] = low(score_grad[source] * query_rows * scale)
                    pair_out[source, at_rows, lanes:] = low(widen(low(attend[source])) * upper)

            pieces(half, chip, rowset)
            for target in range(depth - 1):

                @pl.when(target < place)
                def _():
                    send(
                        pair_out.at[target, here],
                        pair_in.at[layer, place - 1, here],
                        terms_send.at[layer, half, target, chip],
                        terms_recv.at[layer, half, place - 1, chip],
                        (target, spot),
                    )

        return compute

    def finish_terms(layer):
        for half in range(2):

            def sent(chip):
                for target in range(depth - 1):

                    @pl.when(target < place)
                    def _():
                        wait(pair_out.at[target, grouped(half, chip)], terms_send.at[layer, half, target, chip])

            looped(CHAIN, sent)

    def project_first_back(layer):
        def compute(half, chip):
            here = grouped(half, chip)
            for source in range(1, depth):

                @pl.when(source > place)
                def _():
                    wait(pair_in.at[layer, source - 1, here], terms_recv.at[layer, half, source - 1, chip])

            def rowset(which, at_rows):
                total = widen(pair_out[place, at_rows])
                for source in range(1, depth):
                    total += widen(pair_in[layer, source - 1, at_rows])
                packed_grad[at_rows, lanes:] = low(total)

            pieces(half, chip, rowset)
            return dot_back(packed_grad[here], first_w[layer])

        return compute

    def carry_sink(layer):
        def sink(half, at_rows, total):
            index = 2 * layer
            value = carry[at_rows] + norm_back(total, state_at(index, at_rows), gain_row(index), index)
            if layer:
                carry[at_rows] = value
                branch[at_own(half, at_rows)] = low(value)
            else:
                input_grad[at_rows] = low(value)

        return sink

    def grad_parts(layer, kind):
        if kind == 0:
            for number in range(3):
                yield number * lanes, lanes, grads[layer][number], number
        else:
            for number in range(2):
                yield number * hidden_cols, hidden_cols, grads[layer][4 + number], 3 + number

    def grad_task(layer, kind, step):
        target = other(step)
        stage = (stage_first, stage_second)[kind]
        left = (normed, inner)[kind]
        right = (packed_grad, both_grad)[kind]
        stage[step] = low(dot_rows(left[layer, :, column(target, lanes)], right[...]))

    def grad_first(layer, job):
        @pl.when((job >= 0) & (job < count - 1))
        def _():
            step = far_first(job)
            target = other(step)
            for start, size, out, number in grad_parts(layer, 0):
                send(
                    stage_first.at[step, :, start : start + size],
                    out.at[:, column(spot, size)],
                    grad_send.at[layer, number, step],
                    grad_recv.at[layer, number, spot],
                    (place, target),
                )

    def grad_second(layer, job):
        def emit(step, which, rows_at):
            start = which * hidden_cols
            send(
                stage_second.at[step, rows_at, start : start + hidden_cols],
                grads[layer][4 + which].at[rows_at, column(spot, hidden_cols)],
                grad_send.at[layer, 3 + which, step],
                grad_recv.at[layer, 3 + which, spot],
                (place, other(step)),
            )

        second_job(job, emit)

    def grad_keep(layer, kind):
        stage = (stage_first, stage_second)[kind]
        for start, size, out, number in grad_parts(layer, kind):
            pltpu.make_async_copy(
                stage.at[0, :, start : start + size], out.at[:, column(spot, size)], grad_recv.at[layer, number, spot]
            ).start()

    def grad_sent(layer, kind):
        def sent(index):
            for start, size, out, number in grad_parts(layer, kind):
                wait(out.at[:, 0:size], grad_send.at[layer, number, index + 1])

        looped(count - 1, sent)
        for start, size, out, number in grad_parts(layer, kind):
            wait(out.at[:, 0:size], grad_recv.at[layer, number, spot])

    def grad_arrived(layer, kind):
        def arrived(index):
            source = other(index + 1)
            for start, size, out, number in grad_parts(layer, kind):
                wait(out.at[:, column(source, size)], grad_recv.at[layer, number, source])

        looped(count - 1, arrived)

    def down_task(layer, index):
        size = stage_down.shape[0] // 4
        at_rows = pl.ds(pl.multiple_of(index * size, size), size)
        stage_down[at_rows] = low(dot_rows(hidden[layer, :, column(index, size)], branch[...]))

    def down_start(layer):
        return pltpu.make_async_copy(stage_down, grads[layer][6], local_sem.at[4 + 2 * layer])

    def out_task(layer):
        stage_out[...] = low(dot_rows(mixed[layer], back[...]))

    def out_start(layer):
        return pltpu.make_async_copy(stage_out, grads[layer][3], local_sem.at[5 + 2 * layer])

    def send_sums(layer):
        for index in (2 * layer, 2 * layer + 1):

            def step(number):
                target = other(number + 1)
                send(
                    gain_sum.at[index, :, column(target, lanes)],
                    gain_back.at[index, spot],
                    sum_send.at[index, number + 1],
                    sum_recv.at[index, spot],
                    (place, target),
                )

            looped(count - 1, step)
            gain_back[index, spot] = gain_sum[index, :, column(spot, lanes)]

    def finish_sums(layer):
        for index in (2 * layer, 2 * layer + 1):

            def step(number):
                source = other(number + 1)
                wait(gain_back.at[index, source], sum_recv.at[index, source])
                wait(gain_back.at[index, 0], sum_send.at[index, number + 1])

            looped(count - 1, step)
            gains_out[index : index + 1, :] = jnp.sum(gain_back[index], axis=(0, 1), keepdims=True)[0]

    carry[...] = jnp.where(active_ref[...] > 0.0, widen(cot_ref[...]), 0.0)

    def gains_arrived(index):
        source = other(index + 1)
        wait(gain_in.at[source], gain_recv.at[source])

    looped(count - 1, gains_arrived)
    for source in range(count):
        gain_full[:, source * lanes : (source + 1) * lanes] = gain_in[source]

    for half in range(2):

        def first_rows(at_rows):
            normed[0, at_own(half, at_rows)] = normalize(state_at(0, at_rows), gain_row(0))
            branch[at_own(half, at_rows)] = low(carry[at_rows])

        by_half(half, first_rows)

    for layer in range(2):
        gather_normed = [(2 * layer, half, normed.at[layer], project_first(layer)) for half in range(2)]
        gather_inner = [(2 * layer + 1, half, inner.at[layer], second_and_back if layer else project_second(0)) for half in range(2)]
        scatter_out = [(2 * layer, half, attention(layer), middle_sink(layer)) for half in range(2)]
        if layer == 0:
            wait_weights(0, (0, 1, 2))
            phase(gathers=gather_normed[:1], slack=lambda index, point: send_second(0, index * 3 + point))
            loads[0].wait()
            phase(scatter_out[:1], gather_normed[1:], lambda index, point: send_second(0, 15 + index * 3 + point))
            wait_weights(0, (3, 4))

            def feed(index, point):
                if point < 2:
                    send_first(1, index * 2 + point)

            phase(scatter_out[1:], gather_inner[:1], feed)
            loads[1].wait()
            scatter_down = [(1, half, project_down(0), state_sink) for half in range(2)]

            def feed(index, point, base=0):
                if point < 2:
                    send_second(1, base + index * 2 + point)

            phase(scatter_down[:1], gather_inner[1:], feed)
            finish_weights(0)
            finish_pairs(0)
        else:
            wait_weights(1, (0, 1, 2))
            phase(scatter_down[1:], gather_normed[:1] + [(4, 0, branch, None)], functools.partial(feed, base=10))
            loads[2].wait()
            phase(scatter_out[:1], gather_normed[1:] + [(4, 1, branch, None)], functools.partial(feed, base=20))
            wait_weights(1, (3, 4))
            loads[3].wait()
            phase(scatter_out[1:], gather_inner[:1])
            finish_weights(1)
            finish_pairs(1)

    scatter_inner = [(4, half, project_second_back(1), inner_sink(1)) for half in range(2)]
    phase(scatter_inner[:1], gather_inner[1:])
    for layer in (1, 0):
        gather_back = [(5 if layer else 7, half, back, attention_back(layer)) for half in range(2)]
        scatter_normed = [(5 if layer else 7, half, project_first_back(layer), carry_sink(layer)) for half in range(2)]
        if layer == 0:
            grad_sent(1, 1)
            down_start(1).wait()
            out_start(1).wait()

        def second_grads(index, point, layer=layer):
            if point == 0:

                @pl.when(index < CHAIN)
                def _():
                    grad_task(layer, 1, far_first(2 * index))
                    grad_task(layer, 1, far_first(2 * index + 1))
                    down_task(layer, index)

            @pl.when(index > 0)
            def _():
                grad_second(layer, (index - 1) * 3 + point)

        def more_second_grads(index, point, layer=layer):
            grad_second(layer, 12 + index * 3 + point)

        phase(scatter_inner[1:], gather_back[:1], second_grads)
        down_start(layer).start()
        grad_keep(layer, 1)
        if layer:
            last = [(LAST_OUT, half, project_down(1), frames_sink) for half in range(2)]
            phase(scatter_normed[:1], gather_back[1:], more_second_grads)
            gather_branch = [(6, half, branch, hidden_back(0)) for half in range(2)]

            def rest(index, point):
                if point == 0:
                    grad_second(1, 27 + index)

            phase(scatter_normed[1:] + last[:1], gather_branch[:1], rest)
            finish_terms(1)
            out_task(1)
            out_start(1).start()
            send_sums(1)

            def first_grads(index, point):
                if point == 0:

                    @pl.when(index < CHAIN)
                    def _():
                        grad_task(1, 0, far_first(2 * index))
                        grad_task(1, 0, far_first(2 * index + 1))

                else:
                    grad_first(1, index * 2 + point - 1)

            scatter_inner = [(6, half, project_second_back(0), inner_sink(0)) for half in range(2)]
            phase(scatter_inner[:1] + last[1:], gather_branch[1:], first_grads)
            grad_keep(1, 0)
        else:
            phase(scatter_normed[:1], gather_back[1:], more_second_grads)
            out_task(0)
            out_start(0).start()
            grad_sent(1, 0)

            def last_grads(index, point):
                if point == 0:
                    grad_second(0, 27 + index)

                    @pl.when(index == CHAIN - 1)
                    def _():
                        def both_tasks(job):
                            grad_task(0, 0, far_first(job))
                            grad_first(0, job)

                        looped(count, both_tasks)

            phase(scatter_normed[1:], (), last_grads)
            grad_keep(0, 0)
            send_sums(0)
            finish_terms(0)

    for done in pending:
        done()
    down_start(0).wait()
    out_start(0).wait()
    for layer in (1, 0):
        finish_sums(layer)
        for kind in range(2):
            grad_arrived(layer, kind)
    for kind in range(2):
        grad_sent(0, kind)
    for step in range(1, count):
        wait(gain_in.at[0], gain_send.at[step])


def split_body(*args):
    frames_in, depth_counts, out_grad = args[0][:, 0], args[1], args[-1][:, 0]
    rows, width = frames_in.shape
    depth = lax.axis_size("section")
    count = lax.axis_size("dp")
    lanes = width // count
    layers = [tuple(a[0] for a in args[2:11]), tuple(a[0] for a in args[11:20])]
    ff_cols = layers[0][6].shape[1]
    hidden_cols = ff_cols // count
    down_rows = layers[0][8].shape[0]
    place = lax.axis_index("section")
    active = (place < depth_counts).astype(jnp.float32)[:, None]
    gains = jnp.stack([layers[0][0], layers[0][5], layers[1][0], layers[1][5]]).astype(jnp.float32)
    gains = jnp.concatenate([gains, jnp.zeros((4, lanes), jnp.float32)])
    index = jnp.arange(lanes) // HEAD_DIM
    segments = (index[:, None] == index[None, :]).astype(jnp.bfloat16)
    weights = [layer[i] for layer in layers for i in (1, 2, 3, 4, 6, 7, 8)]
    total = rows * count
    low_type, full_type = jnp.bfloat16, jnp.float32
    grad_shapes = [(lanes, width)] * 4 + [(lanes, ff_cols)] * 2 + [(down_rows, width)]
    out_shape = (
        [jax.ShapeDtypeStruct((rows, width), low_type)] * 2
        + [jax.ShapeDtypeStruct((4, lanes), full_type)]
        + [jax.ShapeDtypeStruct(shape, low_type) for shape in grad_shapes * 2]
    )
    vmem, anywhere = pl.BlockSpec(memory_space=pltpu.VMEM), pl.BlockSpec(memory_space=pl.ANY)
    held = pltpu.VMEM
    sems = pltpu.SemaphoreType.DMA
    scratch = [
        held((2, width, 3 * lanes), low_type),
        held((2, width, 2 * hidden_cols), low_type),
        held((2, lanes, width), low_type),
        held((2, down_rows, width), low_type),
        held((2, total, width), low_type),
        held((2, total, width), low_type),
        held((total, width), low_type),
        held((total, width), low_type),
        held((2, total, lanes), low_type),
        held((2, depth, total, 2 * lanes), low_type),
        held((2, total, lanes), low_type),
        held((2, total, 2 * hidden_cols), low_type),
        held((2, total, hidden_cols), low_type),
        held((total, 2 * hidden_cols), low_type),
        held((total, 3 * lanes), low_type),
        held((2, depth - 1, total, 2 * lanes), low_type),
        held((depth, total, 2 * lanes), low_type),
        held((2, 2, rows, width), full_type),
        held((2, CHAIN, rows, width), full_type),
        held((2, CHAIN + 1, rows, width), low_type),
        held((2, CHAIN - 1, rows, width), low_type),
        held((3, rows, width), full_type),
        held((rows, width), full_type),
        held((count, 8, lanes), full_type),
        held((8, width), full_type),
        held((4, 8, width), full_type),
        held((4, count, 8, lanes), full_type),
        held((count, lanes, 3 * lanes), low_type),
        held((count, lanes, 2 * hidden_cols), low_type),
        held((down_rows, width), low_type),
        held((lanes, width), low_type),
        held((2 * -(-rows // (2 * CHUNK)) * CHUNK, width), full_type),
        sems((8, 2, 15)),
        sems((8, 2, count)),
        sems((8, 2, CHAIN)),
        sems((8, 2, CHAIN)),
        sems((8, 2, CHAIN)),
        sems((8, 2, CHAIN + 1)),
        sems((2, 2, depth, CHAIN)),
        sems((2, 2, depth, CHAIN)),
        sems((2, 2, depth, CHAIN)),
        sems((2, 2, depth, CHAIN)),
        sems((2, 5, count)),
        sems((2, 5, count)),
        sems((2, 5, count)),
        sems((2, 5, count)),
        sems((count,)),
        sems((count,)),
        sems((4, count)),
        sems((4, count)),
        sems((8,)),
    ]
    outs = pl.pallas_call(
        split_kernel,
        out_shape=out_shape,
        in_specs=[vmem] * 5 + [anywhere] * 14,
        out_specs=[vmem] * 3 + [anywhere] * 14,
        scratch_shapes=scratch,
        compiler_params=pltpu.CompilerParams(
            collective_id=0, has_side_effects=True, vmem_limit_bytes=VMEM_BYTES
        ),
        cost_estimate=pl.CostEstimate(flops=2 * 6 * total * width * (4 * lanes + 3 * hidden_cols), bytes_accessed=1 << 26, transcendentals=1 << 22),
    )(frames_in, out_grad, active, gains, segments, *weights)
    gain_grads = outs[2]
    result = [outs[0][:, None], outs[1][:, None]]
    for layer in range(2):
        wide = [out.astype(jnp.float32)[None] for out in outs[3 + 7 * layer : 10 + 7 * layer]]
        result += [gain_grads[2 * layer][None], *wide[:4], gain_grads[2 * layer + 1][None], *wide[4:]]
    return tuple(result)


def solution(mesh):
    in_specs = (
        P("dp", "section", None),
        P("dp"),
        P("section", "dp"),
        P("section", "dp", None),
        P("section", "dp", None),
        P("section", "dp", None),
        P("section", "dp", None),
        P("section", "dp"),
        P("section", "dp", None),
        P("section", "dp", None),
        P("section", "dp", None),
        P("section", "dp"),
        P("section", "dp", None),
        P("section", "dp", None),
        P("section", "dp", None),
        P("section", "dp", None),
        P("section", "dp"),
        P("section", "dp", None),
        P("section", "dp", None),
        P("section", "dp", None),
        P("dp", "section", None),
    )
    out_specs = (
        P("dp", "section", None),
        P("dp", "section", None),
        P("section", "dp"),
        P("section", "dp", None),
        P("section", "dp", None),
        P("section", "dp", None),
        P("section", "dp", None),
        P("section", "dp"),
        P("section", "dp", None),
        P("section", "dp", None),
        P("section", "dp", None),
        P("section", "dp"),
        P("section", "dp", None),
        P("section", "dp", None),
        P("section", "dp", None),
        P("section", "dp", None),
        P("section", "dp"),
        P("section", "dp", None),
        P("section", "dp", None),
        P("section", "dp", None),
    )
    parts, sections = mesh.shape["dp"], mesh.shape["section"]
    chosen = split_body if parts == 2 * CHAIN and sections == 4 else body
    return jax.shard_map(chosen, mesh=mesh, in_specs=in_specs, out_specs=out_specs, check_vma=False)
```

```python
import functools

import jax
import jax.numpy as jnp
from jax import lax
from jax.experimental import pallas as pl
from jax.experimental.pallas import tpu as pltpu
from jax.sharding import PartitionSpec as P

HEAD_DIM = 64
MICRO = 2


EPSILON = 1e-05
VMEM_BYTES = 63 * 2**20


def rms_apply(state, gain):
    inverse = lax.rsqrt(jnp.mean(state * state, axis=-1, keepdims=True) + EPSILON)
    return (state * inverse * gain.astype(jnp.float32)[None], inverse)


def rms_back(upper, state, inverse, gain):
    gain_grad = jnp.sum(upper * state * inverse, axis=0)
    scaled = upper * gain.astype(jnp.float32)[None]
    lower = inverse * scaled - state * (inverse * inverse * inverse) * jnp.mean(
        scaled * state, axis=-1, keepdims=True
    )
    return (lower, gain_grad)


def project(left, weight):
    return jnp.einsum("fpd,pde->fpe", left, weight, preferred_element_type=jnp.float32)


def project_back(grad, weight):
    return jnp.einsum("fpe,pde->fpd", grad, weight, preferred_element_type=jnp.float32)


def outer(left, grad):
    return jnp.einsum("fpd,fpe->pde", left, grad, preferred_element_type=jnp.float32)


def fetch(params):
    attn_gain, query_w, key_w, value_w, out_w, ffn_gain, gate_w, up_w, down_w = params
    return (
        lax.all_gather(attn_gain, "dp", axis=1, tiled=True),
        lax.all_gather(query_w, "dp", axis=1, tiled=True),
        lax.all_gather(key_w, "dp", axis=1, tiled=True),
        lax.all_gather(value_w, "dp", axis=1, tiled=True),
        lax.all_gather(out_w, "dp", axis=1, tiled=True),
        lax.all_gather(ffn_gain, "dp", axis=1, tiled=True),
        lax.all_gather(gate_w, "dp", axis=1, tiled=True),
        lax.all_gather(up_w, "dp", axis=1, tiled=True),
        lax.all_gather(down_w, "dp", axis=1, tiled=True),
    )


def fetch_again(params):
    attn_gain, query_w, key_w, value_w, out_w, ffn_gain, gate_w, up_w, down_w = params
    return (
        lax.all_gather(attn_gain, "dp", axis=1, tiled=True),
        lax.all_gather(query_w, "dp", axis=1, tiled=True),
        lax.all_gather(key_w, "dp", axis=1, tiled=True),
        lax.all_gather(value_w, "dp", axis=1, tiled=True),
        lax.all_gather(out_w, "dp", axis=1, tiled=True),
        lax.all_gather(ffn_gain, "dp", axis=1, tiled=True),
        lax.all_gather(gate_w, "dp", axis=1, tiled=True),
        lax.all_gather(up_w, "dp", axis=1, tiled=True),
        lax.all_gather(down_w, "dp", axis=1, tiled=True),
    )


def layer_forward(state, params, positions):
    attn_gain, query_w, key_w, value_w, out_w, ffn_gain, gate_w, up_w, down_w = params
    frames, local, width = state.shape
    heads = width // HEAD_DIM
    normed_full, inverse_one = rms_apply(state, attn_gain)
    normed = normed_full.astype(jnp.bfloat16)
    query = project(normed, query_w).astype(jnp.bfloat16)
    keys = project(normed, key_w).astype(jnp.bfloat16)
    values = project(normed, value_w).astype(jnp.bfloat16)
    all_keys, all_values = (
        lax.all_gather(keys, "section", axis=1, tiled=True),
        lax.all_gather(values, "section", axis=1, tiled=True),
    )
    depth = all_keys.shape[1]
    query_heads = query.reshape(frames, local, heads, HEAD_DIM)
    key_heads = all_keys.reshape(frames, depth, heads, HEAD_DIM)
    value_heads = all_values.reshape(frames, depth, heads, HEAD_DIM)
    scores = jnp.einsum(
        "fphc,fshc->fhps", query_heads, key_heads, preferred_element_type=jnp.float32
    ) * HEAD_DIM ** (-0.5)
    allowed = positions[:, None] >= jnp.arange(depth)[None, :]
    scores = jnp.where(allowed[None, None], scores, -1e30)
    largest = jnp.max(scores, axis=-1, keepdims=True)
    expd = jnp.exp(scores - largest)
    attend = expd / jnp.sum(expd, axis=-1, keepdims=True)
    attend_low = attend.astype(jnp.bfloat16)
    mixed = jnp.einsum(
        "fhps,fshc->fphc", attend_low, value_heads, preferred_element_type=jnp.float32
    )
    mixed = mixed.reshape(frames, local, width).astype(jnp.bfloat16)
    middle = state + project(mixed, out_w)
    inner_full, inverse_two = rms_apply(middle, ffn_gain)
    inner = inner_full.astype(jnp.bfloat16)
    gate = project(inner, gate_w)
    up = project(inner, up_w)
    hidden = (jax.nn.silu(gate) * up).astype(jnp.bfloat16)
    result = middle + project(hidden, down_w)
    kept = (
        state,
        inverse_one,
        normed,
        query_heads,
        key_heads,
        value_heads,
        attend,
        attend_low,
        mixed,
        middle,
        inverse_two,
        inner,
        gate,
        up,
        hidden,
    )
    return (result, kept)


def layer_backward(carried, params, kept):
    attn_gain, query_w, key_w, value_w, out_w, ffn_gain, gate_w, up_w, down_w = params
    (
        state,
        inverse_one,
        normed,
        query_heads,
        key_heads,
        value_heads,
        attend,
        attend_low,
        mixed,
        middle,
        inverse_two,
        inner,
        gate,
        up,
        hidden,
    ) = kept
    frames, local, width = state.shape
    depth = key_heads.shape[1]
    branch_grad = carried.astype(jnp.bfloat16)
    hidden_grad = project_back(branch_grad, down_w)
    sigma = jax.nn.sigmoid(gate)
    gate_grad = (hidden_grad * up * sigma * (1.0 + gate * (1.0 - sigma))).astype(jnp.bfloat16)
    up_grad = (hidden_grad * gate * sigma).astype(jnp.bfloat16)
    inner_grad = project_back(gate_grad, gate_w) + project_back(up_grad, up_w)
    lower_two, grad_ffn_gain = rms_back(inner_grad, middle, inverse_two, ffn_gain)
    middle_grad = carried + lower_two
    mixed_back = middle_grad.astype(jnp.bfloat16)
    mixed_grad = project_back(mixed_back, out_w).astype(jnp.bfloat16)
    mixed_heads = mixed_grad.reshape(frames, local, -1, HEAD_DIM)
    attend_grad = jnp.einsum(
        "fphc,fshc->fhps", mixed_heads, value_heads, preferred_element_type=jnp.float32
    )
    value_terms = jnp.einsum(
        "fhps,fphc->fshc", attend_low, mixed_heads, preferred_element_type=jnp.float32
    ).reshape(frames, depth, width)
    score_grad = attend * (attend_grad - jnp.sum(attend * attend_grad, axis=-1, keepdims=True))
    score_grad = score_grad.astype(jnp.bfloat16)
    scale = HEAD_DIM ** (-0.5)
    query_grad = (
        jnp.einsum("fhps,fshc->fphc", score_grad, key_heads, preferred_element_type=jnp.float32)
        * scale
    )
    query_grad = query_grad.reshape(frames, local, width).astype(jnp.bfloat16)
    key_terms = (
        jnp.einsum("fhps,fphc->fshc", score_grad, query_heads, preferred_element_type=jnp.float32)
        * scale
    )
    key_terms = key_terms.reshape(frames, depth, width)
    keys_sum, values_sum = (
        lax.psum_scatter(key_terms, "section", scatter_dimension=1, tiled=True),
        lax.psum_scatter(value_terms, "section", scatter_dimension=1, tiled=True),
    )
    keys_grad = keys_sum.astype(jnp.bfloat16)
    values_grad = values_sum.astype(jnp.bfloat16)
    normed_grad = (
        project_back(query_grad, query_w)
        + project_back(keys_grad, key_w)
        + project_back(values_grad, value_w)
    )
    lower_one, grad_attn_gain = rms_back(normed_grad, state, inverse_one, attn_gain)
    deferred = (
        grad_attn_gain,
        grad_ffn_gain,
        hidden,
        branch_grad,
        inner,
        gate_grad,
        up_grad,
        mixed,
        mixed_back,
        normed,
        query_grad,
        keys_grad,
        values_grad,
    )
    return (middle_grad + lower_one, deferred)


def join_deferred(pieces):
    gains = tuple(
        (sum((piece[index] for piece in pieces[1:])) + pieces[0][index] for index in (0, 1))
    )
    rest = tuple(
        (jnp.concatenate([piece[index] for piece in pieces], axis=0) for index in range(2, 13))
    )
    return gains + rest


def weight_terms(deferred):
    (
        grad_attn_gain,
        grad_ffn_gain,
        hidden,
        branch_grad,
        inner,
        gate_grad,
        up_grad,
        mixed,
        mixed_back,
        normed,
        query_grad,
        keys_grad,
        values_grad,
    ) = deferred
    return (
        grad_attn_gain,
        outer(normed, query_grad),
        outer(normed, keys_grad),
        outer(normed, values_grad),
        outer(mixed, mixed_back),
        grad_ffn_gain,
        outer(inner, gate_grad),
        outer(inner, up_grad),
        outer(hidden, branch_grad),
    )


def reduce_grads(full):
    (
        grad_attn_gain,
        grad_query,
        grad_key,
        grad_value,
        grad_out,
        grad_ffn_gain,
        grad_gate,
        grad_up,
        grad_down,
    ) = full
    return (
        lax.psum_scatter(grad_attn_gain, "dp", scatter_dimension=1, tiled=True),
        lax.psum_scatter(grad_query, "dp", scatter_dimension=1, tiled=True),
        lax.psum_scatter(grad_key, "dp", scatter_dimension=1, tiled=True),
        lax.psum_scatter(grad_value, "dp", scatter_dimension=1, tiled=True),
        lax.psum_scatter(grad_out, "dp", scatter_dimension=1, tiled=True),
        lax.psum_scatter(grad_ffn_gain, "dp", scatter_dimension=1, tiled=True),
        lax.psum_scatter(grad_gate, "dp", scatter_dimension=1, tiled=True),
        lax.psum_scatter(grad_up, "dp", scatter_dimension=1, tiled=True),
        lax.psum_scatter(grad_down, "dp", scatter_dimension=1, tiled=True),
    )


def body(
    frames_in,
    depth_counts,
    attn_gain_1,
    query_weight_1,
    key_weight_1,
    value_weight_1,
    out_weight_1,
    ffn_gain_1,
    gate_weight_1,
    up_weight_1,
    down_weight_1,
    attn_gain_2,
    query_weight_2,
    key_weight_2,
    value_weight_2,
    out_weight_2,
    ffn_gain_2,
    gate_weight_2,
    up_weight_2,
    down_weight_2,
    out_grad,
):
    layers = (
        (
            attn_gain_1,
            query_weight_1,
            key_weight_1,
            value_weight_1,
            out_weight_1,
            ffn_gain_1,
            gate_weight_1,
            up_weight_1,
            down_weight_1,
        ),
        (
            attn_gain_2,
            query_weight_2,
            key_weight_2,
            value_weight_2,
            out_weight_2,
            ffn_gain_2,
            gate_weight_2,
            up_weight_2,
            down_weight_2,
        ),
    )
    frames_dev = frames_in.shape[0]
    local = frames_in.shape[1]
    portion = frames_dev // MICRO
    positions = lax.axis_index("section") * local + jnp.arange(local)
    active = positions[None, :] < depth_counts[:, None]
    gathered = [fetch(layers[0]), fetch(layers[1])]
    keeps = [[], []]
    results = []
    for micro in range(MICRO):
        state = frames_in[micro * portion : (micro + 1) * portion].astype(jnp.float32)
        for number in (0, 1):
            state, kept = layer_forward(state, gathered[number], positions)
            keeps[number].append(kept)
        results.append(state)
    state = jnp.concatenate(results, axis=0)
    frames_out = jnp.where(active[:, :, None], state, 0.0).astype(jnp.bfloat16)
    masked = jnp.where(active[:, :, None], out_grad.astype(jnp.float32), 0.0)
    carries = [masked[micro * portion : (micro + 1) * portion] for micro in range(MICRO)]
    reduced = [None, None]
    for number in (1, 0):
        params = fetch_again(layers[number])
        pieces = []
        for micro in range(MICRO):
            carries[micro], deferred = layer_backward(carries[micro], params, keeps[number][micro])
            pieces.append(deferred)
        reduced[number] = reduce_grads(weight_terms(join_deferred(pieces)))
    first, second = reduced
    input_grad = jnp.concatenate(carries, axis=0).astype(jnp.bfloat16)
    return (
        frames_out,
        input_grad,
        first[0],
        first[1],
        first[2],
        first[3],
        first[4],
        first[5],
        first[6],
        first[7],
        first[8],
        second[0],
        second[1],
        second[2],
        second[3],
        second[4],
        second[5],
        second[6],
        second[7],
        second[8],
    )


HEAD_LANES = 128
CHAIN = 4
CHUNK = 16
LAST_OUT = 3
MESH = pl.DeviceIdType.MESH


def widen(value):
    return value.astype(jnp.float32)


def low(value):
    return value.astype(jnp.bfloat16)


def dot(left, right):
    return jnp.dot(left, right, preferred_element_type=jnp.float32)


def dot_rows(left, right):
    return lax.dot_general(left, right, (((0,), (0,)), ((), ())), preferred_element_type=jnp.float32)


def dot_back(left, right):
    return lax.dot_general(left, right, (((1,), (1,)), ((), ())), preferred_element_type=jnp.float32)


def looped(count, step):
    lax.fori_loop(0, count, lambda index, carry: (step(index), carry)[1], 0)


def by_rows(rows, step, size=CHUNK):
    looped(rows // size, lambda index: step(pl.ds(pl.multiple_of(index * size, size), size)))


def split_kernel(*refs):
    (frames_ref, cot_ref, counts_ref), gain_refs, refs = refs[:3], refs[3:7], refs[7:]
    weights, refs = (refs[:7], refs[7:14]), refs[14:]
    (frames_out, input_grad), gains_out, refs = refs[:2], refs[2:6], refs[6:]
    grads, refs = (refs[:7], refs[7:14]), refs[14:]
    (
        first_w, second_w, out_w, down_w, normed, inner, branch, back, query, pairs, mixed, both, hidden,
        both_grad, packed_grad, pair_in, pair_out, part, core_in, chain_in, chain_out, states, carry,
        gain_in, gain_full, gain_sum, gain_back, stage_first, stage_second, stage_down, stage_out, room,
        active_ref, gains_ref, segments_ref,
    ), refs = refs[:35], refs[35:]
    (
        gather_send, gather_recv, core_send, core_recv, chain_send, chain_recv, pair_send, pair_recv,
        terms_send, terms_recv, weight_send, weight_recv, grad_send, grad_recv, gain_send, gain_recv,
        sum_send, sum_recv, local_sem,
    ) = refs

    rows, width = frames_ref.shape
    count = 2 * CHAIN
    lanes = width // count
    hidden_cols = second_w.shape[2] // 2
    depth = pairs.shape[1]
    scale = HEAD_DIM ** (-0.5)
    place = lax.axis_index("section")
    spot = lax.axis_index("dp")
    z = spot // 2
    core = spot % 2
    twin = 1 - core

    def at(chip, which):
        return (place, chip * 2 + which)

    def send(source, target, send_sem, recv_sem, device):
        pltpu.make_async_remote_copy(
            src_ref=source, dst_ref=target, send_sem=send_sem, recv_sem=recv_sem, device_id=device, device_id_type=MESH
        ).start()

    def wait(ref, sem):
        pltpu.make_async_copy(ref, ref, sem).wait()

    first_size = -(-rows // (2 * CHUNK)) * CHUNK
    sizes = (first_size, rows - first_size)
    spans = (pl.ds(0, first_size), pl.ds(first_size, rows - first_size))
    starts = (0, count * first_size)

    def half_rows(half, index):
        return pl.ds(pl.multiple_of(starts[half] + index * sizes[half], CHUNK), sizes[half])

    def grouped(half, chip):
        return pl.ds(pl.multiple_of(starts[half] + chip * 2 * sizes[half], 2 * CHUNK), 2 * sizes[half])

    def by_half(half, step):
        by_rows(sizes[half], lambda at_rows: step(pl.ds(pl.multiple_of(at_rows.start + spans[half].start, CHUNK), CHUNK)))

    def column(index, size):
        return pl.ds(pl.multiple_of(index * size, size), size)

    def other(step):
        hop, cross = step // 2, step % 2
        chip = jnp.where(hop == 1, z + 1 - 2 * (z % 2), jnp.where(hop == 2, (z + 2) % 4, jnp.where(hop == 3, 3 - z, z)))
        return chip * 2 + jnp.where(cross == 1, twin, core)

    barrier = pltpu.get_barrier_semaphore()
    for step in range(1, count):
        pl.semaphore_signal(barrier, inc=1, device_id=(place, (spot + step) % count), device_id_type=MESH)
    for step in range(1, depth):
        pl.semaphore_signal(barrier, inc=1, device_id=((place + step) % depth, spot), device_id_type=MESH)

    loads = []
    for layer in range(2):
        loads.append(pltpu.make_async_copy(weights[layer][3], out_w.at[layer], local_sem.at[2 * layer]))
        loads.append(pltpu.make_async_copy(weights[layer][6], down_w.at[layer], local_sem.at[2 * layer + 1]))
    for load in loads:
        load.start()
    mine = pl.ds(pl.multiple_of(spot * lanes, lanes), lanes)

    def weight_parts(layer):
        for number in range(3):
            yield weights[layer][number], first_w, number * lanes, lanes, number
        for number in range(2):
            yield weights[layer][4 + number], second_w, number * hidden_cols, hidden_cols, 3 + number

    def own_weights(layer):
        for source, held, start, size, number in weight_parts(layer):
            yield pltpu.make_async_copy(
                source.at[:, column(spot, size)], held.at[layer, mine, start : start + size], weight_recv.at[layer, number, spot]
            )

    for layer in range(2):
        for copy in own_weights(layer):
            copy.start()

    def send_weights(layer, numbers, step):
        target = other(step)
        for source, held, start, size, number in weight_parts(layer):
            if number in numbers:
                send(
                    source.at[:, column(target, size)],
                    held.at[layer, mine, start : start + size],
                    weight_send.at[layer, number, step],
                    weight_recv.at[layer, number, spot],
                    (place, target),
                )

    def far_first(index):
        step = 0
        for number, value in enumerate((4, 2, 5, 6, 3, 7, 1)):
            step = jnp.where(index == number, value, step)
        return step

    def second_job(job, emit):
        step = far_first(job % (count - 1))
        piece = job // (count - 1)
        rows_at = pl.ds(pl.multiple_of(piece // 2 * (lanes // 2), lanes // 2), lanes // 2)
        for which in range(2):

            @pl.when((piece % 2 == which) & (job >= 0) & (job < 4 * (count - 1)))
            def _():
                emit(step, which, rows_at)

    def send_second(layer, job):
        def emit(step, which, rows_at):
            target = other(step)
            start = which * hidden_cols
            to = pl.ds(pl.multiple_of(spot * lanes + rows_at.start, lanes // 2), lanes // 2)
            send(
                weights[layer][4 + which].at[rows_at, column(target, hidden_cols)],
                second_w.at[layer, to, start : start + hidden_cols],
                weight_send.at[layer, 3 + which, step],
                weight_recv.at[layer, 3 + which, spot],
                (place, target),
            )

        second_job(job, emit)

    def send_first(layer, job):
        @pl.when((job >= 0) & (job < count - 1))
        def _():
            send_weights(layer, (0, 1, 2), far_first(job))

    def wait_weights(layer, numbers):
        def arrived(index):
            for _, held, start, size, number in weight_parts(layer):
                if number in numbers:
                    wait(held.at[layer, column(index, lanes), start : start + size], weight_recv.at[layer, number, index])

        looped(count, arrived)

    def finish_weights(layer):
        def sent(index):
            for _, held, start, size, number in weight_parts(layer):
                wait(held.at[layer, pl.ds(0, lanes), start : start + size], weight_send.at[layer, number, index + 1])

        looped(count - 1, sent)

    gains_ref[...] = jnp.zeros_like(gains_ref)
    for index, ref in enumerate(gain_refs):
        gains_ref[index : index + 1] = widen(ref[...])
    gain_in[spot] = gains_ref[...]

    pl.semaphore_wait(barrier, count - 1 + depth - 1)

    for step in range(1, count):
        send(gains_ref, gain_in.at[spot], gain_send.at[step], gain_recv.at[spot], (place, other(step)))
    looped(count - 1, lambda index: send_first(0, index))

    for layer in range(2):
        for source in range(1, depth):

            @pl.when(place < source)
            def _():
                pairs[layer, source] = jnp.zeros(pairs.shape[2:], pairs.dtype)

            @pl.when(place >= source)
            def _():
                pair_in[layer, source - 1] = jnp.zeros(pair_in.shape[2:], pair_in.dtype)

    for parity in range(2):

        @pl.when(z == 0)
        def _():
            for index in range(CHAIN):
                chain_in[parity, index] = jnp.zeros(chain_in.shape[2:], chain_in.dtype)

        @pl.when(z == CHAIN - 1)
        def _():
            for index in (0, 1, 2, 4):
                chain_in[parity, index] = jnp.zeros(chain_in.shape[2:], chain_in.dtype)
    gain_sum[...] = jnp.zeros_like(gain_sum)

    def own_rows(half):
        return half_rows(half, spot)

    def gather_start(number, half, held):
        own = held.at[own_rows(half)]
        send(own, own, gather_send.at[number, half, 0], gather_recv.at[number, half, spot], at(z, twin))

        @pl.when(z < CHAIN - 1)
        def _():
            send(own, own, gather_send.at[number, half, 1], gather_recv.at[number, half, spot], at(z + 1, core))

        @pl.when(z > 0)
        def _():
            send(own, own, gather_send.at[number, half, 2], gather_recv.at[number, half, spot], at(z - 1, core))

    def gather_arrive(number, half, held, index):
        below, above = z - index, z + index

        @pl.when((index > 0) & (index < CHAIN) & (below >= 0))
        def _():
            source = below * 2 + core
            here = held.at[half_rows(half, source)]
            wait(here, gather_recv.at[number, half, source])

            @pl.when(z < CHAIN - 1)
            def _():
                send(here, here, gather_send.at[number, half, 2 + index], gather_recv.at[number, half, source], at(z + 1, core))

            send(here, here, gather_send.at[number, half, 8 + index], gather_recv.at[number, half, source], at(z, twin))

        @pl.when((index > 0) & (above < CHAIN))
        def _():
            source = above * 2 + core
            here = held.at[half_rows(half, source)]
            wait(here, gather_recv.at[number, half, source])

            @pl.when(z > 0)
            def _():
                send(here, here, gather_send.at[number, half, 5 + index], gather_recv.at[number, half, source], at(z - 1, core))

            send(here, here, gather_send.at[number, half, 11 + index], gather_recv.at[number, half, source], at(z, twin))

    def gather_compute(number, half, held, compute, index):
        def side(which):
            chip = z - index + 2 * index * which

            @pl.when((chip >= 0) & (chip < CHAIN) & (index + 1 > which) & (index < CHAIN))
            def _():
                source = chip * 2 + twin
                wait(held.at[half_rows(half, source)], gather_recv.at[number, half, source])
                if compute is not None:
                    compute(half, chip)

        looped(2, side)

    def gather_finish(number, half, held):
        one = held.at[half_rows(half, 0)]
        wait(one, gather_send.at[number, half, 0])

        @pl.when(z < CHAIN - 1)
        def _():
            wait(one, gather_send.at[number, half, 1])

        @pl.when(z > 0)
        def _():
            wait(one, gather_send.at[number, half, 2])

        def step(index):
            @pl.when(z - index >= 0)
            def _():
                @pl.when(z < CHAIN - 1)
                def _():
                    wait(one, gather_send.at[number, half, 2 + index])

                wait(one, gather_send.at[number, half, 8 + index])

            @pl.when(z + index < CHAIN)
            def _():
                @pl.when(z > 0)
                def _():
                    wait(one, gather_send.at[number, half, 5 + index])

                wait(one, gather_send.at[number, half, 11 + index])

        looped(CHAIN - 1, lambda index: step(index + 1))

    def order(index):
        first = 3 * (1 - z // 2)
        second = 2 - z // 2
        third = 1 - z % 2 + 2 * (z // 2)
        return jnp.where(index == 0, first, jnp.where(index == 1, second, jnp.where(index == 2, third, z)))

    def scatter_compute(number, half, compute, index):
        bank = 1 if number == LAST_OUT else 0
        span = spans[half]

        @pl.when(index < CHAIN)
        def _():
            slot = index % 2

            @pl.when(index > 1)
            def _():
                wait(part.at[slot, twin, span], core_send.at[number, half, index - 2])

            product = compute(half, order(index))
            part[slot, 0, span] = product[: sizes[half]]
            part[slot, 1, span] = product[sizes[half] :]
            send(
                part.at[slot, twin, span],
                core_in.at[bank, index, span],
                core_send.at[number, half, index],
                core_recv.at[number, half, index],
                at(z, twin),
            )

    def scatter_send(number, half, index, allowed):
        bank = 1 if number == LAST_OUT else 0
        span = spans[half]

        @pl.when((index > 0) & (index < CHAIN) & allowed)
        def _():
            held = index - 1
            slot = held % 2
            target = order(held)
            wait(core_in.at[bank, held, span], core_recv.at[number, half, held])

            @pl.when(((target > z) & (z > 0)) | ((target < z) & (z < CHAIN - 1)))
            def _():
                wait(chain_in.at[bank, target, span], chain_recv.at[number, half, target])

            def add(at_rows):
                total = part[slot, core, at_rows] + core_in[bank, held, at_rows]
                chain_out[bank, held, at_rows] = low(total + widen(chain_in[bank, target, at_rows]))

            by_half(half, add)

            @pl.when(target > z)
            def _():
                send(
                    chain_out.at[bank, held, span],
                    chain_in.at[bank, target, span],
                    chain_send.at[number, half, held],
                    chain_recv.at[number, half, target],
                    at(z + 1, core),
                )

            @pl.when(target < z)
            def _():
                landing = jnp.where(target == z - 1, CHAIN, target)
                send(
                    chain_out.at[bank, held, span],
                    chain_in.at[bank, landing, span],
                    chain_send.at[number, half, held],
                    chain_recv.at[number, half, landing],
                    at(z - 1, core),
                )

    def scatter_end(number, half, sink, index):
        bank = 1 if number == LAST_OUT else 0
        span = spans[half]
        held = CHAIN - 1
        slot = held % 2

        @pl.when(index == CHAIN)
        def _():
            wait(core_in.at[bank, held, span], core_recv.at[number, half, held])

            @pl.when(z > 0)
            def _():
                wait(chain_in.at[bank, z, span], chain_recv.at[number, half, z])

            @pl.when(z < CHAIN - 1)
            def _():
                wait(chain_in.at[bank, CHAIN, span], chain_recv.at[number, half, CHAIN])

            def total(at_rows):
                sink(
                    half,
                    at_rows,
                    part[slot, core, at_rows]
                    + core_in[bank, held, at_rows]
                    + widen(chain_in[bank, z, at_rows])
                    + widen(chain_in[bank, CHAIN, at_rows]),
                )

            by_half(half, total)

    def scatter_finish(number, half):
        span = spans[half]

        def sent(index):
            wait(chain_out.at[0, index, span], chain_send.at[number, half, index])

        looped(CHAIN - 1, sent)

    def core_finish(number, half):
        for index in (CHAIN - 2, CHAIN - 1):
            wait(part.at[index % 2, twin, spans[half]], core_send.at[number, half, index])

    pending = []

    def phase(scatters=(), gathers=(), slack=None, ready=None):
        for number, half, held, _ in gathers:
            gather_start(number, half, held)

        outer = (z == 0) | (z == CHAIN - 1)
        inside = (z > 0) & (z < CHAIN - 1)

        def step(index):
            for number, half, compute, sink in scatters:
                scatter_compute(number, half, compute, index)
                scatter_send(number, half, index, outer)
            if slack is not None:
                slack(index, 0)
            for number, half, held, _ in gathers:
                gather_arrive(number, half, held, index)
            for number, half, compute, sink in scatters:
                scatter_send(number, half, index, inside)
            if slack is not None:
                slack(index, 1)
            if ready is not None:
                pl.when(index == 0)(ready)
            for number, half, held, compute in gathers:
                gather_compute(number, half, held, compute, index)
            for number, half, compute, sink in scatters:
                scatter_end(number, half, sink, index)
            if slack is not None:
                slack(index, 2)

        looped(CHAIN + 1, step)
        for number, half, _, _ in scatters:
            core_finish(number, half)
        for done in pending:
            done()
        pending.clear()
        for number, half, held, _ in gathers:
            pending.append(functools.partial(gather_finish, number, half, held))
        for number, half, _, _ in scatters:
            pending.append(functools.partial(scatter_finish, number, half))

    def state_at(index, at_rows):
        return states[index - 1, at_rows] if index else widen(frames_ref[at_rows])

    def gain_row(index):
        return gain_full[index : index + 1, :]

    def inverse_of(value):
        return lax.rsqrt(jnp.mean(value * value, axis=-1, keepdims=True) + EPSILON)

    def at_own(half, at_rows):
        start = starts[half] + spot * sizes[half] + at_rows.start - spans[half].start
        return pl.ds(pl.multiple_of(start, CHUNK), CHUNK)

    def pieces(half, chip, step):
        looped(2, lambda which: step(which, half_rows(half, chip * 2 + which)))

    def project_first(layer):
        def compute(half, chip):
            here = grouped(half, chip)
            packed = low(dot(normed[layer, here], first_w[layer]))
            query[layer, here] = packed[:, :lanes]
            pairs[layer, place, here] = packed[:, lanes:]
            for step in range(1, depth):

                @pl.when(place + step < depth)
                def _():
                    ref = pairs.at[layer, place, here]
                    send(ref, ref, pair_send.at[layer, half, step, chip], pair_recv.at[layer, half, place, chip], (place + step, spot))

        return compute

    def finish_pairs(layer):
        for half in range(2):

            def sent(chip):
                for step in range(1, depth):

                    @pl.when(place + step < depth)
                    def _():
                        wait(pairs.at[layer, place, grouped(half, chip)], pair_send.at[layer, half, step, chip])

            looped(CHAIN, sent)

    def segment_sums(values):
        size = values[0].shape[0]
        high = [low(value) for value in values]
        rest = [low(value - widen(upper)) for value, upper in zip(values, high)]
        sums = dot(jnp.concatenate(high + rest, axis=0), segments_ref[...])
        half = len(values) * size
        return [sums[i * size : (i + 1) * size] + sums[half + i * size : half + (i + 1) * size] for i in range(len(values))]

    def attend_of(query_rows, keys):
        scores = segment_sums([query_rows * key for key in keys])
        scores = [jnp.where(index <= place, score * scale, -1e30) for index, score in enumerate(scores)]
        largest = functools.reduce(jnp.maximum, scores)
        expd = [jnp.exp(score - largest) for score in scores]
        inverse = 1.0 / functools.reduce(jnp.add, expd)
        return [value * inverse for value in expd]

    def attention(layer):
        def compute(half, chip):
            here = grouped(half, chip)
            for source in range(depth - 1):

                @pl.when(source < place)
                def _():
                    wait(pairs.at[layer, source, here], pair_recv.at[layer, half, source, chip])

            def rowset(which, at_rows):
                query_rows = widen(query[layer, at_rows])
                keys = [widen(pairs[layer, source, at_rows, :lanes]) for source in range(depth)]
                attend = attend_of(query_rows, keys)
                terms = [widen(low(a)) * widen(pairs[layer, source, at_rows, lanes:]) for source, a in enumerate(attend)]
                mixed[layer, at_rows] = low(functools.reduce(jnp.add, terms))

            pieces(half, chip, rowset)
            return dot(mixed[layer, here], out_w[layer])

        return compute

    def normalize(value, gain):
        return low(value * inverse_of(value) * gain)

    def middle_sink(layer):
        def sink(half, at_rows, total):
            value = state_at(2 * layer, at_rows) + total
            states[2 * layer, at_rows] = value
            inner[layer, at_own(half, at_rows)] = normalize(value, gain_row(2 * layer + 1))

        return sink

    def by_group(half, chip, step):
        def shifted(at_rows):
            start = starts[half] + chip * 2 * sizes[half] + at_rows.start
            step(at_rows, pl.ds(pl.multiple_of(start, CHUNK), CHUNK))

        by_rows(2 * sizes[half], shifted)

    def project_second(layer):
        def compute(half, chip):
            room[: 2 * sizes[half]] = dot(inner[layer, grouped(half, chip)], second_w[layer])

            def gated(at_rows, to):
                gate = room[at_rows, :hidden_cols]
                up = room[at_rows, hidden_cols:]
                both[layer, to, :hidden_cols] = low(gate)
                both[layer, to, hidden_cols:] = low(up)
                hidden[layer, to] = low(gate * jax.nn.sigmoid(gate) * up)

            by_group(half, chip, gated)

        return compute

    def project_down(layer):
        def compute(half, chip):
            return dot(hidden[layer, grouped(half, chip)], down_w[layer])

        return compute

    def state_sink(half, at_rows, total):
        value = state_at(1, at_rows) + total
        states[1, at_rows] = value
        normed[1, at_own(half, at_rows)] = normalize(value, gain_row(2))

    def frames_sink(half, at_rows, total):
        value = state_at(3, at_rows) + total
        frames_out[at_rows] = low(jnp.where(active_ref[at_rows] > 0.0, value, 0.0))

    def hidden_back(layer):
        def compute(half, chip):
            room[: 2 * sizes[half], :hidden_cols] = dot_back(branch[grouped(half, chip)], down_w[layer])

            def gated(at_rows, to):
                upper = room[at_rows, :hidden_cols]
                gate = widen(both[layer, to, :hidden_cols])
                up = widen(both[layer, to, hidden_cols:])
                sigma = jax.nn.sigmoid(gate)
                scaled = upper * sigma
                both_grad[to, :hidden_cols] = low(scaled * up * (1.0 + gate * (1.0 - sigma)))
                both_grad[to, hidden_cols:] = low(scaled * gate)

            by_group(half, chip, gated)

        return compute

    def second_and_back(half, chip):
        project_second(1)(half, chip)
        hidden_back(1)(half, chip)

    def project_second_back(layer):
        def compute(half, chip):
            return dot_back(both_grad[grouped(half, chip)], second_w[layer])

        return compute

    def norm_back(total, value, gain, index):
        inverse = inverse_of(value)
        product = total * value * inverse
        gain_sum[index] += product[:8] + product[8:]
        scaled = total * gain
        return inverse * scaled - value * (inverse * inverse * inverse) * jnp.mean(scaled * value, axis=-1, keepdims=True)

    def inner_sink(layer):
        def sink(half, at_rows, total):
            index = 2 * layer + 1
            value = carry[at_rows] + norm_back(total, state_at(index, at_rows), gain_row(index), index)
            carry[at_rows] = value
            back[at_own(half, at_rows)] = low(value)

        return sink

    def attention_back(layer):
        def compute(half, chip):
            here = grouped(half, chip)
            room[: 2 * sizes[half], :lanes] = widen(low(dot_back(back[here], out_w[layer])))

            def rowset(which, at_rows):
                upper = room[pl.ds(pl.multiple_of(which * sizes[half], CHUNK), sizes[half]), :lanes]
                query_rows = widen(query[layer, at_rows])
                keys = [widen(pairs[layer, source, at_rows, :lanes]) for source in range(depth)]
                attend = attend_of(query_rows, keys)
                attend_grad = segment_sums([upper * widen(pairs[layer, source, at_rows, lanes:]) for source in range(depth)])
                inside = functools.reduce(jnp.add, [a * g for a, g in zip(attend, attend_grad)])
                score_grad = [widen(low(a * (g - inside))) for a, g in zip(attend, attend_grad)]
                packed_grad[at_rows, :lanes] = low(functools.reduce(jnp.add, [g * k for g, k in zip(score_grad, keys)]) * scale)
                for source in range(depth):
                    pair_out[source, at_rows, :lanes] = low(score_grad[source] * query_rows * scale)
                    pair_out[source, at_rows, lanes:] = low(widen(low(attend[source])) * upper)

            pieces(half, chip, rowset)
            for target in range(depth - 1):

                @pl.when(target < place)
                def _():
                    send(
                        pair_out.at[target, here],
                        pair_in.at[layer, place - 1, here],
                        terms_send.at[layer, half, target, chip],
                        terms_recv.at[layer, half, place - 1, chip],
                        (target, spot),
                    )

        return compute

    def finish_terms(layer):
        for half in range(2):

            def sent(chip):
                for target in range(depth - 1):

                    @pl.when(target < place)
                    def _():
                        wait(pair_out.at[target, grouped(half, chip)], terms_send.at[layer, half, target, chip])

            looped(CHAIN, sent)

    def project_first_back(layer):
        def compute(half, chip):
            here = grouped(half, chip)
            for source in range(1, depth):

                @pl.when(source > place)
                def _():
                    wait(pair_in.at[layer, source - 1, here], terms_recv.at[layer, half, source - 1, chip])

            def rowset(which, at_rows):
                total = widen(pair_out[place, at_rows])
                for source in range(1, depth):
                    total += widen(pair_in[layer, source - 1, at_rows])
                packed_grad[at_rows, lanes:] = low(total)

            pieces(half, chip, rowset)
            return dot_back(packed_grad[here], first_w[layer])

        return compute

    def carry_sink(layer):
        def sink(half, at_rows, total):
            index = 2 * layer
            value = carry[at_rows] + norm_back(total, state_at(index, at_rows), gain_row(index), index)
            if layer:
                carry[at_rows] = value
                branch[at_own(half, at_rows)] = low(value)
            else:
                input_grad[at_rows] = low(value)

        return sink

    def grad_parts(layer, kind):
        if kind == 0:
            for number in range(3):
                yield number * lanes, lanes, grads[layer][number], number
        else:
            for number in range(2):
                yield number * hidden_cols, hidden_cols, grads[layer][4 + number], 3 + number

    def grad_task(layer, kind, step, start=0, stop=None):
        target = other(step)
        stage = (stage_first, stage_second)[kind]
        left = (normed, inner)[kind]
        right = (packed_grad, both_grad)[kind]
        stop = stop or right.shape[1]
        stage[step, :, start:stop] = low(dot_rows(left[layer, :, column(target, lanes)], right[:, start:stop]))

    def grad_first(layer, job, numbers=(0, 1, 2)):
        @pl.when((job >= 0) & (job < count - 1))
        def _():
            step = far_first(job)
            target = other(step)
            for start, size, out, number in grad_parts(layer, 0):
                if number not in numbers:
                    continue
                send(
                    stage_first.at[step, :, start : start + size],
                    out.at[:, column(spot, size)],
                    grad_send.at[layer, number, step],
                    grad_recv.at[layer, number, spot],
                    (place, target),
                )

    def grad_second(layer, job):
        def emit(step, which, rows_at):
            start = which * hidden_cols
            send(
                stage_second.at[step, rows_at, start : start + hidden_cols],
                grads[layer][4 + which].at[rows_at, column(spot, hidden_cols)],
                grad_send.at[layer, 3 + which, step],
                grad_recv.at[layer, 3 + which, spot],
                (place, other(step)),
            )

        second_job(job, emit)

    def grad_keep(layer, kind):
        stage = (stage_first, stage_second)[kind]
        for start, size, out, number in grad_parts(layer, kind):
            pltpu.make_async_copy(
                stage.at[0, :, start : start + size], out.at[:, column(spot, size)], grad_recv.at[layer, number, spot]
            ).start()

    def grad_sent(layer, kind):
        def sent(index):
            for start, size, out, number in grad_parts(layer, kind):
                wait(out.at[:, 0:size], grad_send.at[layer, number, index + 1])

        looped(count - 1, sent)
        for start, size, out, number in grad_parts(layer, kind):
            wait(out.at[:, 0:size], grad_recv.at[layer, number, spot])

    def grad_arrived(layer, kind):
        def arrived(index):
            source = other(index + 1)
            for start, size, out, number in grad_parts(layer, kind):
                wait(out.at[:, column(source, size)], grad_recv.at[layer, number, source])

        looped(count - 1, arrived)

    def down_task(layer, index):
        size = stage_down.shape[0] // 4
        at_rows = pl.ds(pl.multiple_of(index * size, size), size)
        stage_down[at_rows] = low(dot_rows(hidden[layer, :, column(index, size)], branch[...]))

    def down_start(layer):
        return pltpu.make_async_copy(stage_down, grads[layer][6], local_sem.at[4 + 2 * layer])

    def out_task(layer):
        stage_out[...] = low(dot_rows(mixed[layer], back[...]))

    def out_start(layer):
        return pltpu.make_async_copy(stage_out, grads[layer][3], local_sem.at[5 + 2 * layer])

    def send_sums(layer):
        for index in (2 * layer, 2 * layer + 1):

            def step(number):
                target = other(number + 1)
                send(
                    gain_sum.at[index, :, column(target, lanes)],
                    gain_back.at[index, spot],
                    sum_send.at[index, number + 1],
                    sum_recv.at[index, spot],
                    (place, target),
                )

            looped(count - 1, step)
            gain_back[index, spot] = gain_sum[index, :, column(spot, lanes)]

    def finish_sums(layer):
        for index in (2 * layer, 2 * layer + 1):

            def step(number):
                source = other(number + 1)
                wait(gain_back.at[index, source], sum_recv.at[index, source])
                wait(gain_back.at[index, 0], sum_send.at[index, number + 1])

            looped(count - 1, step)
            gains_out[index][...] = jnp.sum(gain_back[index], axis=(0, 1), keepdims=True)[0]

    square = (rows, rows)
    on_row = lax.broadcasted_iota(jnp.int32, square, 0) == lax.broadcasted_iota(jnp.int32, square, 1)
    spread = jnp.sum(jnp.where(on_row, counts_ref[...], 0).astype(jnp.float32), axis=1, keepdims=True)
    active_ref[...] = (spread > place.astype(jnp.float32)).astype(jnp.float32)
    square = segments_ref.shape
    head = [lax.broadcasted_iota(jnp.int32, square, axis) // HEAD_DIM for axis in range(2)]
    segments_ref[...] = low((head[0] == head[1]).astype(jnp.float32))
    carry[...] = jnp.where(active_ref[...] > 0.0, widen(cot_ref[...]), 0.0)

    def gains_arrived(index):
        source = other(index + 1)
        wait(gain_in.at[source], gain_recv.at[source])

    looped(count - 1, gains_arrived)
    for source in range(count):
        gain_full[:, source * lanes : (source + 1) * lanes] = gain_in[source]

    for half in range(2):

        def first_rows(at_rows):
            normed[0, at_own(half, at_rows)] = normalize(state_at(0, at_rows), gain_row(0))
            branch[at_own(half, at_rows)] = low(carry[at_rows])

        by_half(half, first_rows)

    for layer in range(2):
        gather_normed = [(2 * layer, half, normed.at[layer], project_first(layer)) for half in range(2)]
        gather_inner = [(2 * layer + 1, half, inner.at[layer], second_and_back if layer else project_second(0)) for half in range(2)]
        scatter_out = [(2 * layer, half, attention(layer), middle_sink(layer)) for half in range(2)]
        if layer == 0:
            def feed(index, point):
                if point < 2:
                    send_second(0, index * 2 + point)

            phase((), gather_normed[:1], feed, lambda: wait_weights(0, (0, 1, 2)))
            loads[0].wait()

            def feed(index, point):
                send_second(0, 10 + index * 4 + point)
                if point == 2:
                    send_second(0, 13 + index * 4)

            phase(scatter_out[:1], gather_normed[1:], feed)

            def feed(index, point):
                if point < 2:
                    send_first(1, index * 2 + point)
                else:
                    send_second(1, index)

            phase(scatter_out[1:], gather_inner[:1], feed, lambda: wait_weights(0, (3, 4)))
            loads[1].wait()
            scatter_down = [(1, half, project_down(0), state_sink) for half in range(2)]

            def feed(index, point, base=5, limit=13):
                if point < 2:
                    job = base + index * 2 + point

                    @pl.when(job < limit)
                    def _():
                        send_second(1, job)

            phase(scatter_down[:1], gather_inner[1:], feed)
            finish_weights(0)
            finish_pairs(0)
        else:
            phase(scatter_down[1:], gather_normed[:1], functools.partial(feed, base=13, limit=21), lambda: wait_weights(1, (0, 1, 2)))
            loads[2].wait()
            phase(scatter_out[:1], gather_normed[1:], functools.partial(feed, base=21, limit=28))
            loads[3].wait()
            phase(scatter_out[1:], [(4, 0, branch, None)] + gather_inner[:1], None, lambda: wait_weights(1, (3, 4)))
            finish_weights(1)
            finish_pairs(1)

    scatter_inner = [(4, half, project_second_back(1), inner_sink(1)) for half in range(2)]
    phase(scatter_inner[:1], [(4, 1, branch, None)] + gather_inner[1:])
    for layer in (1, 0):
        gather_back = [(5 if layer else 7, half, back, attention_back(layer)) for half in range(2)]
        scatter_normed = [(5 if layer else 7, half, project_first_back(layer), carry_sink(layer)) for half in range(2)]
        if layer == 0:
            grad_sent(1, 1)
            down_start(1).wait()
            out_start(1).wait()

        def second_grads(index, point, layer=layer):
            if point == 0:

                @pl.when(index < CHAIN)
                def _():
                    grad_task(layer, 1, far_first(2 * index))
                    grad_task(layer, 1, far_first(2 * index + 1))
                    down_task(layer, index)

            @pl.when(index > 0)
            def _():
                grad_second(layer, (index - 1) * 3 + point)

        def more_second_grads(index, point, layer=layer):
            grad_second(layer, 12 + index * 2 + point) if point < 2 else None

        last = [(LAST_OUT, half, project_down(1), frames_sink) for half in range(2)] if layer else [None, None]
        phase(scatter_inner[1:] + last[:1] * layer, gather_back[:1], second_grads)
        down_start(layer).start()
        grad_keep(layer, 1)
        if layer:
            phase(scatter_normed[:1] + last[1:], gather_back[1:], more_second_grads)
            gather_branch = [(6, half, branch, hidden_back(0)) for half in range(2)]

            def rest(index, point):
                if point < 2:
                    grad_second(1, 22 + 2 * index + point)

            phase(scatter_normed[1:], gather_branch[:1], rest)
            finish_terms(1)
            out_task(1)
            out_start(1).start()
            send_sums(1)

            def first_grads(index, point):
                if point == 0:

                    @pl.when(index < CHAIN)
                    def _():
                        grad_task(1, 0, far_first(2 * index))
                        grad_task(1, 0, far_first(2 * index + 1))

                else:
                    grad_first(1, index * 2 + point - 1)

            scatter_inner = [(6, half, project_second_back(0), inner_sink(0)) for half in range(2)]
            phase(scatter_inner[:1], gather_branch[1:], first_grads)
            grad_keep(1, 0)
        else:
            phase(scatter_normed[:1], gather_back[1:], more_second_grads)
            out_task(0)
            out_start(0).start()
            grad_sent(1, 0)

            def last_grads(index, point):
                def query_task(job):
                    grad_task(0, 0, far_first(job), 0, lanes)
                    grad_first(0, job, (0,))

                def rest_task(job):
                    grad_task(0, 0, far_first(job), lanes, 3 * lanes)
                    grad_first(0, job, (1, 2))

                if point < 2:
                    grad_second(0, 22 + 2 * index + point)

                if point == 0:

                    @pl.when(index == 1)
                    def _():
                        looped(count, query_task)

                    @pl.when(index == CHAIN - 1)
                    def _():
                        looped(count, rest_task)

            phase(scatter_normed[1:], (), last_grads)
            grad_keep(0, 0)
            send_sums(0)
            finish_terms(0)

    for done in pending:
        done()
    down_start(0).wait()
    out_start(0).wait()
    for layer in (1, 0):
        finish_sums(layer)
        for kind in range(2):
            grad_arrived(layer, kind)
    for kind in range(2):
        grad_sent(0, kind)
    for step in range(1, count):
        wait(gain_in.at[0], gain_send.at[step])


def widen_kernel(*refs):
    half = len(refs) // 2
    for source, target in zip(refs[:half], refs[half:]):
        target[...] = source[...].astype(target.dtype)


def widen_all(whole, arrays, steps=2):
    specs = [pl.BlockSpec(array.shape, lambda index: (0, 0)) for array in whole]
    specs += [pl.BlockSpec((array.shape[0] // steps, array.shape[1]), lambda index: (index, 0)) for array in arrays]
    shapes = [jax.ShapeDtypeStruct(array.shape, array.dtype) for array in whole]
    shapes += [jax.ShapeDtypeStruct(array.shape, jnp.float32) for array in arrays]
    return pl.pallas_call(
        widen_kernel,
        grid=(steps,),
        out_shape=shapes,
        in_specs=specs,
        out_specs=specs,
        compiler_params=pltpu.CompilerParams(vmem_limit_bytes=VMEM_BYTES),
    )(*whole, *arrays)


def split_body(*args):
    frames_in, depth_counts, out_grad = args[0][:, 0], args[1], args[-1][:, 0]
    rows, width = frames_in.shape
    depth = lax.axis_size("section")
    count = lax.axis_size("dp")
    lanes = width // count
    layers = [tuple(a[0] for a in args[2:11]), tuple(a[0] for a in args[11:20])]
    ff_cols = layers[0][6].shape[1]
    hidden_cols = ff_cols // count
    down_rows = layers[0][8].shape[0]
    gains = [layer[i][None] for layer in layers for i in (0, 5)]
    weights = [layer[i] for layer in layers for i in (1, 2, 3, 4, 6, 7, 8)]
    total = rows * count
    low_type, full_type = jnp.bfloat16, jnp.float32
    grad_shapes = [(lanes, width)] * 4 + [(lanes, ff_cols)] * 2 + [(down_rows, width)]
    out_shape = (
        [jax.ShapeDtypeStruct((rows, width), low_type)] * 2
        + [jax.ShapeDtypeStruct((1, lanes), full_type)] * 4
        + [jax.ShapeDtypeStruct(shape, low_type) for shape in grad_shapes * 2]
    )
    vmem, anywhere = pl.BlockSpec(memory_space=pltpu.VMEM), pl.BlockSpec(memory_space=pl.ANY)
    held = pltpu.VMEM
    sems = pltpu.SemaphoreType.DMA
    scratch = [
        held((2, width, 3 * lanes), low_type),
        held((2, width, 2 * hidden_cols), low_type),
        held((2, lanes, width), low_type),
        held((2, down_rows, width), low_type),
        held((2, total, width), low_type),
        held((2, total, width), low_type),
        held((total, width), low_type),
        held((total, width), low_type),
        held((2, total, lanes), low_type),
        held((2, depth, total, 2 * lanes), low_type),
        held((2, total, lanes), low_type),
        held((2, total, 2 * hidden_cols), low_type),
        held((2, total, hidden_cols), low_type),
        held((total, 2 * hidden_cols), low_type),
        held((total, 3 * lanes), low_type),
        held((2, depth - 1, total, 2 * lanes), low_type),
        held((depth, total, 2 * lanes), low_type),
        held((2, 2, rows, width), full_type),
        held((2, CHAIN, rows, width), full_type),
        held((2, CHAIN + 1, rows, width), low_type),
        held((2, CHAIN - 1, rows, width), low_type),
        held((3, rows, width), full_type),
        held((rows, width), full_type),
        held((count, 8, lanes), full_type),
        held((8, width), full_type),
        held((4, 8, width), full_type),
        held((4, count, 8, lanes), full_type),
        held((count, lanes, 3 * lanes), low_type),
        held((count, lanes, 2 * hidden_cols), low_type),
        held((down_rows, width), low_type),
        held((lanes, width), low_type),
        held((2 * -(-rows // (2 * CHUNK)) * CHUNK, width), full_type),
        held((rows, 1), full_type),
        held((8, lanes), full_type),
        held((lanes, lanes), low_type),
        sems((8, 2, 15)),
        sems((8, 2, count)),
        sems((8, 2, CHAIN)),
        sems((8, 2, CHAIN)),
        sems((8, 2, CHAIN)),
        sems((8, 2, CHAIN + 1)),
        sems((2, 2, depth, CHAIN)),
        sems((2, 2, depth, CHAIN)),
        sems((2, 2, depth, CHAIN)),
        sems((2, 2, depth, CHAIN)),
        sems((2, 5, count)),
        sems((2, 5, count)),
        sems((2, 5, count)),
        sems((2, 5, count)),
        sems((count,)),
        sems((count,)),
        sems((4, count)),
        sems((4, count)),
        sems((8,)),
    ]
    outs = pl.pallas_call(
        split_kernel,
        out_shape=out_shape,
        in_specs=[vmem] * 7 + [anywhere] * 14,
        out_specs=[vmem] * 6 + [anywhere] * 14,
        scratch_shapes=scratch,
        compiler_params=pltpu.CompilerParams(
            collective_id=0, has_side_effects=True, vmem_limit_bytes=VMEM_BYTES
        ),
        cost_estimate=pl.CostEstimate(flops=2 * 6 * total * width * (4 * lanes + 3 * hidden_cols), bytes_accessed=1 << 26, transcendentals=1 << 22),
    )(frames_in, out_grad, depth_counts[None], *gains, *weights)
    wide = widen_all(outs[:6], outs[6:])
    result = [wide[0][:, None], wide[1][:, None]]
    for layer in range(2):
        own = [out[None] for out in wide[6 + 7 * layer : 13 + 7 * layer]]
        result += [wide[2 + 2 * layer], *own[:4], wide[3 + 2 * layer], *own[4:]]
    return tuple(result)


def solution(mesh):
    in_specs = (
        P("dp", "section", None),
        P("dp"),
        P("section", "dp"),
        P("section", "dp", None),
        P("section", "dp", None),
        P("section", "dp", None),
        P("section", "dp", None),
        P("section", "dp"),
        P("section", "dp", None),
        P("section", "dp", None),
        P("section", "dp", None),
        P("section", "dp"),
        P("section", "dp", None),
        P("section", "dp", None),
        P("section", "dp", None),
        P("section", "dp", None),
        P("section", "dp"),
        P("section", "dp", None),
        P("section", "dp", None),
        P("section", "dp", None),
        P("dp", "section", None),
    )
    out_specs = (
        P("dp", "section", None),
        P("dp", "section", None),
        P("section", "dp"),
        P("section", "dp", None),
        P("section", "dp", None),
        P("section", "dp", None),
        P("section", "dp", None),
        P("section", "dp"),
        P("section", "dp", None),
        P("section", "dp", None),
        P("section", "dp", None),
        P("section", "dp"),
        P("section", "dp", None),
        P("section", "dp", None),
        P("section", "dp", None),
        P("section", "dp", None),
        P("section", "dp"),
        P("section", "dp", None),
        P("section", "dp", None),
        P("section", "dp", None),
    )
    parts, sections = mesh.shape["dp"], mesh.shape["section"]
    chosen = split_body if parts == 2 * CHAIN and sections == 4 else body
    return jax.shard_map(chosen, mesh=mesh, in_specs=in_specs, out_specs=out_specs, check_vma=False)
```

```python
import functools

import jax
import jax.numpy as jnp
from jax import lax
from jax.experimental import pallas as pl
from jax.experimental.pallas import tpu as pltpu
from jax.sharding import PartitionSpec as P

HEAD_DIM = 64
MICRO = 2


EPSILON = 1e-05
VMEM_BYTES = 63 * 2**20


def rms_apply(state, gain):
    inverse = lax.rsqrt(jnp.mean(state * state, axis=-1, keepdims=True) + EPSILON)
    return (state * inverse * gain.astype(jnp.float32)[None], inverse)


def rms_back(upper, state, inverse, gain):
    gain_grad = jnp.sum(upper * state * inverse, axis=0)
    scaled = upper * gain.astype(jnp.float32)[None]
    lower = inverse * scaled - state * (inverse * inverse * inverse) * jnp.mean(
        scaled * state, axis=-1, keepdims=True
    )
    return (lower, gain_grad)


def project(left, weight):
    return jnp.einsum("fpd,pde->fpe", left, weight, preferred_element_type=jnp.float32)


def project_back(grad, weight):
    return jnp.einsum("fpe,pde->fpd", grad, weight, preferred_element_type=jnp.float32)


def outer(left, grad):
    return jnp.einsum("fpd,fpe->pde", left, grad, preferred_element_type=jnp.float32)


def fetch(params):
    attn_gain, query_w, key_w, value_w, out_w, ffn_gain, gate_w, up_w, down_w = params
    return (
        lax.all_gather(attn_gain, "dp", axis=1, tiled=True),
        lax.all_gather(query_w, "dp", axis=1, tiled=True),
        lax.all_gather(key_w, "dp", axis=1, tiled=True),
        lax.all_gather(value_w, "dp", axis=1, tiled=True),
        lax.all_gather(out_w, "dp", axis=1, tiled=True),
        lax.all_gather(ffn_gain, "dp", axis=1, tiled=True),
        lax.all_gather(gate_w, "dp", axis=1, tiled=True),
        lax.all_gather(up_w, "dp", axis=1, tiled=True),
        lax.all_gather(down_w, "dp", axis=1, tiled=True),
    )


def fetch_again(params):
    attn_gain, query_w, key_w, value_w, out_w, ffn_gain, gate_w, up_w, down_w = params
    return (
        lax.all_gather(attn_gain, "dp", axis=1, tiled=True),
        lax.all_gather(query_w, "dp", axis=1, tiled=True),
        lax.all_gather(key_w, "dp", axis=1, tiled=True),
        lax.all_gather(value_w, "dp", axis=1, tiled=True),
        lax.all_gather(out_w, "dp", axis=1, tiled=True),
        lax.all_gather(ffn_gain, "dp", axis=1, tiled=True),
        lax.all_gather(gate_w, "dp", axis=1, tiled=True),
        lax.all_gather(up_w, "dp", axis=1, tiled=True),
        lax.all_gather(down_w, "dp", axis=1, tiled=True),
    )


def layer_forward(state, params, positions):
    attn_gain, query_w, key_w, value_w, out_w, ffn_gain, gate_w, up_w, down_w = params
    frames, local, width = state.shape
    heads = width // HEAD_DIM
    normed_full, inverse_one = rms_apply(state, attn_gain)
    normed = normed_full.astype(jnp.bfloat16)
    query = project(normed, query_w).astype(jnp.bfloat16)
    keys = project(normed, key_w).astype(jnp.bfloat16)
    values = project(normed, value_w).astype(jnp.bfloat16)
    all_keys, all_values = (
        lax.all_gather(keys, "section", axis=1, tiled=True),
        lax.all_gather(values, "section", axis=1, tiled=True),
    )
    depth = all_keys.shape[1]
    query_heads = query.reshape(frames, local, heads, HEAD_DIM)
    key_heads = all_keys.reshape(frames, depth, heads, HEAD_DIM)
    value_heads = all_values.reshape(frames, depth, heads, HEAD_DIM)
    scores = jnp.einsum(
        "fphc,fshc->fhps", query_heads, key_heads, preferred_element_type=jnp.float32
    ) * HEAD_DIM ** (-0.5)
    allowed = positions[:, None] >= jnp.arange(depth)[None, :]
    scores = jnp.where(allowed[None, None], scores, -1e30)
    largest = jnp.max(scores, axis=-1, keepdims=True)
    expd = jnp.exp(scores - largest)
    attend = expd / jnp.sum(expd, axis=-1, keepdims=True)
    attend_low = attend.astype(jnp.bfloat16)
    mixed = jnp.einsum(
        "fhps,fshc->fphc", attend_low, value_heads, preferred_element_type=jnp.float32
    )
    mixed = mixed.reshape(frames, local, width).astype(jnp.bfloat16)
    middle = state + project(mixed, out_w)
    inner_full, inverse_two = rms_apply(middle, ffn_gain)
    inner = inner_full.astype(jnp.bfloat16)
    gate = project(inner, gate_w)
    up = project(inner, up_w)
    hidden = (jax.nn.silu(gate) * up).astype(jnp.bfloat16)
    result = middle + project(hidden, down_w)
    kept = (
        state,
        inverse_one,
        normed,
        query_heads,
        key_heads,
        value_heads,
        attend,
        attend_low,
        mixed,
        middle,
        inverse_two,
        inner,
        gate,
        up,
        hidden,
    )
    return (result, kept)


def layer_backward(carried, params, kept):
    attn_gain, query_w, key_w, value_w, out_w, ffn_gain, gate_w, up_w, down_w = params
    (
        state,
        inverse_one,
        normed,
        query_heads,
        key_heads,
        value_heads,
        attend,
        attend_low,
        mixed,
        middle,
        inverse_two,
        inner,
        gate,
        up,
        hidden,
    ) = kept
    frames, local, width = state.shape
    depth = key_heads.shape[1]
    branch_grad = carried.astype(jnp.bfloat16)
    hidden_grad = project_back(branch_grad, down_w)
    sigma = jax.nn.sigmoid(gate)
    gate_grad = (hidden_grad * up * sigma * (1.0 + gate * (1.0 - sigma))).astype(jnp.bfloat16)
    up_grad = (hidden_grad * gate * sigma).astype(jnp.bfloat16)
    inner_grad = project_back(gate_grad, gate_w) + project_back(up_grad, up_w)
    lower_two, grad_ffn_gain = rms_back(inner_grad, middle, inverse_two, ffn_gain)
    middle_grad = carried + lower_two
    mixed_back = middle_grad.astype(jnp.bfloat16)
    mixed_grad = project_back(mixed_back, out_w).astype(jnp.bfloat16)
    mixed_heads = mixed_grad.reshape(frames, local, -1, HEAD_DIM)
    attend_grad = jnp.einsum(
        "fphc,fshc->fhps", mixed_heads, value_heads, preferred_element_type=jnp.float32
    )
    value_terms = jnp.einsum(
        "fhps,fphc->fshc", attend_low, mixed_heads, preferred_element_type=jnp.float32
    ).reshape(frames, depth, width)
    score_grad = attend * (attend_grad - jnp.sum(attend * attend_grad, axis=-1, keepdims=True))
    score_grad = score_grad.astype(jnp.bfloat16)
    scale = HEAD_DIM ** (-0.5)
    query_grad = (
        jnp.einsum("fhps,fshc->fphc", score_grad, key_heads, preferred_element_type=jnp.float32)
        * scale
    )
    query_grad = query_grad.reshape(frames, local, width).astype(jnp.bfloat16)
    key_terms = (
        jnp.einsum("fhps,fphc->fshc", score_grad, query_heads, preferred_element_type=jnp.float32)
        * scale
    )
    key_terms = key_terms.reshape(frames, depth, width)
    keys_sum, values_sum = (
        lax.psum_scatter(key_terms, "section", scatter_dimension=1, tiled=True),
        lax.psum_scatter(value_terms, "section", scatter_dimension=1, tiled=True),
    )
    keys_grad = keys_sum.astype(jnp.bfloat16)
    values_grad = values_sum.astype(jnp.bfloat16)
    normed_grad = (
        project_back(query_grad, query_w)
        + project_back(keys_grad, key_w)
        + project_back(values_grad, value_w)
    )
    lower_one, grad_attn_gain = rms_back(normed_grad, state, inverse_one, attn_gain)
    deferred = (
        grad_attn_gain,
        grad_ffn_gain,
        hidden,
        branch_grad,
        inner,
        gate_grad,
        up_grad,
        mixed,
        mixed_back,
        normed,
        query_grad,
        keys_grad,
        values_grad,
    )
    return (middle_grad + lower_one, deferred)


def join_deferred(pieces):
    gains = tuple(
        (sum((piece[index] for piece in pieces[1:])) + pieces[0][index] for index in (0, 1))
    )
    rest = tuple(
        (jnp.concatenate([piece[index] for piece in pieces], axis=0) for index in range(2, 13))
    )
    return gains + rest


def weight_terms(deferred):
    (
        grad_attn_gain,
        grad_ffn_gain,
        hidden,
        branch_grad,
        inner,
        gate_grad,
        up_grad,
        mixed,
        mixed_back,
        normed,
        query_grad,
        keys_grad,
        values_grad,
    ) = deferred
    return (
        grad_attn_gain,
        outer(normed, query_grad),
        outer(normed, keys_grad),
        outer(normed, values_grad),
        outer(mixed, mixed_back),
        grad_ffn_gain,
        outer(inner, gate_grad),
        outer(inner, up_grad),
        outer(hidden, branch_grad),
    )


def reduce_grads(full):
    (
        grad_attn_gain,
        grad_query,
        grad_key,
        grad_value,
        grad_out,
        grad_ffn_gain,
        grad_gate,
        grad_up,
        grad_down,
    ) = full
    return (
        lax.psum_scatter(grad_attn_gain, "dp", scatter_dimension=1, tiled=True),
        lax.psum_scatter(grad_query, "dp", scatter_dimension=1, tiled=True),
        lax.psum_scatter(grad_key, "dp", scatter_dimension=1, tiled=True),
        lax.psum_scatter(grad_value, "dp", scatter_dimension=1, tiled=True),
        lax.psum_scatter(grad_out, "dp", scatter_dimension=1, tiled=True),
        lax.psum_scatter(grad_ffn_gain, "dp", scatter_dimension=1, tiled=True),
        lax.psum_scatter(grad_gate, "dp", scatter_dimension=1, tiled=True),
        lax.psum_scatter(grad_up, "dp", scatter_dimension=1, tiled=True),
        lax.psum_scatter(grad_down, "dp", scatter_dimension=1, tiled=True),
    )


def body(
    frames_in,
    depth_counts,
    attn_gain_1,
    query_weight_1,
    key_weight_1,
    value_weight_1,
    out_weight_1,
    ffn_gain_1,
    gate_weight_1,
    up_weight_1,
    down_weight_1,
    attn_gain_2,
    query_weight_2,
    key_weight_2,
    value_weight_2,
    out_weight_2,
    ffn_gain_2,
    gate_weight_2,
    up_weight_2,
    down_weight_2,
    out_grad,
):
    layers = (
        (
            attn_gain_1,
            query_weight_1,
            key_weight_1,
            value_weight_1,
            out_weight_1,
            ffn_gain_1,
            gate_weight_1,
            up_weight_1,
            down_weight_1,
        ),
        (
            attn_gain_2,
            query_weight_2,
            key_weight_2,
            value_weight_2,
            out_weight_2,
            ffn_gain_2,
            gate_weight_2,
            up_weight_2,
            down_weight_2,
        ),
    )
    frames_dev = frames_in.shape[0]
    local = frames_in.shape[1]
    portion = frames_dev // MICRO
    positions = lax.axis_index("section") * local + jnp.arange(local)
    active = positions[None, :] < depth_counts[:, None]
    gathered = [fetch(layers[0]), fetch(layers[1])]
    keeps = [[], []]
    results = []
    for micro in range(MICRO):
        state = frames_in[micro * portion : (micro + 1) * portion].astype(jnp.float32)
        for number in (0, 1):
            state, kept = layer_forward(state, gathered[number], positions)
            keeps[number].append(kept)
        results.append(state)
    state = jnp.concatenate(results, axis=0)
    frames_out = jnp.where(active[:, :, None], state, 0.0).astype(jnp.bfloat16)
    masked = jnp.where(active[:, :, None], out_grad.astype(jnp.float32), 0.0)
    carries = [masked[micro * portion : (micro + 1) * portion] for micro in range(MICRO)]
    reduced = [None, None]
    for number in (1, 0):
        params = fetch_again(layers[number])
        pieces = []
        for micro in range(MICRO):
            carries[micro], deferred = layer_backward(carries[micro], params, keeps[number][micro])
            pieces.append(deferred)
        reduced[number] = reduce_grads(weight_terms(join_deferred(pieces)))
    first, second = reduced
    input_grad = jnp.concatenate(carries, axis=0).astype(jnp.bfloat16)
    return (
        frames_out,
        input_grad,
        first[0],
        first[1],
        first[2],
        first[3],
        first[4],
        first[5],
        first[6],
        first[7],
        first[8],
        second[0],
        second[1],
        second[2],
        second[3],
        second[4],
        second[5],
        second[6],
        second[7],
        second[8],
    )


HEAD_LANES = 128
CHAIN = 4
CHUNK = 16
LAST_OUT = 3
MESH = pl.DeviceIdType.MESH


def widen(value):
    return value.astype(jnp.float32)


def low(value):
    return value.astype(jnp.bfloat16)


def dot(left, right):
    return jnp.dot(left, right, preferred_element_type=jnp.float32)


def dot_rows(left, right):
    return lax.dot_general(left, right, (((0,), (0,)), ((), ())), preferred_element_type=jnp.float32)


def dot_back(left, right):
    return lax.dot_general(left, right, (((1,), (1,)), ((), ())), preferred_element_type=jnp.float32)


def looped(count, step):
    lax.fori_loop(0, count, lambda index, carry: (step(index), carry)[1], 0)


def by_rows(rows, step, size=CHUNK):
    looped(rows // size, lambda index: step(pl.ds(pl.multiple_of(index * size, size), size)))


def split_kernel(*refs):
    (frames_ref, cot_ref, counts_ref), gain_refs, refs = refs[:3], refs[3:7], refs[7:]
    weights, refs = (refs[:7], refs[7:14]), refs[14:]
    (frames_out, input_grad), gains_out, refs = refs[:2], refs[2:6], refs[6:]
    grads, refs = (refs[:7], refs[7:14]), refs[14:]
    (
        first_w, second_w, out_w, down_w, normed, inner, branch, back, query, pairs, mixed, both, hidden,
        both_grad, packed_grad, pair_in, pair_out, part, core_in, chain_in, chain_out, states, carry,
        gain_in, gain_full, gain_sum, gain_back, stage_first, stage_second, stage_down, stage_out, room,
        active_ref, gains_ref, segments_ref,
    ), refs = refs[:35], refs[35:]
    (
        gather_send, gather_recv, core_send, core_recv, chain_send, chain_recv, pair_send, pair_recv,
        terms_send, terms_recv, weight_send, weight_recv, grad_send, grad_recv, gain_send, gain_recv,
        sum_send, sum_recv, local_sem,
    ) = refs

    rows, width = frames_ref.shape
    count = 2 * CHAIN
    lanes = width // count
    hidden_cols = second_w.shape[2] // 2
    depth = pairs.shape[1]
    scale = HEAD_DIM ** (-0.5)
    place = lax.axis_index("section")
    spot = lax.axis_index("dp")
    z = spot // 2
    core = spot % 2
    twin = 1 - core

    def at(chip, which):
        return (place, chip * 2 + which)

    def send(source, target, send_sem, recv_sem, device):
        pltpu.make_async_remote_copy(
            src_ref=source, dst_ref=target, send_sem=send_sem, recv_sem=recv_sem, device_id=device, device_id_type=MESH
        ).start()

    def wait(ref, sem):
        pltpu.make_async_copy(ref, ref, sem).wait()

    first_size = -(-rows // (2 * CHUNK)) * CHUNK
    sizes = (first_size, rows - first_size)
    spans = (pl.ds(0, first_size), pl.ds(first_size, rows - first_size))
    starts = (0, count * first_size)

    def half_rows(half, index):
        return pl.ds(pl.multiple_of(starts[half] + index * sizes[half], CHUNK), sizes[half])

    def grouped(half, chip):
        return pl.ds(pl.multiple_of(starts[half] + chip * 2 * sizes[half], 2 * CHUNK), 2 * sizes[half])

    def by_half(half, step):
        by_rows(sizes[half], lambda at_rows: step(pl.ds(pl.multiple_of(at_rows.start + spans[half].start, CHUNK), CHUNK)))

    def column(index, size):
        return pl.ds(pl.multiple_of(index * size, size), size)

    def other(step):
        hop, cross = step // 2, step % 2
        chip = jnp.where(hop == 1, z + 1 - 2 * (z % 2), jnp.where(hop == 2, (z + 2) % 4, jnp.where(hop == 3, 3 - z, z)))
        return chip * 2 + jnp.where(cross == 1, twin, core)

    barrier = pltpu.get_barrier_semaphore()
    for step in range(1, count):
        pl.semaphore_signal(barrier, inc=1, device_id=(place, (spot + step) % count), device_id_type=MESH)
    for step in range(1, depth):
        pl.semaphore_signal(barrier, inc=1, device_id=((place + step) % depth, spot), device_id_type=MESH)

    loads = []
    for layer in range(2):
        loads.append(pltpu.make_async_copy(weights[layer][3], out_w.at[layer], local_sem.at[2 * layer]))
        loads.append(pltpu.make_async_copy(weights[layer][6], down_w.at[layer], local_sem.at[2 * layer + 1]))
    for load in loads:
        load.start()
    mine = pl.ds(pl.multiple_of(spot * lanes, lanes), lanes)

    def weight_parts(layer):
        for number in range(3):
            yield weights[layer][number], first_w, number * lanes, lanes, number
        for number in range(2):
            yield weights[layer][4 + number], second_w, number * hidden_cols, hidden_cols, 3 + number

    def own_weights(layer):
        for source, held, start, size, number in weight_parts(layer):
            yield pltpu.make_async_copy(
                source.at[:, column(spot, size)], held.at[layer, mine, start : start + size], weight_recv.at[layer, number, spot]
            )

    for layer in range(2):
        for copy in own_weights(layer):
            copy.start()

    def send_weights(layer, numbers, step):
        target = other(step)
        for source, held, start, size, number in weight_parts(layer):
            if number in numbers:
                send(
                    source.at[:, column(target, size)],
                    held.at[layer, mine, start : start + size],
                    weight_send.at[layer, number, step],
                    weight_recv.at[layer, number, spot],
                    (place, target),
                )

    def far_first(index):
        step = 0
        for number, value in enumerate((4, 2, 5, 6, 3, 7, 1)):
            step = jnp.where(index == number, value, step)
        return step

    def second_job(job, emit):
        step = far_first(job % (count - 1))
        piece = job // (count - 1)
        rows_at = pl.ds(pl.multiple_of(piece // 2 * (lanes // 2), lanes // 2), lanes // 2)
        for which in range(2):

            @pl.when((piece % 2 == which) & (job >= 0) & (job < 4 * (count - 1)))
            def _():
                emit(step, which, rows_at)

    def send_second(layer, job):
        def emit(step, which, rows_at):
            target = other(step)
            start = which * hidden_cols
            to = pl.ds(pl.multiple_of(spot * lanes + rows_at.start, lanes // 2), lanes // 2)
            send(
                weights[layer][4 + which].at[rows_at, column(target, hidden_cols)],
                second_w.at[layer, to, start : start + hidden_cols],
                weight_send.at[layer, 3 + which, step],
                weight_recv.at[layer, 3 + which, spot],
                (place, target),
            )

        second_job(job, emit)

    def send_first(layer, job):
        @pl.when((job >= 0) & (job < count - 1))
        def _():
            send_weights(layer, (0, 1, 2), far_first(job))

    def wait_weights(layer, numbers):
        def arrived(index):
            for _, held, start, size, number in weight_parts(layer):
                if number in numbers:
                    wait(held.at[layer, column(index, lanes), start : start + size], weight_recv.at[layer, number, index])

        looped(count, arrived)

    def finish_weights(layer):
        def sent(index):
            for _, held, start, size, number in weight_parts(layer):
                wait(held.at[layer, pl.ds(0, lanes), start : start + size], weight_send.at[layer, number, index + 1])

        looped(count - 1, sent)

    gains_ref[...] = jnp.zeros_like(gains_ref)
    for index, ref in enumerate(gain_refs):
        gains_ref[index : index + 1] = widen(ref[...])
    gain_in[spot] = gains_ref[...]

    pl.semaphore_wait(barrier, count - 1 + depth - 1)

    for step in range(1, count):
        send(gains_ref, gain_in.at[spot], gain_send.at[step], gain_recv.at[spot], (place, other(step)))
    looped(count - 1, lambda index: send_first(0, index))

    for layer in range(2):
        for source in range(1, depth):

            @pl.when(place < source)
            def _():
                pairs[layer, source] = jnp.zeros(pairs.shape[2:], pairs.dtype)

            @pl.when(place >= source)
            def _():
                pair_in[layer, source - 1] = jnp.zeros(pair_in.shape[2:], pair_in.dtype)

    for parity in range(2):

        @pl.when(z == 0)
        def _():
            for index in range(CHAIN):
                chain_in[parity, index] = jnp.zeros(chain_in.shape[2:], chain_in.dtype)

        @pl.when(z == CHAIN - 1)
        def _():
            for index in (0, 1, 2, 4):
                chain_in[parity, index] = jnp.zeros(chain_in.shape[2:], chain_in.dtype)
    gain_sum[...] = jnp.zeros_like(gain_sum)

    def own_rows(half):
        return half_rows(half, spot)

    def gather_start(number, half, held):
        own = held.at[own_rows(half)]
        send(own, own, gather_send.at[number, half, 0], gather_recv.at[number, half, spot], at(z, twin))

        @pl.when(z < CHAIN - 1)
        def _():
            send(own, own, gather_send.at[number, half, 1], gather_recv.at[number, half, spot], at(z + 1, core))

        @pl.when(z > 0)
        def _():
            send(own, own, gather_send.at[number, half, 2], gather_recv.at[number, half, spot], at(z - 1, core))

    def gather_arrive(number, half, held, index):
        below, above = z - index, z + index

        @pl.when((index > 0) & (index < CHAIN) & (below >= 0))
        def _():
            source = below * 2 + core
            here = held.at[half_rows(half, source)]
            wait(here, gather_recv.at[number, half, source])

            @pl.when(z < CHAIN - 1)
            def _():
                send(here, here, gather_send.at[number, half, 2 + index], gather_recv.at[number, half, source], at(z + 1, core))

            send(here, here, gather_send.at[number, half, 8 + index], gather_recv.at[number, half, source], at(z, twin))

        @pl.when((index > 0) & (above < CHAIN))
        def _():
            source = above * 2 + core
            here = held.at[half_rows(half, source)]
            wait(here, gather_recv.at[number, half, source])

            @pl.when(z > 0)
            def _():
                send(here, here, gather_send.at[number, half, 5 + index], gather_recv.at[number, half, source], at(z - 1, core))

            send(here, here, gather_send.at[number, half, 11 + index], gather_recv.at[number, half, source], at(z, twin))

    def gather_compute(number, half, held, compute, index):
        def side(which):
            chip = z - index + 2 * index * which

            @pl.when((chip >= 0) & (chip < CHAIN) & (index + 1 > which) & (index < CHAIN))
            def _():
                source = chip * 2 + twin
                wait(held.at[half_rows(half, source)], gather_recv.at[number, half, source])
                if compute is not None:
                    compute(half, chip)

        looped(2, side)

    def gather_finish(number, half, held):
        one = held.at[half_rows(half, 0)]
        wait(one, gather_send.at[number, half, 0])

        @pl.when(z < CHAIN - 1)
        def _():
            wait(one, gather_send.at[number, half, 1])

        @pl.when(z > 0)
        def _():
            wait(one, gather_send.at[number, half, 2])

        def step(index):
            @pl.when(z - index >= 0)
            def _():
                @pl.when(z < CHAIN - 1)
                def _():
                    wait(one, gather_send.at[number, half, 2 + index])

                wait(one, gather_send.at[number, half, 8 + index])

            @pl.when(z + index < CHAIN)
            def _():
                @pl.when(z > 0)
                def _():
                    wait(one, gather_send.at[number, half, 5 + index])

                wait(one, gather_send.at[number, half, 11 + index])

        looped(CHAIN - 1, lambda index: step(index + 1))

    def order(index):
        first = 3 * (1 - z // 2)
        second = 2 - z // 2
        third = 1 - z % 2 + 2 * (z // 2)
        return jnp.where(index == 0, first, jnp.where(index == 1, second, jnp.where(index == 2, third, z)))

    def scatter_compute(number, half, compute, index):
        bank = 1 if number == LAST_OUT else 0
        span = spans[half]

        @pl.when(index < CHAIN)
        def _():
            slot = index % 2

            @pl.when(index > 1)
            def _():
                wait(part.at[slot, twin, span], core_send.at[number, half, index - 2])

            product = compute(half, order(index))
            part[slot, 0, span] = product[: sizes[half]]
            part[slot, 1, span] = product[sizes[half] :]
            send(
                part.at[slot, twin, span],
                core_in.at[bank, index, span],
                core_send.at[number, half, index],
                core_recv.at[number, half, index],
                at(z, twin),
            )

    def scatter_send(number, half, index, allowed):
        bank = 1 if number == LAST_OUT else 0
        span = spans[half]

        @pl.when((index > 0) & (index < CHAIN) & allowed)
        def _():
            held = index - 1
            slot = held % 2
            target = order(held)
            wait(core_in.at[bank, held, span], core_recv.at[number, half, held])

            @pl.when(((target > z) & (z > 0)) | ((target < z) & (z < CHAIN - 1)))
            def _():
                wait(chain_in.at[bank, target, span], chain_recv.at[number, half, target])

            def add(at_rows):
                total = part[slot, core, at_rows] + core_in[bank, held, at_rows]
                chain_out[bank, held, at_rows] = low(total + widen(chain_in[bank, target, at_rows]))

            by_half(half, add)

            @pl.when(target > z)
            def _():
                send(
                    chain_out.at[bank, held, span],
                    chain_in.at[bank, target, span],
                    chain_send.at[number, half, held],
                    chain_recv.at[number, half, target],
                    at(z + 1, core),
                )

            @pl.when(target < z)
            def _():
                landing = jnp.where(target == z - 1, CHAIN, target)
                send(
                    chain_out.at[bank, held, span],
                    chain_in.at[bank, landing, span],
                    chain_send.at[number, half, held],
                    chain_recv.at[number, half, landing],
                    at(z - 1, core),
                )

    def scatter_end(number, half, sink, index):
        bank = 1 if number == LAST_OUT else 0
        span = spans[half]
        held = CHAIN - 1
        slot = held % 2

        @pl.when(index == CHAIN)
        def _():
            wait(core_in.at[bank, held, span], core_recv.at[number, half, held])

            @pl.when(z > 0)
            def _():
                wait(chain_in.at[bank, z, span], chain_recv.at[number, half, z])

            @pl.when(z < CHAIN - 1)
            def _():
                wait(chain_in.at[bank, CHAIN, span], chain_recv.at[number, half, CHAIN])

            def total(at_rows):
                sink(
                    half,
                    at_rows,
                    part[slot, core, at_rows]
                    + core_in[bank, held, at_rows]
                    + widen(chain_in[bank, z, at_rows])
                    + widen(chain_in[bank, CHAIN, at_rows]),
                )

            by_half(half, total)

    def scatter_finish(number, half):
        span = spans[half]

        def sent(index):
            wait(chain_out.at[0, index, span], chain_send.at[number, half, index])

        looped(CHAIN - 1, sent)

    def core_finish(number, half):
        for index in (CHAIN - 2, CHAIN - 1):
            wait(part.at[index % 2, twin, spans[half]], core_send.at[number, half, index])

    pending = []

    def phase(scatters=(), gathers=(), slack=None, ready=None):
        for number, half, held, _ in gathers:
            gather_start(number, half, held)

        outer = (z == 0) | (z == CHAIN - 1)
        inside = (z > 0) & (z < CHAIN - 1)

        def step(index):
            for number, half, compute, sink in scatters:
                scatter_compute(number, half, compute, index)
                scatter_send(number, half, index, outer)
            if slack is not None:
                slack(index, 0)
            for number, half, held, _ in gathers:
                gather_arrive(number, half, held, index)
            for number, half, compute, sink in scatters:
                scatter_send(number, half, index, inside)
            if slack is not None:
                slack(index, 1)
            if ready is not None:
                pl.when(index == 0)(ready)
            for number, half, held, compute in gathers:
                gather_compute(number, half, held, compute, index)
            for number, half, compute, sink in scatters:
                scatter_end(number, half, sink, index)
            if slack is not None:
                slack(index, 2)

        looped(CHAIN + 1, step)
        for number, half, _, _ in scatters:
            core_finish(number, half)
        for done in pending:
            done()
        pending.clear()
        for number, half, held, _ in gathers:
            pending.append(functools.partial(gather_finish, number, half, held))
        for number, half, _, _ in scatters:
            pending.append(functools.partial(scatter_finish, number, half))

    def state_at(index, at_rows):
        return states[index - 1, at_rows] if index else widen(frames_ref[at_rows])

    def gain_row(index):
        return gain_full[index : index + 1, :]

    def inverse_of(value):
        return lax.rsqrt(jnp.mean(value * value, axis=-1, keepdims=True) + EPSILON)

    def at_own(half, at_rows):
        start = starts[half] + spot * sizes[half] + at_rows.start - spans[half].start
        return pl.ds(pl.multiple_of(start, CHUNK), CHUNK)

    def pieces(half, chip, step):
        looped(2, lambda which: step(which, half_rows(half, chip * 2 + which)))

    def project_first(layer):
        def compute(half, chip):
            here = grouped(half, chip)
            packed = low(dot(normed[layer, here], first_w[layer]))
            query[layer, here] = packed[:, :lanes]
            pairs[layer, place, here] = packed[:, lanes:]
            for step in range(1, depth):

                @pl.when(place + step < depth)
                def _():
                    ref = pairs.at[layer, place, here]
                    send(ref, ref, pair_send.at[layer, half, step, chip], pair_recv.at[layer, half, place, chip], (place + step, spot))

        return compute

    def finish_pairs(layer):
        for half in range(2):

            def sent(chip):
                for step in range(1, depth):

                    @pl.when(place + step < depth)
                    def _():
                        wait(pairs.at[layer, place, grouped(half, chip)], pair_send.at[layer, half, step, chip])

            looped(CHAIN, sent)

    def segment_sums(values):
        size = values[0].shape[0]
        high = [low(value) for value in values]
        rest = [low(value - widen(upper)) for value, upper in zip(values, high)]
        sums = dot(jnp.concatenate(high + rest, axis=0), segments_ref[...])
        half = len(values) * size
        return [sums[i * size : (i + 1) * size] + sums[half + i * size : half + (i + 1) * size] for i in range(len(values))]

    def attend_of(query_rows, keys):
        scores = segment_sums([query_rows * key for key in keys])
        scores = [jnp.where(index <= place, score * scale, -1e30) for index, score in enumerate(scores)]
        largest = functools.reduce(jnp.maximum, scores)
        expd = [jnp.exp(score - largest) for score in scores]
        inverse = 1.0 / functools.reduce(jnp.add, expd)
        return [value * inverse for value in expd]

    def attention(layer):
        def compute(half, chip):
            here = grouped(half, chip)
            for source in range(depth - 1):

                @pl.when(source < place)
                def _():
                    wait(pairs.at[layer, source, here], pair_recv.at[layer, half, source, chip])

            def rowset(which, at_rows):
                query_rows = widen(query[layer, at_rows])
                keys = [widen(pairs[layer, source, at_rows, :lanes]) for source in range(depth)]
                attend = attend_of(query_rows, keys)
                terms = [widen(low(a)) * widen(pairs[layer, source, at_rows, lanes:]) for source, a in enumerate(attend)]
                mixed[layer, at_rows] = low(functools.reduce(jnp.add, terms))

            pieces(half, chip, rowset)
            return dot(mixed[layer, here], out_w[layer])

        return compute

    def normalize(value, gain):
        return low(value * inverse_of(value) * gain)

    def middle_sink(layer):
        def sink(half, at_rows, total):
            value = state_at(2 * layer, at_rows) + total
            states[2 * layer, at_rows] = value
            inner[layer, at_own(half, at_rows)] = normalize(value, gain_row(2 * layer + 1))

        return sink

    def by_group(half, chip, step):
        def shifted(at_rows):
            start = starts[half] + chip * 2 * sizes[half] + at_rows.start
            step(at_rows, pl.ds(pl.multiple_of(start, CHUNK), CHUNK))

        by_rows(2 * sizes[half], shifted)

    def project_second(layer):
        def compute(half, chip):
            room[: 2 * sizes[half]] = dot(inner[layer, grouped(half, chip)], second_w[layer])

            def gated(at_rows, to):
                gate = room[at_rows, :hidden_cols]
                up = room[at_rows, hidden_cols:]
                both[layer, to, :hidden_cols] = low(gate)
                both[layer, to, hidden_cols:] = low(up)
                hidden[layer, to] = low(gate * jax.nn.sigmoid(gate) * up)

            by_group(half, chip, gated)

        return compute

    def project_down(layer):
        def compute(half, chip):
            return dot(hidden[layer, grouped(half, chip)], down_w[layer])

        return compute

    def state_sink(half, at_rows, total):
        value = state_at(1, at_rows) + total
        states[1, at_rows] = value
        normed[1, at_own(half, at_rows)] = normalize(value, gain_row(2))

    def frames_sink(half, at_rows, total):
        value = state_at(3, at_rows) + total
        frames_out[at_rows] = low(jnp.where(active_ref[at_rows] > 0.0, value, 0.0))

    def hidden_back(layer):
        def compute(half, chip):
            room[: 2 * sizes[half], :hidden_cols] = dot_back(branch[grouped(half, chip)], down_w[layer])

            def gated(at_rows, to):
                upper = room[at_rows, :hidden_cols]
                gate = widen(both[layer, to, :hidden_cols])
                up = widen(both[layer, to, hidden_cols:])
                sigma = jax.nn.sigmoid(gate)
                scaled = upper * sigma
                both_grad[to, :hidden_cols] = low(scaled * up * (1.0 + gate * (1.0 - sigma)))
                both_grad[to, hidden_cols:] = low(scaled * gate)

            by_group(half, chip, gated)

        return compute

    def second_and_back(half, chip):
        project_second(1)(half, chip)
        hidden_back(1)(half, chip)

    def project_second_back(layer):
        def compute(half, chip):
            return dot_back(both_grad[grouped(half, chip)], second_w[layer])

        return compute

    def norm_back(total, value, gain, index):
        inverse = inverse_of(value)
        product = total * value * inverse
        gain_sum[index] += product[:8] + product[8:]
        scaled = total * gain
        return inverse * scaled - value * (inverse * inverse * inverse) * jnp.mean(scaled * value, axis=-1, keepdims=True)

    def inner_sink(layer):
        def sink(half, at_rows, total):
            index = 2 * layer + 1
            value = carry[at_rows] + norm_back(total, state_at(index, at_rows), gain_row(index), index)
            carry[at_rows] = value
            back[at_own(half, at_rows)] = low(value)

        return sink

    def attention_back(layer):
        def compute(half, chip):
            here = grouped(half, chip)
            room[: 2 * sizes[half], :lanes] = widen(low(dot_back(back[here], out_w[layer])))

            def rowset(which, at_rows):
                upper = room[pl.ds(pl.multiple_of(which * sizes[half], CHUNK), sizes[half]), :lanes]
                query_rows = widen(query[layer, at_rows])
                keys = [widen(pairs[layer, source, at_rows, :lanes]) for source in range(depth)]
                attend = attend_of(query_rows, keys)
                attend_grad = segment_sums([upper * widen(pairs[layer, source, at_rows, lanes:]) for source in range(depth)])
                inside = functools.reduce(jnp.add, [a * g for a, g in zip(attend, attend_grad)])
                score_grad = [widen(low(a * (g - inside))) for a, g in zip(attend, attend_grad)]
                packed_grad[at_rows, :lanes] = low(functools.reduce(jnp.add, [g * k for g, k in zip(score_grad, keys)]) * scale)
                for source in range(depth):
                    pair_out[source, at_rows, :lanes] = low(score_grad[source] * query_rows * scale)
                    pair_out[source, at_rows, lanes:] = low(widen(low(attend[source])) * upper)

            pieces(half, chip, rowset)
            for target in range(depth - 1):

                @pl.when(target < place)
                def _():
                    send(
                        pair_out.at[target, here],
                        pair_in.at[layer, place - 1, here],
                        terms_send.at[layer, half, target, chip],
                        terms_recv.at[layer, half, place - 1, chip],
                        (target, spot),
                    )

        return compute

    def finish_terms(layer):
        for half in range(2):

            def sent(chip):
                for target in range(depth - 1):

                    @pl.when(target < place)
                    def _():
                        wait(pair_out.at[target, grouped(half, chip)], terms_send.at[layer, half, target, chip])

            looped(CHAIN, sent)

    def pair_sums(layer, half, chip):
        here = grouped(half, chip)
        for source in range(1, depth):

            @pl.when(source > place)
            def _():
                wait(pair_in.at[layer, source - 1, here], terms_recv.at[layer, half, source - 1, chip])

        def rowset(which, at_rows):
            total = widen(pair_out[place, at_rows])
            for source in range(1, depth):
                total += widen(pair_in[layer, source - 1, at_rows])
            packed_grad[at_rows, lanes:] = low(total)

        pieces(half, chip, rowset)

    def project_first_back(layer):
        def compute(half, chip):
            if layer or not half:
                pair_sums(layer, half, chip)
            return dot_back(packed_grad[grouped(half, chip)], first_w[layer])

        return compute

    def carry_sink(layer):
        def sink(half, at_rows, total):
            index = 2 * layer
            value = carry[at_rows] + norm_back(total, state_at(index, at_rows), gain_row(index), index)
            if layer:
                carry[at_rows] = value
                branch[at_own(half, at_rows)] = low(value)
            else:
                input_grad[at_rows] = low(value)

        return sink

    def grad_parts(layer, kind):
        if kind == 0:
            for number in range(3):
                yield number * lanes, lanes, grads[layer][number], number
        else:
            for number in range(2):
                yield number * hidden_cols, hidden_cols, grads[layer][4 + number], 3 + number

    def grad_task(layer, kind, step, start=0, stop=None):
        target = other(step)
        stage = (stage_first, stage_second)[kind]
        left = (normed, inner)[kind]
        right = (packed_grad, both_grad)[kind]
        stop = stop or right.shape[1]
        stage[step, :, start:stop] = low(dot_rows(left[layer, :, column(target, lanes)], right[:, start:stop]))

    def grad_first(layer, job, numbers=(0, 1, 2)):
        @pl.when((job >= 0) & (job < count - 1))
        def _():
            step = far_first(job)
            target = other(step)
            for start, size, out, number in grad_parts(layer, 0):
                if number not in numbers:
                    continue
                send(
                    stage_first.at[step, :, start : start + size],
                    out.at[:, column(spot, size)],
                    grad_send.at[layer, number, step],
                    grad_recv.at[layer, number, spot],
                    (place, target),
                )

    def grad_second(layer, job):
        def emit(step, which, rows_at):
            start = which * hidden_cols
            send(
                stage_second.at[step, rows_at, start : start + hidden_cols],
                grads[layer][4 + which].at[rows_at, column(spot, hidden_cols)],
                grad_send.at[layer, 3 + which, step],
                grad_recv.at[layer, 3 + which, spot],
                (place, other(step)),
            )

        second_job(job, emit)

    def grad_keep(layer, kind):
        stage = (stage_first, stage_second)[kind]
        for start, size, out, number in grad_parts(layer, kind):
            pltpu.make_async_copy(
                stage.at[0, :, start : start + size], out.at[:, column(spot, size)], grad_recv.at[layer, number, spot]
            ).start()

    def grad_sent(layer, kind):
        def sent(index):
            for start, size, out, number in grad_parts(layer, kind):
                wait(out.at[:, 0:size], grad_send.at[layer, number, index + 1])

        looped(count - 1, sent)
        for start, size, out, number in grad_parts(layer, kind):
            wait(out.at[:, 0:size], grad_recv.at[layer, number, spot])

    def grad_arrived(layer, kind):
        def arrived(index):
            source = other(index + 1)
            for start, size, out, number in grad_parts(layer, kind):
                wait(out.at[:, column(source, size)], grad_recv.at[layer, number, source])

        looped(count - 1, arrived)

    def down_task(layer, index):
        size = stage_down.shape[0] // 4
        at_rows = pl.ds(pl.multiple_of(index * size, size), size)
        stage_down[at_rows] = low(dot_rows(hidden[layer, :, column(index, size)], branch[...]))

    def down_start(layer):
        return pltpu.make_async_copy(stage_down, grads[layer][6], local_sem.at[4 + 2 * layer])

    def out_task(layer):
        stage_out[...] = low(dot_rows(mixed[layer], back[...]))

    def out_start(layer):
        return pltpu.make_async_copy(stage_out, grads[layer][3], local_sem.at[5 + 2 * layer])

    def send_sums(indices):
        for index in indices:

            def step(number):
                target = other(number + 1)
                send(
                    gain_sum.at[index, :, column(target, lanes)],
                    gain_back.at[index, spot],
                    sum_send.at[index, number + 1],
                    sum_recv.at[index, spot],
                    (place, target),
                )

            looped(count - 1, step)
            gain_back[index, spot] = gain_sum[index, :, column(spot, lanes)]

    def finish_sums(indices):
        for index in indices:

            def step(number):
                source = other(number + 1)
                wait(gain_back.at[index, source], sum_recv.at[index, source])
                wait(gain_back.at[index, 0], sum_send.at[index, number + 1])

            looped(count - 1, step)
            gains_out[index][...] = jnp.sum(gain_back[index], axis=(0, 1), keepdims=True)[0]

    square = (rows, rows)
    on_row = lax.broadcasted_iota(jnp.int32, square, 0) == lax.broadcasted_iota(jnp.int32, square, 1)
    spread = jnp.sum(jnp.where(on_row, counts_ref[...], 0).astype(jnp.float32), axis=1, keepdims=True)
    active_ref[...] = (spread > place.astype(jnp.float32)).astype(jnp.float32)
    square = segments_ref.shape
    head = [lax.broadcasted_iota(jnp.int32, square, axis) // HEAD_DIM for axis in range(2)]
    segments_ref[...] = low((head[0] == head[1]).astype(jnp.float32))
    carry[...] = jnp.where(active_ref[...] > 0.0, widen(cot_ref[...]), 0.0)

    def gains_arrived(index):
        source = other(index + 1)
        wait(gain_in.at[source], gain_recv.at[source])

    looped(count - 1, gains_arrived)
    for source in range(count):
        gain_full[:, source * lanes : (source + 1) * lanes] = gain_in[source]

    for half in range(2):

        def first_rows(at_rows):
            normed[0, at_own(half, at_rows)] = normalize(state_at(0, at_rows), gain_row(0))
            branch[at_own(half, at_rows)] = low(carry[at_rows])

        by_half(half, first_rows)

    for layer in range(2):
        gather_normed = [(2 * layer, half, normed.at[layer], project_first(layer)) for half in range(2)]
        gather_inner = [(2 * layer + 1, half, inner.at[layer], second_and_back if layer else project_second(0)) for half in range(2)]
        scatter_out = [(2 * layer, half, attention(layer), middle_sink(layer)) for half in range(2)]
        if layer == 0:
            def feed(index, point):
                if point < 2:
                    send_second(0, index * 2 + point)

            phase((), gather_normed[:1], feed, lambda: wait_weights(0, (0, 1, 2)))
            loads[0].wait()

            def feed(index, point):
                send_second(0, 10 + index * 4 + point)
                if point == 2:
                    send_second(0, 13 + index * 4)

            phase(scatter_out[:1], gather_normed[1:], feed)

            def feed(index, point):
                if point < 2:
                    send_first(1, index * 2 + point)
                else:
                    send_second(1, index)

            phase(scatter_out[1:], gather_inner[:1], feed, lambda: wait_weights(0, (3, 4)))
            loads[1].wait()
            scatter_down = [(1, half, project_down(0), state_sink) for half in range(2)]

            def feed(index, point, base=5, limit=13):
                if point < 2:
                    job = base + index * 2 + point

                    @pl.when(job < limit)
                    def _():
                        send_second(1, job)

            phase(scatter_down[:1], gather_inner[1:], feed)
            finish_weights(0)
            finish_pairs(0)
        else:
            phase(scatter_down[1:], gather_normed[:1], functools.partial(feed, base=13, limit=21), lambda: wait_weights(1, (0, 1, 2)))
            loads[2].wait()
            phase(scatter_out[:1], gather_normed[1:], functools.partial(feed, base=21, limit=28))
            loads[3].wait()
            phase(scatter_out[1:], [(4, 0, branch, None)] + gather_inner[:1], None, lambda: wait_weights(1, (3, 4)))
            finish_weights(1)
            finish_pairs(1)

    scatter_inner = [(4, half, project_second_back(1), inner_sink(1)) for half in range(2)]
    phase(scatter_inner[:1], [(4, 1, branch, None)] + gather_inner[1:])
    for layer in (1, 0):
        gather_back = [(5 if layer else 7, half, back, attention_back(layer)) for half in range(2)]
        scatter_normed = [(5 if layer else 7, half, project_first_back(layer), carry_sink(layer)) for half in range(2)]
        if layer == 0:
            grad_sent(1, 1)
            down_start(1).wait()
            out_start(1).wait()

        def second_grads(index, point, layer=layer):
            if point == 0:

                @pl.when(index < CHAIN)
                def _():
                    grad_task(layer, 1, far_first(2 * index))
                    grad_task(layer, 1, far_first(2 * index + 1))
                    down_task(layer, index)

            @pl.when(index > 0)
            def _():
                grad_second(layer, (index - 1) * 3 + point)

        def more_second_grads(index, point, layer=layer):
            grad_second(layer, 12 + index * 2 + point) if point < 2 else None

        last = [(LAST_OUT, half, project_down(1), frames_sink) for half in range(2)] if layer else [None, None]
        phase(scatter_inner[1:], gather_back[:1], second_grads)
        down_start(layer).start()
        grad_keep(layer, 1)
        if layer:
            phase(scatter_normed[:1] + last[1:], gather_back[1:], more_second_grads)
            gather_branch = [(6, half, branch, hidden_back(0)) for half in range(2)]

            def rest(index, point):
                if point < 2:
                    grad_second(1, 22 + 2 * index + point)

            phase(scatter_normed[1:] + last[:1], gather_branch[:1], rest)
            finish_terms(1)
            out_task(1)
            out_start(1).start()
            send_sums((2, 3))

            def first_grads(index, point):
                if point == 0:

                    @pl.when(index < CHAIN)
                    def _():
                        grad_task(1, 0, far_first(2 * index))
                        grad_task(1, 0, far_first(2 * index + 1))

                else:
                    grad_first(1, index * 2 + point - 1)

            scatter_inner = [(6, half, project_second_back(0), inner_sink(0)) for half in range(2)]
            phase(scatter_inner[:1], gather_branch[1:], first_grads)
            grad_keep(1, 0)
        else:
            phase(scatter_normed[:1], gather_back[1:], more_second_grads)
            out_task(0)
            out_start(0).start()
            grad_sent(1, 0)
            send_sums((1,))

            def settle():
                for step in range(1, count):
                    wait(gain_in.at[0], gain_send.at[step])
                grad_arrived(1, 0)
                grad_arrived(1, 1)
                finish_sums((2, 3, 1))


            def last_grads(index, point):
                def last_task(job):
                    grad_task(0, 0, far_first(job))
                    grad_first(0, job)

                if point < 2:
                    grad_second(0, 22 + 2 * index + point)

                if point == 0:

                    @pl.when(index == 0)
                    def _():
                        looped(count, last_task)

                if point == 1:

                    @pl.when(index == 2)
                    def _():
                        settle()

            looped(CHAIN, lambda chip: pair_sums(0, 1, chip))
            phase(scatter_normed[1:], (), last_grads)
            send_sums((0,))
            grad_keep(0, 0)
            finish_terms(0)

    for done in pending:
        done()
    down_start(0).wait()
    out_start(0).wait()
    for kind in (1, 0):
        grad_sent(0, kind)
        grad_arrived(0, kind)
    finish_sums((0,))


def widen_kernel(*refs):
    half = len(refs) // 2
    for source, target in zip(refs[:half], refs[half:]):
        target[...] = source[...].astype(target.dtype)


def widen_all(whole, arrays, steps=2):
    specs = [pl.BlockSpec(array.shape, lambda index: (0, 0)) for array in whole]
    specs += [pl.BlockSpec((array.shape[0] // steps, array.shape[1]), lambda index: (index, 0)) for array in arrays]
    shapes = [jax.ShapeDtypeStruct(array.shape, array.dtype) for array in whole]
    shapes += [jax.ShapeDtypeStruct(array.shape, jnp.float32) for array in arrays]
    return pl.pallas_call(
        widen_kernel,
        grid=(steps,),
        out_shape=shapes,
        in_specs=specs,
        out_specs=specs,
        compiler_params=pltpu.CompilerParams(vmem_limit_bytes=VMEM_BYTES),
    )(*whole, *arrays)


def split_body(*args):
    frames_in, depth_counts, out_grad = args[0][:, 0], args[1], args[-1][:, 0]
    rows, width = frames_in.shape
    depth = lax.axis_size("section")
    count = lax.axis_size("dp")
    lanes = width // count
    layers = [tuple(a[0] for a in args[2:11]), tuple(a[0] for a in args[11:20])]
    ff_cols = layers[0][6].shape[1]
    hidden_cols = ff_cols // count
    down_rows = layers[0][8].shape[0]
    gains = [layer[i][None] for layer in layers for i in (0, 5)]
    weights = [layer[i] for layer in layers for i in (1, 2, 3, 4, 6, 7, 8)]
    total = rows * count
    low_type, full_type = jnp.bfloat16, jnp.float32
    grad_shapes = [(lanes, width)] * 4 + [(lanes, ff_cols)] * 2 + [(down_rows, width)]
    out_shape = (
        [jax.ShapeDtypeStruct((rows, width), low_type)] * 2
        + [jax.ShapeDtypeStruct((1, lanes), full_type)] * 4
        + [jax.ShapeDtypeStruct(shape, low_type) for shape in grad_shapes * 2]
    )
    vmem, anywhere = pl.BlockSpec(memory_space=pltpu.VMEM), pl.BlockSpec(memory_space=pl.ANY)
    held = pltpu.VMEM
    sems = pltpu.SemaphoreType.DMA
    scratch = [
        held((2, width, 3 * lanes), low_type),
        held((2, width, 2 * hidden_cols), low_type),
        held((2, lanes, width), low_type),
        held((2, down_rows, width), low_type),
        held((2, total, width), low_type),
        held((2, total, width), low_type),
        held((total, width), low_type),
        held((total, width), low_type),
        held((2, total, lanes), low_type),
        held((2, depth, total, 2 * lanes), low_type),
        held((2, total, lanes), low_type),
        held((2, total, 2 * hidden_cols), low_type),
        held((2, total, hidden_cols), low_type),
        held((total, 2 * hidden_cols), low_type),
        held((total, 3 * lanes), low_type),
        held((2, depth - 1, total, 2 * lanes), low_type),
        held((depth, total, 2 * lanes), low_type),
        held((2, 2, rows, width), full_type),
        held((2, CHAIN, rows, width), full_type),
        held((2, CHAIN + 1, rows, width), low_type),
        held((2, CHAIN - 1, rows, width), low_type),
        held((3, rows, width), full_type),
        held((rows, width), full_type),
        held((count, 8, lanes), full_type),
        held((8, width), full_type),
        held((4, 8, width), full_type),
        held((4, count, 8, lanes), full_type),
        held((count, lanes, 3 * lanes), low_type),
        held((count, lanes, 2 * hidden_cols), low_type),
        held((down_rows, width), low_type),
        held((lanes, width), low_type),
        held((2 * -(-rows // (2 * CHUNK)) * CHUNK, width), full_type),
        held((rows, 1), full_type),
        held((8, lanes), full_type),
        held((lanes, lanes), low_type),
        sems((8, 2, 15)),
        sems((8, 2, count)),
        sems((8, 2, CHAIN)),
        sems((8, 2, CHAIN)),
        sems((8, 2, CHAIN)),
        sems((8, 2, CHAIN + 1)),
        sems((2, 2, depth, CHAIN)),
        sems((2, 2, depth, CHAIN)),
        sems((2, 2, depth, CHAIN)),
        sems((2, 2, depth, CHAIN)),
        sems((2, 5, count)),
        sems((2, 5, count)),
        sems((2, 5, count)),
        sems((2, 5, count)),
        sems((count,)),
        sems((count,)),
        sems((4, count)),
        sems((4, count)),
        sems((8,)),
    ]
    outs = pl.pallas_call(
        split_kernel,
        out_shape=out_shape,
        in_specs=[vmem] * 7 + [anywhere] * 14,
        out_specs=[vmem] * 6 + [anywhere] * 14,
        scratch_shapes=scratch,
        compiler_params=pltpu.CompilerParams(
            collective_id=0, has_side_effects=True, vmem_limit_bytes=VMEM_BYTES
        ),
        cost_estimate=pl.CostEstimate(flops=2 * 6 * total * width * (4 * lanes + 3 * hidden_cols), bytes_accessed=1 << 26, transcendentals=1 << 22),
    )(frames_in, out_grad, depth_counts[None], *gains, *weights)
    wide = widen_all(outs[:6], outs[6:])
    result = [wide[0][:, None], wide[1][:, None]]
    for layer in range(2):
        own = [out[None] for out in wide[6 + 7 * layer : 13 + 7 * layer]]
        result += [wide[2 + 2 * layer], *own[:4], wide[3 + 2 * layer], *own[4:]]
    return tuple(result)


def solution(mesh):
    in_specs = (
        P("dp", "section", None),
        P("dp"),
        P("section", "dp"),
        P("section", "dp", None),
        P("section", "dp", None),
        P("section", "dp", None),
        P("section", "dp", None),
        P("section", "dp"),
        P("section", "dp", None),
        P("section", "dp", None),
        P("section", "dp", None),
        P("section", "dp"),
        P("section", "dp", None),
        P("section", "dp", None),
        P("section", "dp", None),
        P("section", "dp", None),
        P("section", "dp"),
        P("section", "dp", None),
        P("section", "dp", None),
        P("section", "dp", None),
        P("dp", "section", None),
    )
    out_specs = (
        P("dp", "section", None),
        P("dp", "section", None),
        P("section", "dp"),
        P("section", "dp", None),
        P("section", "dp", None),
        P("section", "dp", None),
        P("section", "dp", None),
        P("section", "dp"),
        P("section", "dp", None),
        P("section", "dp", None),
        P("section", "dp", None),
        P("section", "dp"),
        P("section", "dp", None),
        P("section", "dp", None),
        P("section", "dp", None),
        P("section", "dp", None),
        P("section", "dp"),
        P("section", "dp", None),
        P("section", "dp", None),
        P("section", "dp", None),
    )
    parts, sections = mesh.shape["dp"], mesh.shape["section"]
    chosen = split_body if parts == 2 * CHAIN and sections == 4 else body
    return jax.shard_map(chosen, mesh=mesh, in_specs=in_specs, out_specs=out_specs, check_vma=False)
```
